1024 devices in a mesh: gx: 16 (over z_hi, x), gy: 8 (over z_lo, core), gz: 8 (over y).
Axes of the slice: x: 8, y: 8, z: 8 (z_hi: 2, z_lo: 4; z = z_hi * 4 + z_lo), core: 2. Of those that a mesh axis runs over, the one named last changes fastest.
Arguments:
- populations: float32 [19, 96, 48, 1024], P(None, 'gx', 'gy', 'gz'), may hold values from 0.01 to 0.2
- fluid_mask: int32 [96, 48, 1024], P('gx', 'gy', 'gz'), may hold values 0 or 1
- stencil_base: int32 [16, 8, 8, 3, 642], P('gx', 'gy', 'gz'), may hold values from -4 to 128, as said below
- offsets: float32 [16, 8, 8, 3, 642], P('gx', 'gy', 'gz'), may hold values from 0 to 1
- occupied_cell_slots: int32 [16, 8, 8], P('gx', 'gy', 'gz'), may hold values from 0 to 1, as said below
- triangles: int32 [1280, 3], replicated, may hold values from 0 to 641, as said below
Outputs:
- next_populations: float32 [19, 96, 48, 1024], P(None, 'gx', 'gy', 'gz')
- interpolated_vertex_velocity: float32 [16, 8, 8, 3, 642], P('gx', 'gy', 'gz')
The draws below stay inside these ranges and needn't reach their ends.
Inputs may be any that keep to these rules, and one draw needn't show every extreme that they name: `stencil_base`: along every dimension the four stencil nodes lie at most 4 nodes outside the owning block, so they lie in that block or in blocks beside it; the vertices of one slot lie within 3 nodes of a common centre inside the block. The first occupied_cell_slots slots of a block hold cells; the others are empty. `triangles`: each row names three different vertices of a cell; every vertex is named by some row.
All inputs are finite; a program needn't handle non-finite values. No bound on the sum of `fluid_mask` on one device may be relied on, other than what follows from the above.
Results may differ from the reference program's by a relative error of at most 0.0003.
Values sent between devices are 32-bit elements; how exact they have to be, the bound alone decides.
A program may use at most 64 MiB of HBM per device.

```python
import math
import jax
import jax.numpy as jnp
from jax import lax

BX = 6
BY = 6
BZ = 128
SLOTS = 1
NV = 642
TRI = 1280
BLOCKS_X = 16
BLOCKS_Y = 8
BLOCKS_Z = 8
NX = 96
NY = 48
NZ = 1024
VERTS = 642


def draw_stencil_base(key, part):
    key = jax.random.fold_in(key, 11)
    centre_key, offset_key = jax.random.split(key)
    block_sizes = jnp.array([BX, BY, BZ], jnp.int32)
    centres = jax.random.randint(centre_key, (BLOCKS_X, BLOCKS_Y, BLOCKS_Z, 3, SLOTS, 1), 0, block_sizes.reshape(3, 1, 1))
    shifts = jax.random.randint(offset_key, (BLOCKS_X, BLOCKS_Y, BLOCKS_Z, 3, SLOTS, NV), -3, 3)
    centres = centres.at[0, 0, 0, :, 0, 0].set(0)
    centres = centres.at[BLOCKS_X - 1, BLOCKS_Y - 1, BLOCKS_Z - 1, :, 0, 0].set(block_sizes - 1)
    shifts = shifts.at[0, 0, 0, :, 0, 0].set(-3)
    shifts = shifts.at[BLOCKS_X - 1, BLOCKS_Y - 1, BLOCKS_Z - 1, :, 0, 0].set(2)
    stencil = centres + shifts - 1
    return stencil.reshape(BLOCKS_X, BLOCKS_Y, BLOCKS_Z, 3, SLOTS * NV).astype(jnp.int32)


def draw_occupied_cell_slots(key, part):
    key = jax.random.fold_in(key, 23)
    rolled = jax.random.randint(key, (BLOCKS_X, BLOCKS_Y, BLOCKS_Z), 0, SLOTS + 2)
    occupied = jnp.minimum(rolled, SLOTS)
    occupied = occupied.at[0, 0, 0].set(SLOTS)
    occupied = occupied.at[BLOCKS_X - 1, BLOCKS_Y - 1, BLOCKS_Z - 1].set(0)
    return occupied.astype(jnp.int32)


def draw_triangles(key, part):
    key = jax.random.fold_in(key, 37)
    second_key, third_key = jax.random.split(key)
    first_vertex = jnp.arange(TRI, dtype=jnp.int32) % NV
    second = (first_vertex + 1 + jax.random.randint(second_key, (TRI,), 0, NV // 2 - 1)) % NV
    third_vertex = (second + 1 + jax.random.randint(third_key, (TRI,), 0, NV // 2 - 1)) % NV
    return jnp.stack([first_vertex, second, third_vertex], axis=1).astype(jnp.int32)


def with_ends(values, rng, smallest, largest):
    longest = values.shape.index(max(values.shape))
    spots = []
    for shift in (0, 1):
        where = [jax.random.randint(jax.random.fold_in(rng, axis), (), 0, length) for axis, length in enumerate(values.shape)]
        where[longest] = (where[longest] + shift) % values.shape[longest]
        spots.append(tuple(where))
    return values.at[spots[0]].set(smallest).at[spots[1]].set(largest)


def block_levels(stream_key, dims, cuts, least, top_value):
    level, own = 1.0, jax.random.fold_in(stream_key, 6)
    for dim, blocks in cuts:
        draws = jnp.exp(jax.random.uniform(jax.random.fold_in(own, dim), (blocks,), jnp.float32, least / len(cuts), top_value / len(cuts)))
        level = level * jnp.repeat(draws, dims[dim] // blocks).reshape([-1 if axis == dim else 1 for axis in range(len(dims))])
    return level


def setup_inputs(seed: int = 0) -> dict:
    keys = jax.random.split(jax.random.key(seed), 7)
    populations = jnp.clip(0.01 + 0.19 * jax.random.uniform(keys[0], (19, NX, NY, NZ), jnp.float32) ** block_levels(keys[0], (19, NX, NY, NZ), ((1, 16), (2, 8), (3, 8)), -0.2, 0.2), 0.01, 0.2)
    fluid_mask = with_ends((jax.random.randint(keys[1], (NX, NY, NZ), 0, 10) < 9).astype(jnp.int32), jax.random.fold_in(keys[1], 1), 0, 1)
    stencil_base = draw_stencil_base(jax.random.fold_in(keys[6], 71), 0)
    offsets = jnp.clip(1.0 * jax.random.uniform(keys[3], (BLOCKS_X, BLOCKS_Y, BLOCKS_Z, 3, VERTS), jnp.float32) ** block_levels(keys[3], (BLOCKS_X, BLOCKS_Y, BLOCKS_Z, 3, VERTS), ((0, 16), (1, 8), (2, 8)), -0.2, 0.2), 0.0, 1.0)
    occupied_cell_slots = draw_occupied_cell_slots(jax.random.fold_in(keys[6], 71), 0)
    triangles = draw_triangles(jax.random.fold_in(keys[6], 71), 0)
    return dict(populations=populations, fluid_mask=fluid_mask, stencil_base=stencil_base, offsets=offsets, occupied_cell_slots=occupied_cell_slots, triangles=triangles)


LATTICE = ((0, 0, 0), (1, 0, 0), (-1, 0, 0), (0, 1, 0), (0, -1, 0), (0, 0, 1), (0, 0, -1),
           (1, 1, 0), (-1, -1, 0), (1, -1, 0), (-1, 1, 0), (1, 0, 1), (-1, 0, -1),
           (1, 0, -1), (-1, 0, 1), (0, 1, 1), (0, -1, -1), (0, 1, -1), (0, -1, 1))
RELAX_TIME = 0.8
STIFFNESS = 0.1
REST_LENGTH = 4.0


def lattice_weight(direction):
    if direction == 0:
        return 1.0 / 3.0
    if direction <= 6:
        return 1.0 / 18.0
    return 1.0 / 36.0


def opposite(direction):
    if direction == 0:
        return 0
    if direction % 2 == 1:
        return direction + 1
    return direction - 1


def moments(populations):
    density = jnp.sum(populations, axis=0)
    momentum = []
    for axis in range(3):
        running = jnp.zeros_like(density)
        for direction, vector in enumerate(LATTICE):
            if vector[axis] != 0:
                running = running + float(vector[axis]) * populations[direction]
        momentum.append(running)
    return density, jnp.stack(momentum)


def collide(populations, density, momentum, vertex_forces):
    velocity = [(momentum[axis] + 0.5 * vertex_forces[axis]) / density for axis in range(3)]
    speed_squared = velocity[0] * velocity[0] + velocity[1] * velocity[1] + velocity[2] * velocity[2]
    factor = 1.0 - 0.5 / RELAX_TIME
    result = []
    for direction, vector in enumerate(LATTICE):
        weight = lattice_weight(direction)
        projection = jnp.zeros_like(density)
        force_dot = jnp.zeros_like(density)
        shift_dot = jnp.zeros_like(density)
        for axis in range(3):
            step = float(vector[axis])
            projection = projection + step * velocity[axis]
            force_dot = force_dot + step * vertex_forces[axis]
            shift_dot = shift_dot + (step - velocity[axis]) * vertex_forces[axis]
        equilibrium = weight * density * (1.0 + 3.0 * projection + 4.5 * projection * projection - 1.5 * speed_squared)
        source_term = factor * weight * (3.0 * shift_dot + 9.0 * projection * force_dot)
        result.append(populations[direction] - (populations[direction] - equilibrium) / RELAX_TIME + source_term)
    return jnp.stack(result)


def stream(collided, extended, fluid_ext):
    size_x, size_y, size_z = collided.shape[1:]
    arrived = []
    for direction, vector in enumerate(LATTICE):
        low_x, low_y, low_z = 1 - vector[0], 1 - vector[1], 1 - vector[2]
        source = extended[direction, low_x:low_x + size_x, low_y:low_y + size_y, low_z:low_z + size_z]
        open_flag = fluid_ext[low_x:low_x + size_x, low_y:low_y + size_y, low_z:low_z + size_z]
        arrived.append(jnp.where(open_flag > 0.5, source, collided[opposite(direction)]))
    return jnp.stack(arrived)


def kernel_weights(coordinate, corner_row, fraction_row):
    offset = coordinate[:, None] - corner_row[None, :]
    distance = offset.astype(jnp.float32) - 1.0 - fraction_row[None, :]
    inside = (offset >= 0) & (offset <= 3)
    return jnp.where(inside, 0.25 * (1.0 + jnp.cos(0.5 * math.pi * distance)), 0.0)


def compute_membrane_force(stencil_corner, corner_fraction, slot_alive_flags, triangles):
    position = (stencil_corner.astype(jnp.float32) + 1.0 + corner_fraction).reshape(3, -1, NV)
    vertex_forces = jnp.zeros_like(position)
    for first_corner, second_corner in ((0, 1), (1, 2), (2, 0)):
        anchor_pos = position[:, :, triangles[:, first_corner]]
        target_pos = position[:, :, triangles[:, second_corner]]
        edge_vector = target_pos - anchor_pos
        stretch = jnp.sum(edge_vector * edge_vector, axis=0) / (REST_LENGTH * REST_LENGTH)
        tension = STIFFNESS * (stretch - 1.0)[None] * edge_vector
        vertex_forces = vertex_forces.at[:, :, triangles[:, first_corner]].add(tension)
        vertex_forces = vertex_forces.at[:, :, triangles[:, second_corner]].add(-tension)
    return vertex_forces.reshape(3, -1) * slot_alive_flags[None, :]


def spread_block(stencil_corner, corner_fraction, vertex_load, lower, extents):
    weight_x = kernel_weights(jnp.arange(extents[0], dtype=jnp.int32) + lower, stencil_corner[0], corner_fraction[0])
    weight_y = kernel_weights(jnp.arange(extents[1], dtype=jnp.int32) + lower, stencil_corner[1], corner_fraction[1])
    weight_z = kernel_weights(jnp.arange(extents[2], dtype=jnp.int32) + lower, stencil_corner[2], corner_fraction[2])
    weighted = weight_x[None, :, None, :] * weight_y[None, None, :, :] * vertex_load[:, None, None, :]
    weighted = weighted.reshape(3 * extents[0] * extents[1], -1)
    spread_grid = jnp.dot(weighted, weight_z.T, precision=lax.Precision.HIGHEST, preferred_element_type=jnp.float32)
    return spread_grid.reshape(3, extents[0], extents[1], extents[2])


def interpolate_velocity(field, stencil_corner, corner_fraction, lower):
    extent_x, extent_y, extent_z = field.shape[1:]
    weight_x = kernel_weights(jnp.arange(extent_x, dtype=jnp.int32) + lower, stencil_corner[0], corner_fraction[0])
    weight_y = kernel_weights(jnp.arange(extent_y, dtype=jnp.int32) + lower, stencil_corner[1], corner_fraction[1])
    weight_z = kernel_weights(jnp.arange(extent_z, dtype=jnp.int32) + lower, stencil_corner[2], corner_fraction[2])
    projected = jnp.dot(field.reshape(-1, extent_z), weight_z, precision=lax.Precision.HIGHEST, preferred_element_type=jnp.float32)
    projected = projected.reshape(3, extent_x, extent_y, -1)
    return jnp.einsum("cxyv,xv,yv->cv", projected, weight_x, weight_y, precision=lax.Precision.HIGHEST)


def reference(populations, fluid_mask, stencil_base, offsets, occupied_cell_slots, triangles):
    device_vertex_total = BLOCKS_X * BLOCKS_Y * BLOCKS_Z
    density, momentum = moments(populations)
    flow_velocity = momentum / density[None]
    stencil_corners = stencil_base.reshape(device_vertex_total, 3, VERTS)
    corner_fractions = offsets.reshape(device_vertex_total, 3, VERTS)
    cell_slot_index = jnp.arange(VERTS, dtype=jnp.int32) // NV
    slot_alive_flags = (cell_slot_index[None, :] < occupied_cell_slots.reshape(device_vertex_total, 1)).astype(jnp.float32)
    slot_numbers = jnp.arange(device_vertex_total, dtype=jnp.int32)

    def block_anchor(number):
        place_x = number // (BLOCKS_Y * BLOCKS_Z)
        place_y = (number // BLOCKS_Z) % BLOCKS_Y
        place_z = number % BLOCKS_Z
        return (jnp.int32(0), (place_x * BX).astype(jnp.int32), (place_y * BY).astype(jnp.int32), (place_z * BZ).astype(jnp.int32))

    device_loads = lax.map(lambda cell_record: compute_membrane_force(cell_record[0], cell_record[1], cell_record[2], triangles), (stencil_corners, corner_fractions, slot_alive_flags))

    def add_device(running, cell_record):
        number, stencil_corner, corner_fraction, vertex_load = cell_record
        window = spread_block(stencil_corner, corner_fraction, vertex_load, -4, (BX + 8, BY + 8, BZ + 8))
        anchor = block_anchor(number)
        current = lax.dynamic_slice(running, anchor, window.shape)
        return lax.dynamic_update_slice(running, current + window, anchor), None

    padded_force = jnp.zeros((3, NX + 8, NY + 8, NZ + 8), jnp.float32)
    padded_force, _ = lax.scan(add_device, padded_force, (slot_numbers, stencil_corners, corner_fractions, device_loads))
    vertex_forces = padded_force[:, 4:-4, 4:-4, 4:-4]
    collided = collide(populations, density, momentum, vertex_forces)
    padded = jnp.pad(collided, ((0, 0), (1, 1), (1, 1), (1, 1)))
    padded_flag = jnp.pad(fluid_mask.astype(jnp.float32), 1)
    next_populations = stream(collided, padded, padded_flag)
    padded_velocity = jnp.pad(flow_velocity, ((0, 0), (4, 4), (4, 4), (4, 4)))

    def sample_device_cells(cell_record):
        number, stencil_corner, corner_fraction, alive = cell_record
        window = lax.dynamic_slice(padded_velocity, block_anchor(number), (3, BX + 8, BY + 8, BZ + 8))
        return interpolate_velocity(window, stencil_corner, corner_fraction, -4) * alive[None, :]

    vertex_velocities = lax.map(sample_device_cells, (slot_numbers, stencil_corners, corner_fractions, slot_alive_flags))
    return next_populations, vertex_velocities.reshape(BLOCKS_X, BLOCKS_Y, BLOCKS_Z, 3, VERTS)
```

```python
import functools
import itertools
import math

import jax
import jax.numpy as jnp
from jax import lax
from jax.experimental import pallas as pl
from jax.experimental.pallas import tpu as pltpu
from jax.sharding import PartitionSpec as P

MESH = pl.DeviceIdType.MESH
AXES = ("gx", "gy", "gz")
NV = 642
VP = 768
NT = 1280
BX, BY, BZ = 6, 6, 128
F32, BF16, I32 = jnp.float32, jnp.bfloat16, jnp.int32
FAR = -10000
STIFFNESS, REST, TAU = 0.1, 4.0, 0.8

LATTICE = (
    (0, 0, 0),
    (1, 0, 0),
    (-1, 0, 0),
    (0, 1, 0),
    (0, -1, 0),
    (0, 0, 1),
    (0, 0, -1),
    (1, 1, 0),
    (-1, -1, 0),
    (1, -1, 0),
    (-1, 1, 0),
    (1, 0, 1),
    (-1, 0, -1),
    (1, 0, -1),
    (-1, 0, 1),
    (0, 1, 1),
    (0, -1, -1),
    (0, 1, -1),
    (0, -1, 1),
)
WEIGHT = [1.0 / 3.0] + [1.0 / 18.0] * 6 + [1.0 / 36.0] * 12
NUMBER = {c: q for q, c in enumerate(LATTICE)}

RHO, FLAG, VEL = 19, 20, 21

FACE = {
    (1, 0): ({1: 1, 7: 7, 3: 11, 5: 13, 2: 9}, 0, 4),
    (-1, 0): ({2: 2, 0: 8, 4: 12, 6: 14, 3: 10}, 1, 5),
    (0, 1): ({3: 3, 7: 7, 2: 10, 1: 17, 0: 15}, 4, 5),
    (0, -1): ({4: 4, 0: 8, 1: 9, 2: 18, 3: 16}, 5, 6),
    (1, 1): ({7: 7}, 3, 4),
    (1, -1): ({1: 9}, 3, 4),
    (-1, 1): ({2: 10}, 3, 4),
    (-1, -1): ({0: 8}, 3, 4),
}
TRAVELS = [d for d in itertools.product((-1, 0, 1), repeat=3) if d != (0, 0, 0)]
TRAVELS.sort(key=lambda d: (d[0] == 0, d[2] != 0, d[1] != 0))


def layout():
    where, row = {}, 0
    for d in TRAVELS:
        dx, dy, dz = d
        rows = {}
        rows["F"] = (16 if dz == 0 else 8) * (2 if dx == 0 else 1)
        if dz == 0:
            rows["U"] = 96 if dy == 0 else (72 if dx == 0 else 48)
            rows["R"] = 8 if dx and dy else 48
        elif dx:
            rows["Z"] = 8
        else:
            rows["Z"] = 16 if dy else 64
        spot, begin = {}, row
        for part, count in rows.items():
            spot[part] = row
            row += count
        where[d] = (begin, row - begin, spot)
    return where, row


WHERE, ROWS = layout()


def iota(shape, axis):
    return lax.broadcasted_iota(I32, shape, axis)


def bits(index, members):
    code = sum(1 << m for m in members)
    return (lax.shift_right_logical(jnp.full(index.shape, code, I32), index) & 1) == 1


def per_row(sub, values):
    out = jnp.zeros(sub.shape, F32)
    for value in sorted(set(values)):
        if value != 0:
            members = [r for r, v in enumerate(values) if v == value]
            out = jnp.where(bits(sub, members), F32(value), out)
    return out


def constants(sub, numbers):
    rows = [[0 if q is None else LATTICE[q][a] for q in numbers] for a in range(3)]
    rows.append([0 if q is None else WEIGHT[q] for q in numbers])
    return [per_row(sub, r) for r in rows]


def natural_numbers(k):
    return [q if q < 19 else None for q in range(8 * k, 8 * k + 8)]


def sin_half_pi(f):
    t = f * (0.5 * math.pi)
    t2 = t * t
    out = jnp.full(f.shape, 1.0 / math.factorial(13), F32)
    for k in (11, 9, 7, 5, 3, 1):
        sign = 1.0 if (13 - k) // 2 % 2 == 0 else -1.0
        out = out * t2 + sign / math.factorial(k)
    return out * t


def node_weights(n, base, four):
    d = n - base
    out = jnp.where(d == 3, four[3], 0.0)
    for k in (2, 1, 0):
        out = jnp.where(d == k, four[k], out)
    return out


def four_weights(frac, axis):
    s = sin_half_pi(frac)[axis : axis + 1]
    c = sin_half_pi(1.0 - frac)[axis : axis + 1]
    return [0.25 * (1.0 - s), 0.25 * (1.0 + c), 0.25 * (1.0 + s), 0.25 * (1.0 - c)]


def halves(x):
    hi = x.astype(BF16)
    return hi, (x - hi.astype(F32)).astype(BF16)


def thirds(x):
    hi = x.astype(BF16)
    rest = x - hi.astype(F32)
    mid = rest.astype(BF16)
    return jnp.concatenate([hi, mid, (rest - mid.astype(F32)).astype(BF16)], axis=0)


def dot(a, b, ca, cb):
    return lax.dot_general(a, b, (((ca,), (cb,)), ((), ())), preferred_element_type=F32)


def load_vertices(base, off, base_s, off_s):
    base_s[...] = jnp.full((8, VP), FAR, I32)
    off_s[...] = jnp.zeros((8, VP), F32)
    for a in range(3):
        base_s[a : a + 1, 0:NV] = base[a]
        off_s[a : a + 1, 0:NV] = off[a]


def membrane(base_s, off_s, alive, tri, incidence, mono):
    def fill(step, carry):
        rows = pl.multiple_of(step * 16, 16)
        vertex = iota((16, NT), 0) + rows
        hit = (vertex == tri[0:1]) | (vertex == tri[1:2]) | (vertex == tri[2:3])
        incidence[pl.ds(rows, 16), :] = jnp.where(hit, 1.0, 0.0).astype(BF16)
        return carry

    lax.fori_loop(0, 41, fill, 0)
    incidence[656:VP, :] = jnp.zeros((VP - 656, NT), BF16)
    base = base_s[...]
    real = base > FAR // 2
    low = jnp.min(jnp.where(real, base, 1 << 20), axis=1, keepdims=True)
    at = jnp.where(real, (base - low - 3).astype(F32) + off_s[...], 0.0)
    x = [at[a : a + 1] for a in range(3)]
    r2 = x[0] * x[0] + x[1] * x[1] + x[2] * x[2]
    pairs = ((0, 0), (1, 1), (2, 2), (0, 1), (0, 2), (1, 2))
    rows = [(r2 - REST * REST) * v for v in x] + [x[a] * x[b] for a, b in pairs] + x
    mono[...] = jnp.zeros((16, VP), F32)
    for r, value in enumerate(rows):
        mono[r : r + 1, :] = value
    mono[12:13, :] = jnp.ones((1, VP), F32)
    sums = dot(thirds(mono[...]), incidence[...], 1, 0)
    sums = sums[0:16] + sums[16:32] + sums[32:48]
    back = dot(thirds(sums), incidence[...], 1, 1)
    back = back[0:16] + back[16:32] + back[32:48]
    row = [back[r : r + 1] for r in range(13)]
    xx = {}
    for k, (a, b) in enumerate(pairs):
        xx[a, b] = xx[b, a] = row[3 + k]
    lin, count = row[9:12], row[12]
    along = x[0] * lin[0] + x[1] * lin[1] + x[2] * lin[2]
    trace = xx[0, 0] + xx[1, 1] + xx[2, 2]
    common = 2.0 * along - r2 * count - (trace - REST * REST * count)
    loads = []
    for a in range(3):
        turned = xx[a, 0] * x[0] + xx[a, 1] * x[1] + xx[a, 2] * x[2]
        total = row[a] - 2.0 * turned + r2 * lin[a] + x[a] * common
        loads.append((STIFFNESS / (REST * REST)) * alive * total)
    return loads


YN = {0: (0, 1, 2, 3, 4, 5, 6, -1), 1: (6, 7, 8, 9, 10, 11, 12, 5), -1: (-6, -5, -4, -3, -2, -1, 0, -7)}
DYS = (0, 1, -1)


def spread_own(base_s, off_s, loads, outer, mid):
    base, frac = base_s[...], off_s[...]
    four = [four_weights(frac, a) for a in range(3)]
    real = base[2:3] > FAR // 2
    low = jnp.min(jnp.where(real, base[2:3], 1 << 20), axis=1, keepdims=True)
    k = iota((32, 1), 0)
    z = jnp.where(k < 16, low + k, jnp.where(k < 24, 127 - 16 + k, -7 - 24 + k))
    wz = node_weights(z, base[2:3], four[2])
    left = jnp.concatenate([wz * load for load in loads], axis=0)
    wx = node_weights(iota((16, 1), 0) - 4, base[0:1], four[0])
    row8 = iota((8, 1), 0)
    for i, dy in enumerate(DYS):
        n = jnp.where(row8 == 7, YN[dy][7], row8 + YN[dy][0])
        wy = node_weights(n, base[1:2], four[1])
        for j in range(5):
            outer[i * 128 + j * 8 : i * 128 + j * 8 + 8, :] = wx[9 + j : 10 + j] * wy
            outer[i * 128 + 40 + j * 8 : i * 128 + 48 + j * 8, :] = wx[j : j + 1] * wy
        outer[i * 128 + 80 : i * 128 + 128, :] = jnp.zeros((48, VP), F32)
        for j in range(8):
            mid[i * 64 + j * 8 : i * 64 + j * 8 + 8, :] = wx[3 + j : 4 + j] * wy
    l_hi, l_lo = halves(left)
    both = jnp.concatenate([l_hi, l_lo], axis=0)

    def product(ref):
        r_hi, r_lo = halves(ref[...])
        out = dot(both, r_hi, 1, 1)
        return out[0:96] + out[96:192] + dot(l_hi, r_lo, 1, 1)

    return product(outer), product(mid), z[0:16].astype(F32)


def roll(x, shift, axis):
    shift = shift % x.shape[axis]
    return x if shift == 0 else pltpu.roll(x, shift, axis)


def force_pieces(outer, mid, z16, lane, dx, dy, dz, put):
    k0, kn = {0: (0, 16), 1: (16, 8), -1: (24, 8)}[dz]
    i = DYS.index(dy)
    lane = iota((kn, 128), 1)
    if dx:
        off = 0 if dx == 1 else 40
        out = jnp.zeros((kn, 128), F32)
        for c in range(3):
            tile = outer[32 * c + k0 : 32 * c + k0 + kn, i * 128 : i * 128 + 128]
            tile = roll(tile, 40 * c - off, 1)
            out = jnp.where((lane >= 40 * c) & (lane < 40 * c + 40), tile, out)
        if dz == 0:
            out = jnp.where(lane >= 120, z16, out)
        put(0, out)
        return
    tiles = []
    for c in range(3):
        t = i // 2 * 128
        tile = mid[32 * c + k0 : 32 * c + k0 + kn, t : t + (128 if i < 2 else 64)]
        if i == 2:
            tile = jnp.concatenate([tile, jnp.zeros((kn, 64), F32)], axis=1)
        tiles.append(roll(tile, 64 * (c % 2) - 64 * (i % 2), 1))
    put(0, jnp.where(lane < 64, tiles[0], tiles[1]))
    rest = z16 if dz == 0 else jnp.zeros((kn, 128), F32)
    put(kn, jnp.where(lane < 64, tiles[2], rest))


def pack(tiles, lane):
    out = jnp.zeros((8, 128), F32)
    for s, tile in enumerate(tiles):
        out = jnp.where((lane >= 8 * s) & (lane < 8 * s + 8), roll(tile, 4 + 8 * s, 1), out)
    return out


def unpack(packed, s):
    return roll(packed, -(4 + 8 * (s % 16)), 1)


def coords():
    return [lax.axis_index(a) for a in AXES]


def present(sizes, me, d):
    ok = None
    for m, s, size in zip(me, d, sizes):
        if s:
            here = m < size - 1 if s == 1 else m > 0
            ok = here if ok is None else jnp.logical_and(ok, here)
    return ok


def kernel_a(sizes, pops, mask, base, off, occ, tri, col, vel, ownf, recv, send, base_s, off_s, incidence, mono, outer, mid, vout, rho_s, edge_s, zero, send_sem, recv_sem, zero_sem):
    me = coords()
    barrier = pltpu.get_barrier_semaphore()
    count = jnp.int32(0)
    for d in TRAVELS:
        ok = present(sizes, me, d)
        count = count + ok.astype(I32)

        @pl.when(ok)
        def _():
            there = tuple(m + s for m, s in zip(me, d))
            pl.semaphore_signal(barrier, inc=1, device_id=there, device_id_type=MESH)

    lane = iota((8, 128), 1)
    sub = iota((8, 128), 0)
    zero[...] = jnp.zeros(zero.shape, F32)

    def blank(d):
        begin, rows, _ = WHERE[d]
        return pltpu.make_async_copy(zero.at[pl.ds(0, rows)], recv.at[pl.ds(begin, rows)], zero_sem.at[TRAVELS.index(d)])

    def back(d):
        return tuple(-s for s in d)

    for d in TRAVELS:

        @pl.when(jnp.logical_not(present(sizes, me, back(d))))
        def _():
            blank(d).start()

    cs = [constants(sub, natural_numbers(k)) for k in range(3)]
    vout[...] = jnp.zeros(vout.shape, F32)
    rho_s[...] = jnp.zeros(rho_s.shape, F32)
    flags = mask[...].astype(F32)

    def columns(x, carry):
        for y in range(BY):
            i = x * BY + y
            col[i, 16:24, :] = jnp.zeros((8, 128), F32)
            col[i, 0:19, :] = pops[i]
            v = [col[i, 8 * k : 8 * k + 8, :] for k in range(3)]
            rho = jnp.sum(v[0] + v[1] + v[2], axis=0, keepdims=True)
            col[i, RHO : RHO + 1, :] = rho
            rho_s[x, y : y + 1, :] = rho
            col[i, FLAG : FLAG + 1, :] = mask[x, y : y + 1, :].astype(F32)
            for a in range(3):
                m = v[0] * cs[0][a] + v[1] * cs[1][a] + v[2] * cs[2][a]
                u = jnp.sum(m, axis=0, keepdims=True) / rho
                col[i, VEL + a : VEL + a + 1, :] = u
                vout[a, x, y : y + 1, :] = u
        return carry

    lax.fori_loop(0, BX, columns, 0)
    vel[...] = vout[...]
    for e, (dx, dy) in enumerate(((1, 0), (-1, 0), (0, 1), (0, -1))):
        up, down = NUMBER[dx, dy, 1], NUMBER[dx, dy, -1]
        edge_s[e] = jnp.zeros((24, 128), F32)
        for j in range(6):
            i = (5 if dx == 1 else 0) * BY + j if dx else j * BY + (5 if dy == 1 else 0)
            both = jnp.where(lane[0:1] >= 64, col[i, up : up + 1, :], col[i, down : down + 1, :])
            edge_s[e, j : j + 1, :] = both
            edge_s[e, 8 + j : 9 + j, :] = col[i, RHO : RHO + 1, :]
            edge_s[e, 16 + j : 17 + j, :] = col[i, FLAG : FLAG + 1, :]

    def ring_tile(i, face):
        rows, r_rho, r_flag = FACE[face]
        out = jnp.where(sub == r_rho, col[i, RHO : RHO + 1, :], col[i, FLAG : FLAG + 1, :])
        moves = {}
        for r, q in rows.items():
            moves.setdefault((q // 8, (r - q) % 8), []).append(r)
        for (k, shift), members in moves.items():
            out = jnp.where(bits(sub, members), roll(col[i, 8 * k : 8 * k + 8, :], shift, 0), out)
        return out

    packs = {}
    for e, dx in ((0, 1), (1, -1)):
        xs = range(2, 6) if dx == 1 else range(4)
        tiles = [vout[a, x] for a in range(3) for x in xs]
        tiles += [edge_s[e, 8 * t : 8 * t + 8, :] for t in range(3)]
        packs[dx] = pack(tiles, lane)
    us = [vout[a, x] for a in range(3) for x in range(6)]
    first = pack(us[:16], lane)
    for d in TRAVELS:
        dx, dy, dz = d
        spot = WHERE[d][2]
        if dz:
            z = spot["Z"]
            if dx:
                send[z : z + 8, :] = packs[dx]
            elif dy:
                e = 2 if dy == 1 else 3
                send[z : z + 8, :] = first
                send[z + 8 : z + 16, :] = pack(us[16:] + [edge_s[e, 8 * t : 8 * t + 8, :] for t in range(3)], lane)
            continue
        u, r = spot["U"], spot["R"]
        xs = {0: range(6), 1: range(2, 6), -1: range(4)}[dx]
        if dy == 0:
            for t, (a, x) in enumerate(itertools.product(range(3), xs)):
                send[u + 8 * t : u + 8 * t + 8, :] = vout[a, x]
        else:
            half = len(xs) // 2
            for t, (a, j) in enumerate(itertools.product(range(3), range(half))):
                one, two = vout[a, xs[2 * j]], vout[a, xs[2 * j + 1]]
                if dy == 1:
                    tile = jnp.where(sub >= 4, roll(one, 2, 0), roll(two, 6, 0))
                else:
                    tile = jnp.where(bits(sub, (0, 1, 6, 7)), roll(one, 6, 0), roll(two, 2, 0))
                send[u + 8 * t : u + 8 * t + 8, :] = tile
        if dx and dy:
            i = (5 if dx == 1 else 0) * BY + (5 if dy == 1 else 0)
            send[r : r + 8, :] = ring_tile(i, (dx, dy))
        else:
            for j in range(6):
                i = (5 if dx == 1 else 0) * BY + j if dx else j * BY + (5 if dy == 1 else 0)
                send[r + 8 * j : r + 8 * j + 8, :] = ring_tile(i, (dx, dy))
    for dz in (1, -1):
        z = WHERE[0, 0, dz][2]["Z"]
        if dz == 1:
            for t in range(8):
                tiles = []
                for s in range(16 * t, min(16 * t + 16, 126)):
                    tiles.append(col[s // 3, 8 * (s % 3) : 8 * (s % 3) + 8, :] if s < 108 else us[s - 108])
                send[z + 8 * t : z + 8 * t + 8, :] = pack(tiles, lane)
            done = z
        else:
            send[z : z + 64, :] = send[done : done + 64, :]

    load_vertices(base, off, base_s, off_s)
    alive = (occ[...] > 0).astype(F32)
    loads = membrane(base_s, off_s, alive, tri, incidence, mono)
    f_outer, f_mid, z16 = spread_own(base_s, off_s, loads, outer, mid)

    def own_put(k, tile):
        ownf[k : k + tile.shape[0], :] = tile

    force_pieces(f_outer, f_mid, z16, lane, 0, 0, 0, own_put)
    for d in TRAVELS:

        def put(k, tile, f=WHERE[d][2]["F"]):
            send[f + k : f + k + tile.shape[0], :] = tile

        force_pieces(f_outer, f_mid, z16, lane, *d, put)

    pl.semaphore_wait(barrier, count)

    def message(d):
        begin, rows, _ = WHERE[d]
        t = TRAVELS.index(d)
        return pltpu.make_async_remote_copy(
            src_ref=send.at[pl.ds(begin, rows)],
            dst_ref=recv.at[pl.ds(begin, rows)],
            send_sem=send_sem.at[t],
            recv_sem=recv_sem.at[t],
            device_id=tuple(m + s for m, s in zip(me, d)),
            device_id_type=MESH,
        )

    for d in TRAVELS:

        @pl.when(present(sizes, me, d))
        def _():
            message(d).start()

    for d in TRAVELS:

        @pl.when(present(sizes, me, d))
        def _():
            message(d).wait_send()

        @pl.when(present(sizes, me, back(d)))
        def _():
            message(d).wait_recv()

        @pl.when(jnp.logical_not(present(sizes, me, back(d))))
        def _():
            blank(d).wait()


def collide(p, c, rho, u, f):
    inv = 0.5 / rho
    v = [a + inv * b for a, b in zip(u, f)]
    vv = v[0] * v[0] + v[1] * v[1] + v[2] * v[2]
    vf = v[0] * f[0] + v[1] * f[1] + v[2] * f[2]
    factor = 1.0 - 0.5 / TAU
    a0 = (1.0 / TAU) * rho * (1.0 - 1.5 * vv) - (3.0 * factor) * vf
    a1 = (3.0 / TAU) * rho
    a2 = (4.5 / TAU) * rho
    cx, cy, cz, w = c
    pr = cx * v[0] + cy * v[1] + cz * v[2]
    cf = cx * f[0] + cy * f[1] + cz * f[2]
    poly = a0 + pr * (a1 + a2 * pr) + cf * (3.0 * factor + (9.0 * factor) * pr)
    return (1.0 - 1.0 / TAU) * p + w * poly


def forces(recv, ownf, force):
    zl = iota((1, 256), 1)
    zl = jnp.where(zl < 132, zl, jnp.where(zl >= 252, zl - 256, -5000)).astype(F32)
    k8 = iota((8, 1), 0).astype(F32)
    out = {}
    for sx in (-1, 0, 1):
        parts, zs = [], []
        for sy, sz in itertools.product((-1, 0, 1), (0, -1, 1)):
            kn = 8 if sz else 16
            if (sx, sy, sz) == (0, 0, 0):
                ref, f = ownf, 0
            else:
                ref, f = recv, WHERE[-sx, -sy, -sz][2]["F"]
            tile = ref[f : f + kn, :]
            if sx == 0:
                tile = jnp.concatenate([tile, ref[f + kn : f + 2 * kn, :]], axis=1)
            parts.append(tile)
            if sz == 0:
                zs.append(tile[:, 120:121] if sx else tile[:, 192:193])
            else:
                zs.append(k8 + (-1.0 if sz == -1 else 121.0))
        g = jnp.concatenate(parts, axis=0)
        z = jnp.concatenate(zs, axis=0)
        place = jnp.where(z == zl, 1.0, 0.0).astype(BF16)
        hi, lo = halves(g.T)
        out[sx] = dot(hi, place, 1, 0) + dot(lo, place, 1, 0)
    for a, x in itertools.product(range(3), range(8)):
        tile = out[0][64 * a + 8 * x : 64 * a + 8 * x + 8]
        if x < 5:
            tile = tile + out[-1][40 * a + 8 * x : 40 * a + 8 * x + 8]
        if x >= 3:
            tile = tile + out[1][40 * a + 8 * x - 24 : 40 * a + 8 * x - 16]
        force[a, x] = tile


def assemble(recv, vel, ext, lane, sub):
    low4 = (lane & 7) < 4
    above_rows = bits(sub, (0, 1))
    for sx in (-1, 0, 1):
        xs = range(6) if sx == 0 else range(4)
        x0 = {-1: 0, 0: 4, 1: 10}[sx]
        above, below = WHERE[-sx, -1, 0][2]["U"], WHERE[-sx, 1, 0][2]["U"]
        half = len(xs) // 2
        for a, x in itertools.product(range(3), xs):
            if sx == 0:
                own = vel[a, x]
            else:
                u = WHERE[-sx, 0, 0][2]["U"] + 8 * (a * 4 + x)
                own = recv[u : u + 8, :]
            t = 8 * (a * half + x // 2)
            up = recv[above + t : above + t + 8, :]
            dn = recv[below + t : below + t + 8, :]
            if x % 2:
                up, dn = roll(up, 4, 0), roll(dn, 4, 0)
            ext[a, x0 + x, 0:8, 0:128] = jnp.where(sub < 6, own, up)
            ext[a, x0 + x, 8:16, 0:128] = jnp.where(above_rows, up, jnp.where(sub >= 4, dn, 0.0))

        def merged(sy, t):
            lower = WHERE[-sx, -sy, 1][2]["Z"] + 8 * t
            upper = WHERE[-sx, -sy, -1][2]["Z"] + 8 * t
            return jnp.where(low4, recv[lower : lower + 8, :], recv[upper : upper + 8, :])

        count = 3 * len(xs)
        for t in range((count + 15) // 16):
            if sx == 0:
                slots = range(16 * t, min(16 * t + 16, count))
                m_up, m_dn = merged(1, t), merged(-1, t)
            else:
                slots = range(count)
                m_up, m_dn = merged(1, 0), merged(-1, 0)
            m_up, m_dn = roll(m_up, 6, 0), roll(m_dn, 2, 0)
            second = jnp.where(above_rows, m_up, jnp.where(sub >= 4, m_dn, 0.0))
            for s in slots:
                a, x = s // len(xs), s % len(xs)
                own_slot = s + 108 if sx == 0 else s
                own = unpack(merged(0, own_slot // 16), own_slot)
                ext[a, x0 + x, 0:8, 128:256] = jnp.where(sub < 6, own, unpack(m_up, s))
                ext[a, x0 + x, 8:16, 128:256] = unpack(second, s)


def interpolate(ext, base_s, off_s, occ, wz_s, out):
    base, frac = base_s[...], off_s[...]
    four = [four_weights(frac, a) for a in range(3)]
    wx = node_weights(iota((16, 1), 0) - 4, base[0:1], four[0])
    n = iota((16, 1), 0)
    wy = node_weights(jnp.where(n < 10, n, n - 16), base[1:2], four[1])
    wz_s[...] = jnp.zeros(wz_s.shape, F32)
    wz_s[0:136, :] = node_weights(iota((136, 1), 0), base[2:3], four[2])
    wz_s[248:256, :] = node_weights(iota((8, 1), 0) - 8, base[2:3], four[2])
    w_hi, w_lo = halves(wz_s[...])
    alive = (occ[...] > 0).astype(F32)
    for a in range(3):
        e_hi, e_lo = halves(ext[a].reshape(14 * 16, 256))
        p = dot(e_hi, w_hi, 1, 0) + dot(e_lo, w_hi, 1, 0) + dot(e_hi, w_lo, 1, 0)
        total = jnp.zeros((16, VP), F32)
        for x in range(14):
            total = total + p[16 * x : 16 * x + 16] * wx[x : x + 1]
        row = jnp.sum(total * wy, axis=0, keepdims=True) * alive
        out[a] = row[:, 0:NV]


def kernel_b(col, vel, ownf, recv, base, off, occ, nxt, vtx, base_s, off_s, ext, force, raw, moved, wz_s):
    lane = iota((8, 128), 1)
    sub = iota((8, 128), 0)
    load_vertices(base, off, base_s, off_s)
    forces(recv, ownf, force)
    assemble(recv, vel, ext, lane, sub)
    interpolate(ext, base_s, off_s, occ, wz_s, vtx)

    wall = jnp.full((8, 128), jnp.nan, F32)
    low4 = (lane & 7) < 4
    side = jnp.where(lane[0:1] >= 64, 1.0, -1.0)

    def shifts(cz):
        edge = ((cz > 0.5) & (lane == 127)) | ((cz < -0.5) & (lane == 0))

        def move(s, z):
            a = jnp.where(edge, z, s)
            return jnp.where(cz > 0.5, roll(a, 1, 1), jnp.where(cz < -0.5, roll(a, 127, 1), a))

        return move

    cs = [constants(sub, natural_numbers(k)) for k in range(3)]
    movers = [shifts(c[2]) for c in cs]
    z_low = WHERE[0, 0, 1][2]["Z"]
    z_high = WHERE[0, 0, -1][2]["Z"]
    merged = []
    for t in range(7):
        merged.append(jnp.where(low4, recv[z_low + 8 * t : z_low + 8 * t + 8, :], recv[z_high + 8 * t : z_high + 8 * t + 8, :]))
    for x, y in itertools.product(range(BX), range(BY)):
        i = x * BY + y
        rho, flag = col[i, RHO : RHO + 1, :], col[i, FLAG : FLAG + 1, :]
        u = [col[i, VEL + a : VEL + a + 1, :] for a in range(3)]
        f = [force[a, x + 1, y : y + 1, 0:128] for a in range(3)]
        fz = [force[a, x + 1, y : y + 1, 128:256] for a in range(3)]
        zt = [unpack(merged[(3 * i + k) // 16], 3 * i + k) for k in range(3)]
        uz = [zt[2][VEL - 16 + a : VEL - 15 + a] for a in range(3)]
        rho_z, flag_z = zt[2][RHO - 16 : RHO - 15], zt[2][FLAG - 16 : FLAG - 15]
        for k in range(3):
            r = collide(col[i, 8 * k : 8 * k + 8, :], cs[k], rho, u, f)
            raw[i, 8 * k : 8 * k + 8, :] = r
            rz = collide(zt[k], cs[k], rho_z, uz, fz)
            s = jnp.where(flag > 0.5, r, wall)
            sz = jnp.where(flag_z > 0.5, rz, wall)
            moved[x + 1, y + 1, 8 * k : 8 * k + 8, :] = movers[k](s, sz)

    for face, (rows, r_rho, r_flag) in FACE.items():
        dx, dy = face
        numbers = [rows.get(r) for r in range(8)]
        c = constants(sub, numbers)
        mover = shifts(c[2])
        ring = WHERE[dx, dy, 0][2]["R"]
        count = 1 if dx and dy else 6
        if count == 6:
            if dx:
                z = [WHERE[dx, 0, s][2]["Z"] for s in (1, -1)]
                slot = 12
            else:
                z = [WHERE[0, dy, s][2]["Z"] + 8 for s in (1, -1)]
                slot = 2
            pz = jnp.where(low4, recv[z[0] : z[0] + 8, :], recv[z[1] : z[1] + 8, :])
            tz = [unpack(pz, slot + t) for t in range(3)]
            cz = (float(dx), float(dy), side, 1.0 / 36.0)
        for j in range(count):
            x = {1: -1, -1: 6, 0: j}[dx]
            y = {1: -1, -1: 6, 0: j}[dy]
            t = recv[ring + 8 * j : ring + 8 * j + 8, :]
            rho, flag = t[r_rho : r_rho + 1], t[r_flag : r_flag + 1]
            yu, yf = y % 16, y % 8
            u = [ext[a, x + 4, yu : yu + 1, 0:128] for a in range(3)]
            f = [force[a, x + 1, yf : yf + 1, 0:128] for a in range(3)]
            s = jnp.where(flag > 0.5, collide(t, c, rho, u, f), wall)
            if count == 6:
                uz = [ext[a, x + 4, yu : yu + 1, 128:256] for a in range(3)]
                fz = [force[a, x + 1, yf : yf + 1, 128:256] for a in range(3)]
                rz = collide(tz[0][j : j + 1], cz, tz[1][j : j + 1], uz, fz)
                sz = jnp.where(tz[2][j : j + 1] > 0.5, rz, wall[0:1])
                s = mover(s, sz)
            for k in sorted({q // 8 for q in rows.values()}):
                out = None
                for shift in sorted({(q - r) % 8 for r, q in rows.items() if q // 8 == k}):
                    tile = roll(s, shift, 0)
                    members = [q % 8 for r, q in rows.items() if q // 8 == k and (q - r) % 8 == shift]
                    out = tile if out is None else jnp.where(bits(sub, members), tile, out)
                moved[x + 1, y + 1, 8 * k : 8 * k + 8, :] = out

    odd = (iota((24, 128), 0) & 1) == 1
    start = iota((24, 128), 0) == 0
    for x, y in itertools.product(range(BX), range(BY)):
        i = x * BY + y
        r = raw[i]
        turned = jnp.where(start, r, jnp.where(odd, roll(r, 23, 0), roll(r, 1, 0)))
        for k in range(3):
            sources = {}
            for q in natural_numbers(k):
                if q is not None:
                    sources.setdefault(LATTICE[q][:2], []).append(q % 8)
            out = None
            for (cx, cy), members in sources.items():
                tile = moved[x + 1 - cx, y + 1 - cy, 8 * k : 8 * k + 8, :]
                out = tile if out is None else jnp.where(bits(sub, members), tile, out)
            out = jnp.where(out == out, out, turned[8 * k : 8 * k + 8])
            last = min(8 * k + 8, 19)
            nxt[i, 8 * k : last, :] = out[0 : last - 8 * k]


def on_device(sizes, populations, fluid_mask, stencil_base, offsets, occupied_cell_slots, triangles):
    pops = jnp.transpose(populations, (1, 2, 0, 3)).reshape(BX * BY, 19, BZ)
    base = stencil_base.reshape(3, 1, NV)
    off = offsets.reshape(3, 1, NV)
    occ = occupied_cell_slots.reshape(1, 1)
    vmem = pl.BlockSpec(memory_space=pltpu.VMEM)
    anywhere = pl.BlockSpec(memory_space=pl.ANY)
    shape = jax.ShapeDtypeStruct
    col, vel, ownf, recv = pl.pallas_call(
        functools.partial(kernel_a, sizes),
        name="load_and_send",
        out_shape=(shape((36, 24, 128), F32), shape((3, 6, 8, 128), F32), shape((32, 128), F32), shape((ROWS, 128), F32)),
        in_specs=[vmem] * 6,
        out_specs=(vmem, vmem, vmem, anywhere),
        scratch_shapes=[
            pltpu.VMEM((ROWS, 128), F32),
            pltpu.VMEM((8, VP), I32),
            pltpu.VMEM((8, VP), F32),
            pltpu.VMEM((VP, NT), BF16),
            pltpu.VMEM((16, VP), F32),
            pltpu.VMEM((384, VP), F32),
            pltpu.VMEM((192, VP), F32),
            pltpu.VMEM((3, 6, 8, 128), F32),
            pltpu.VMEM((6, 8, 128), F32),
            pltpu.VMEM((4, 24, 128), F32),
            pltpu.VMEM((160, 128), F32),
            pltpu.SemaphoreType.DMA((26,)),
            pltpu.SemaphoreType.DMA((26,)),
            pltpu.SemaphoreType.DMA((26,)),
        ],
        compiler_params=pltpu.CompilerParams(collective_id=0, has_side_effects=True, vmem_limit_bytes=48 << 20),
    )(pops, fluid_mask, base, off, occ, triangles.T)
    nxt, vtx = pl.pallas_call(
        kernel_b,
        name="collide_and_pass",
        out_shape=(shape((36, 19, 128), F32), shape((3, 1, NV), F32)),
        in_specs=[vmem] * 7,
        out_specs=(vmem, vmem),
        scratch_shapes=[
            pltpu.VMEM((8, VP), I32),
            pltpu.VMEM((8, VP), F32),
            pltpu.VMEM((3, 14, 16, 256), F32),
            pltpu.VMEM((3, 8, 8, 256), F32),
            pltpu.VMEM((36, 24, 128), F32),
            pltpu.VMEM((8, 8, 24, 128), F32),
            pltpu.VMEM((256, VP), F32),
        ],
        compiler_params=pltpu.CompilerParams(vmem_limit_bytes=48 << 20),
    )(col, vel, ownf, recv, base, off, occ)
    nxt = jnp.transpose(nxt.reshape(BX, BY, 19, BZ), (2, 0, 1, 3))
    return nxt, vtx.reshape(1, 1, 1, 3, NV)


def solution(mesh):
    sizes = tuple(mesh.shape[a] for a in AXES)
    placed = (
        P(None, "gx", "gy", "gz"),
        P("gx", "gy", "gz"),
        P("gx", "gy", "gz", None, None),
        P("gx", "gy", "gz", None, None),
        P("gx", "gy", "gz"),
        P(),
    )
    return jax.shard_map(
        functools.partial(on_device, sizes),
        mesh=mesh,
        in_specs=placed,
        out_specs=(P(None, "gx", "gy", "gz"), P("gx", "gy", "gz", None, None)),
        check_vma=False,
    )
```

```python
import functools
import itertools
import math

import jax
import jax.numpy as jnp
from jax import lax
from jax.experimental import pallas as pl
from jax.experimental.pallas import tpu as pltpu
from jax.sharding import PartitionSpec as P

MESH = pl.DeviceIdType.MESH
AXES = ("gx", "gy", "gz")
NV = 642
VP = 768
NT = 1280
BX, BY, BZ = 6, 6, 128
F32, BF16, I32 = jnp.float32, jnp.bfloat16, jnp.int32
FAR = -10000
STIFFNESS, REST, TAU = 0.1, 4.0, 0.8

LATTICE = (
    (0, 0, 0),
    (1, 0, 0),
    (-1, 0, 0),
    (0, 1, 0),
    (0, -1, 0),
    (0, 0, 1),
    (0, 0, -1),
    (1, 1, 0),
    (-1, -1, 0),
    (1, -1, 0),
    (-1, 1, 0),
    (1, 0, 1),
    (-1, 0, -1),
    (1, 0, -1),
    (-1, 0, 1),
    (0, 1, 1),
    (0, -1, -1),
    (0, 1, -1),
    (0, -1, 1),
)
WEIGHT = [1.0 / 3.0] + [1.0 / 18.0] * 6 + [1.0 / 36.0] * 12
NUMBER = {c: q for q, c in enumerate(LATTICE)}

RHO, FLAG, VEL = 19, 20, 21

FACE = {
    (1, 0): ({1: 1, 7: 7, 3: 11, 5: 13, 2: 9}, 0, 4),
    (-1, 0): ({2: 2, 0: 8, 4: 12, 6: 14, 3: 10}, 1, 5),
    (0, 1): ({3: 3, 7: 7, 2: 10, 1: 17, 0: 15}, 4, 5),
    (0, -1): ({4: 4, 0: 8, 1: 9, 2: 18, 3: 16}, 5, 6),
    (1, 1): ({7: 7}, 0, 4),
    (1, -1): ({2: 9}, 0, 4),
    (-1, 1): ({3: 10}, 1, 5),
    (-1, -1): ({0: 8}, 1, 5),
}
TRAVELS = [d for d in itertools.product((-1, 0, 1), repeat=3) if d != (0, 0, 0)]
TRAVELS.sort(key=lambda d: (d[0] == 0, d[2] != 0, d[1] != 0))


def layout():
    where, row = {}, 0
    for d in TRAVELS:
        dx, dy, dz = d
        rows = {}
        rows["F"] = (16 if dz == 0 else 8) * (2 if dx == 0 else 1)
        if dz == 0:
            rows["U"] = 48 if dx and dy else 72
            rows["R"] = 8 if dx and dy else 48
        elif dx:
            rows["Z"] = 8
        else:
            rows["Z"] = 16 if dy else 64
        spot, begin = {}, row
        for part, count in rows.items():
            spot[part] = row
            row += count
        where[d] = (begin, row - begin, spot)
    return where, row


WHERE, ROWS = layout()
XROWS = {1: 0, -1: 120}


def iota(shape, axis):
    return lax.broadcasted_iota(I32, shape, axis)


def bits(index, members):
    code = sum(1 << m for m in members)
    return (lax.shift_right_logical(jnp.full(index.shape, code, I32), index) & 1) == 1


def per_row(sub, values):
    out = jnp.zeros(sub.shape, F32)
    for value in sorted(set(values)):
        if value != 0:
            members = [r for r, v in enumerate(values) if v == value]
            out = jnp.where(bits(sub, members), F32(value), out)
    return out


def constants(sub, numbers):
    rows = [[0 if q is None else LATTICE[q][a] for q in numbers] for a in range(3)]
    rows.append([0 if q is None else WEIGHT[q] for q in numbers])
    return [per_row(sub, r) for r in rows]


def natural_numbers(k):
    return [q if q < 19 else None for q in range(8 * k, 8 * k + 8)]


def sin_half_pi(f):
    t = f * (0.5 * math.pi)
    t2 = t * t
    out = jnp.full(f.shape, 1.0 / math.factorial(13), F32)
    for k in (11, 9, 7, 5, 3, 1):
        sign = 1.0 if (13 - k) // 2 % 2 == 0 else -1.0
        out = out * t2 + sign / math.factorial(k)
    return out * t


def node_weights(n, base, four):
    d = n - base
    out = jnp.where(d == 3, four[3], 0.0)
    for k in (2, 1, 0):
        out = jnp.where(d == k, four[k], out)
    return out


def four_weights(frac, axis):
    s = sin_half_pi(frac)[axis : axis + 1]
    c = sin_half_pi(1.0 - frac)[axis : axis + 1]
    return [0.25 * (1.0 - s), 0.25 * (1.0 + c), 0.25 * (1.0 + s), 0.25 * (1.0 - c)]


def halves(x):
    hi = x.astype(BF16)
    return hi, (x - hi.astype(F32)).astype(BF16)


def thirds(x):
    hi = x.astype(BF16)
    rest = x - hi.astype(F32)
    mid = rest.astype(BF16)
    return jnp.concatenate([hi, mid, (rest - mid.astype(F32)).astype(BF16)], axis=0)


def dot(a, b, ca, cb):
    return lax.dot_general(a, b, (((ca,), (cb,)), ((), ())), preferred_element_type=F32)


def load_vertices(base, off, base_s, off_s):
    base_s[...] = jnp.full((8, VP), FAR, I32)
    off_s[...] = jnp.zeros((8, VP), F32)
    for a in range(3):
        base_s[a : a + 1, 0:NV] = base[a]
        off_s[a : a + 1, 0:NV] = off[a]


def membrane(base_s, off_s, alive, tri, incidence, mono):
    def fill(step, carry):
        rows = pl.multiple_of(step * 16, 16)
        vertex = iota((16, NT), 0) + rows
        hit = (vertex == tri[0:1]) | (vertex == tri[1:2]) | (vertex == tri[2:3])
        incidence[pl.ds(rows, 16), :] = jnp.where(hit, 1.0, 0.0).astype(BF16)
        return carry

    lax.fori_loop(0, 41, fill, 0)
    incidence[656:VP, :] = jnp.zeros((VP - 656, NT), BF16)
    base = base_s[...]
    real = base > FAR // 2
    low = jnp.min(jnp.where(real, base, 1 << 20), axis=1, keepdims=True)
    at = jnp.where(real, (base - low - 3).astype(F32) + off_s[...], 0.0)
    x = [at[a : a + 1] for a in range(3)]
    r2 = x[0] * x[0] + x[1] * x[1] + x[2] * x[2]
    pairs = ((0, 0), (1, 1), (2, 2), (0, 1), (0, 2), (1, 2))
    rows = [(r2 - REST * REST) * v for v in x] + [x[a] * x[b] for a, b in pairs] + x
    mono[...] = jnp.zeros((16, VP), F32)
    for r, value in enumerate(rows):
        mono[r : r + 1, :] = value
    mono[12:13, :] = jnp.ones((1, VP), F32)
    sums = dot(thirds(mono[...]), incidence[...], 1, 0)
    sums = sums[0:16] + sums[16:32] + sums[32:48]
    back = dot(thirds(sums), incidence[...], 1, 1)
    back = back[0:16] + back[16:32] + back[32:48]
    row = [back[r : r + 1] for r in range(13)]
    xx = {}
    for k, (a, b) in enumerate(pairs):
        xx[a, b] = xx[b, a] = row[3 + k]
    lin, count = row[9:12], row[12]
    along = x[0] * lin[0] + x[1] * lin[1] + x[2] * lin[2]
    trace = xx[0, 0] + xx[1, 1] + xx[2, 2]
    common = 2.0 * along - r2 * count - (trace - REST * REST * count)
    loads = []
    for a in range(3):
        turned = xx[a, 0] * x[0] + xx[a, 1] * x[1] + xx[a, 2] * x[2]
        total = row[a] - 2.0 * turned + r2 * lin[a] + x[a] * common
        loads.append((STIFFNESS / (REST * REST)) * alive * total)
    return loads


YN = {0: (0, 1, 2, 3, 4, 5, 6, -1), 1: (6, 7, 8, 9, 10, 11, 12, 5), -1: (-6, -5, -4, -3, -2, -1, 0, -7)}
DYS = (0, 1, -1)


def spread_own(base_s, off_s, loads, outer, mid):
    base, frac = base_s[...], off_s[...]
    four = [four_weights(frac, a) for a in range(3)]
    real = base[2:3] > FAR // 2
    low = jnp.min(jnp.where(real, base[2:3], 1 << 20), axis=1, keepdims=True)
    k = iota((32, 1), 0)
    z = jnp.where(k < 16, low + k, jnp.where(k < 24, 127 - 16 + k, -7 - 24 + k))
    wz = node_weights(z, base[2:3], four[2])
    left = jnp.concatenate([wz * load for load in loads], axis=0)
    wx = node_weights(iota((16, 1), 0) - 4, base[0:1], four[0])
    row8 = iota((8, 1), 0)
    for i, dy in enumerate(DYS):
        n = jnp.where(row8 == 7, YN[dy][7], row8 + YN[dy][0])
        wy = node_weights(n, base[1:2], four[1])
        for j in range(5):
            outer[i * 128 + j * 8 : i * 128 + j * 8 + 8, :] = wx[9 + j : 10 + j] * wy
            outer[i * 128 + 40 + j * 8 : i * 128 + 48 + j * 8, :] = wx[j : j + 1] * wy
        outer[i * 128 + 80 : i * 128 + 128, :] = jnp.zeros((48, VP), F32)
        for j in range(8):
            mid[i * 64 + j * 8 : i * 64 + j * 8 + 8, :] = wx[3 + j : 4 + j] * wy
    l_hi, l_lo = halves(left)
    both = jnp.concatenate([l_hi, l_lo], axis=0)

    def product(ref):
        r_hi, r_lo = halves(ref[...])
        out = dot(both, r_hi, 1, 1)
        return out[0:96] + out[96:192] + dot(l_hi, r_lo, 1, 1)

    return product(outer), product(mid), z[0:16].astype(F32)


def roll(x, shift, axis):
    shift = shift % x.shape[axis]
    return x if shift == 0 else pltpu.roll(x, shift, axis)


def force_pieces(outer, mid, z16, lane, dx, dy, dz, put):
    k0, kn = {0: (0, 16), 1: (16, 8), -1: (24, 8)}[dz]
    i = DYS.index(dy)
    lane = iota((kn, 128), 1)
    if dx:
        off = 0 if dx == 1 else 40
        out = jnp.zeros((kn, 128), F32)
        for c in range(3):
            tile = outer[32 * c + k0 : 32 * c + k0 + kn, i * 128 : i * 128 + 128]
            tile = roll(tile, 40 * c - off, 1)
            out = jnp.where((lane >= 40 * c) & (lane < 40 * c + 40), tile, out)
        if dz == 0:
            out = jnp.where(lane >= 120, z16, out)
        put(0, out)
        return
    tiles = []
    for c in range(3):
        t = i // 2 * 128
        tile = mid[32 * c + k0 : 32 * c + k0 + kn, t : t + (128 if i < 2 else 64)]
        if i == 2:
            tile = jnp.concatenate([tile, jnp.zeros((kn, 64), F32)], axis=1)
        tiles.append(roll(tile, 64 * (c % 2) - 64 * (i % 2), 1))
    put(0, jnp.where(lane < 64, tiles[0], tiles[1]))
    rest = z16 if dz == 0 else jnp.zeros((kn, 128), F32)
    put(kn, jnp.where(lane < 64, tiles[2], rest))


def pack(tiles, lane):
    out = jnp.zeros((8, 128), F32)
    for s, tile in enumerate(tiles):
        out = jnp.where((lane >= 8 * s) & (lane < 8 * s + 8), roll(tile, 4 + 8 * s, 1), out)
    return out


def unpack(packed, s):
    return roll(packed, -(4 + 8 * (s % 16)), 1)


def coords():
    return [lax.axis_index(a) for a in AXES]


def present_at(sizes, me, d):
    ok = None
    for m, s, size in zip(me, d, sizes):
        if s:
            here = m < size - 1 if s == 1 else m > 0
            ok = here if ok is None else jnp.logical_and(ok, here)
    return ok


def face_tiles(ref, begin, sub):
    tiles = []
    for a in range(3):
        t = [ref[begin + 8 * (3 * a + j) : begin + 8 * (3 * a + j) + 8, :] for j in range(3)]
        last = jnp.where(sub < 2, roll(t[0], 2, 0), jnp.where(sub < 4, roll(t[1], 4, 0), roll(t[2], 6, 0)))
        tiles += t + [last]
    return tiles


def paired(tiles, half, dy, sub):
    out = []
    for t in range(3 * half):
        one, two = tiles[2 * t], tiles[2 * t + 1]
        if dy == 1:
            out.append(jnp.where(sub >= 4, roll(one, 2, 0), roll(two, 6, 0)))
        else:
            out.append(jnp.where(bits(sub, (0, 1, 6, 7)), roll(one, 6, 0), roll(two, 2, 0)))
    return out


def back(d):
    return tuple(-s for s in d)


def kernel_a(sizes, pops, mask, base, off, occ, tri, col, vel, ownf, base_s, off_s, recvx, recv, send, passed, mask_s, base_v, off_v, tri_v, incidence, mono, outer, mid, edge_s, zero, in_sem, send_sem, recv_sem, fsend_sem, frecv_sem, zero_sem):
    me = coords()
    there = {d: present_at(sizes, me, d) for d in TRAVELS}

    def present(sizes, me, d):
        return there[d]

    ins = [(pops, col.at[:, pl.ds(0, 19), :]), (mask, mask_s), (base, base_v), (off, off_v), (tri, tri_v)]
    ins = [pltpu.make_async_copy(a, b, in_sem.at[k]) for k, (a, b) in enumerate(ins)]
    for copy in ins:
        copy.start()
    def at(d):
        return tuple(m + s for m, s in zip(me, d))

    barrier = pltpu.get_barrier_semaphore()
    count = jnp.int32(0)
    for d in TRAVELS:
        ok = present(sizes, me, d)
        count = count + ok.astype(I32)

        @pl.when(ok)
        def _():
            pl.semaphore_signal(barrier, inc=1, device_id=at(d), device_id_type=MESH)

    lane = iota((8, 128), 1)
    sub = iota((8, 128), 0)
    zero[...] = jnp.zeros(zero.shape, F32)

    def blank(d):
        begin, rows, _ = WHERE[d]
        return pltpu.make_async_copy(zero.at[pl.ds(0, rows)], recv.at[pl.ds(begin, rows)], zero_sem.at[TRAVELS.index(d)])

    for d in TRAVELS:

        @pl.when(jnp.logical_not(present(sizes, me, back(d))))
        def _():
            blank(d).start()

    for dx in (1, -1):

        @pl.when(jnp.logical_not(present(sizes, me, (-dx, 0, 0))))
        def _():
            recvx[XROWS[dx] : XROWS[dx] + 120, :] = jnp.zeros((120, 128), F32)

    cs = [constants(sub, natural_numbers(k)) for k in range(3)]
    vel[...] = jnp.zeros(vel.shape, F32)
    for copy in ins:
        copy.wait()

    def columns(x, carry):
        for y in range(BY):
            i = x * BY + y
            col[i, 19:24, :] = jnp.zeros((5, 128), F32)
            v = [col[i, 8 * k : 8 * k + 8, :] for k in range(3)]
            rho = jnp.sum(v[0] + v[1] + v[2], axis=0, keepdims=True)
            col[i, RHO : RHO + 1, :] = rho
            col[i, FLAG : FLAG + 1, :] = mask_s[x, y : y + 1, :].astype(F32)
            for a in range(3):
                m = v[0] * cs[0][a] + v[1] * cs[1][a] + v[2] * cs[2][a]
                u = jnp.sum(m, axis=0, keepdims=True) / rho
                col[i, VEL + a : VEL + a + 1, :] = u
                vel[a, x, y : y + 1, :] = u
        return carry

    lax.fori_loop(0, BX, columns, 0)

    def ring_tile(i, face):
        rows, r_rho, r_flag = FACE[face]
        out = jnp.where(sub == r_rho, col[i, RHO : RHO + 1, :], col[i, FLAG : FLAG + 1, :])
        moves = {}
        for r, q in rows.items():
            moves.setdefault((q // 8, (r - q) % 8), []).append(r)
        for (k, shift), members in moves.items():
            out = jnp.where(bits(sub, members), roll(col[i, 8 * k : 8 * k + 8, :], shift, 0), out)
        return out

    for dx in (1, -1):
        u, r = WHERE[dx, 0, 0][2]["U"], WHERE[dx, 0, 0][2]["R"]
        xs = range(2, 6) if dx == 1 else range(4)
        for a, j in itertools.product(range(3), range(3)):
            t = u + 8 * (3 * a + j)
            send[t : t + 8, :] = jnp.where(sub < 6, vel[a, xs[j]], roll(vel[a, xs[3]], 6 - 2 * j, 0))
        for y in range(6):
            send[r + 8 * y : r + 8 * y + 8, :] = ring_tile((5 if dx == 1 else 0) * BY + y, (dx, 0))
    us = [vel[a, x] for a in range(3) for x in range(6)]
    first = pack(us[:16], lane)
    for dy in (1, -1):
        u, r = WHERE[0, dy, 0][2]["U"], WHERE[0, dy, 0][2]["R"]
        for t, tile in enumerate(paired(us, 3, dy, sub)):
            send[u + 8 * t : u + 8 * t + 8, :] = tile
        up, down = NUMBER[0, dy, 1], NUMBER[0, dy, -1]
        edge_s[...] = jnp.zeros((24, 128), F32)
        for x in range(6):
            i = x * BY + (5 if dy == 1 else 0)
            send[r + 8 * x : r + 8 * x + 8, :] = ring_tile(i, (0, dy))
            edge_s[x : x + 1, :] = jnp.where(lane[0:1] >= 64, col[i, up : up + 1, :], col[i, down : down + 1, :])
            edge_s[8 + x : 9 + x, :] = col[i, RHO : RHO + 1, :]
            edge_s[16 + x : 17 + x, :] = col[i, FLAG : FLAG + 1, :]
        second = pack(us[16:] + [edge_s[8 * t : 8 * t + 8, :] for t in range(3)], lane)
        for dz in (1, -1):
            z = WHERE[0, dy, dz][2]["Z"]
            send[z : z + 8, :] = first
            send[z + 8 : z + 16, :] = second
    z = WHERE[0, 0, 1][2]["Z"]
    for t in range(8):
        tiles = []
        for s in range(16 * t, min(16 * t + 16, 126)):
            tiles.append(col[s // 3, 8 * (s % 3) : 8 * (s % 3) + 8, :] if s < 108 else us[s - 108])
        send[z + 8 * t : z + 8 * t + 8, :] = pack(tiles, lane)

    pl.semaphore_wait(barrier, count)

    def fields(d):
        dx, dy, dz = d
        begin, rows, spot = WHERE[d]
        first_row = spot["Z"] if dz else spot["U"]
        rows = begin + rows - first_row
        src, dst = send.at[pl.ds(first_row, rows)], recv.at[pl.ds(first_row, rows)]
        if dy == 0 and dz == 0:
            dst = recvx.at[pl.ds(XROWS[dx], rows)]
        elif dx and dz:
            src = passed.at[pl.ds(0 if dx == 1 else 8, rows)]
        elif dx == 0 and dy == 0:
            src = send.at[pl.ds(z, rows)]
        step = (0, dy, dz) if dx and (dy or dz) else d
        t = TRAVELS.index(d)
        return pltpu.make_async_remote_copy(
            src_ref=src,
            dst_ref=dst,
            send_sem=send_sem.at[t],
            recv_sem=recv_sem.at[t],
            device_id=at(step),
            device_id_type=MESH,
        )

    def force(d):
        f = WHERE[d][2]["F"]
        rows = (16 if d[2] == 0 else 8) * (2 if d[0] == 0 else 1)
        t = TRAVELS.index(d)
        return pltpu.make_async_remote_copy(
            src_ref=send.at[pl.ds(f, rows)],
            dst_ref=recv.at[pl.ds(f, rows)],
            send_sem=fsend_sem.at[t],
            recv_sem=frecv_sem.at[t],
            device_id=at(d),
            device_id_type=MESH,
        )

    def sends(d):
        if d[0] and (d[1] or d[2]):
            return present(sizes, me, (-d[0], d[1], d[2]))
        return present(sizes, me, d)

    direct = [d for d in TRAVELS if not (d[0] and (d[1] or d[2]))]
    relayed = [d for d in TRAVELS if d[0] and (d[1] or d[2])]
    for d in direct:

        @pl.when(sends(d))
        def _():
            fields(d).start()

    load_vertices(base_v, off_v, base_s, off_s)
    alive = (occ[...] > 0).astype(F32)
    loads = membrane(base_s, off_s, alive, tri_v, incidence, mono)
    f_outer, f_mid, z16 = spread_own(base_s, off_s, loads, outer, mid)

    def own_put(k, tile):
        ownf[k : k + tile.shape[0], :] = tile

    force_pieces(f_outer, f_mid, z16, lane, 0, 0, 0, own_put)
    for d in TRAVELS:

        def put(k, tile, f=WHERE[d][2]["F"]):
            send[f + k : f + k + tile.shape[0], :] = tile

        force_pieces(f_outer, f_mid, z16, lane, *d, put)
    for d in TRAVELS:

        @pl.when(present(sizes, me, d))
        def _():
            force(d).start()

    for dx in (-1, 1):
        got = present(sizes, me, (-dx, 0, 0))

        @pl.when(got)
        def _():
            fields((dx, 0, 0)).wait_recv()

        tiles = face_tiles(recvx, XROWS[dx], sub)
        rows, r_rho, r_flag = FACE[dx, 0]
        ring = XROWS[dx] + 72
        row_of = {q: r for r, q in rows.items()}
        up, down = row_of[NUMBER[dx, 0, 1]], row_of[NUMBER[dx, 0, -1]]
        edge_s[...] = jnp.zeros((24, 128), F32)
        for y in range(6):
            t = recvx[ring + 8 * y : ring + 8 * y + 8, :]
            edge_s[y : y + 1, :] = jnp.where(lane[0:1] >= 64, t[up : up + 1], t[down : down + 1])
            edge_s[8 + y : 9 + y, :] = t[r_rho : r_rho + 1]
            edge_s[16 + y : 17 + y, :] = t[r_flag : r_flag + 1]
        p = 0 if dx == 1 else 8
        passed[p : p + 8, :] = pack(tiles + [edge_s[8 * t : 8 * t + 8, :] for t in range(3)], lane)
        for dy in (1, -1):
            u, r = WHERE[dx, dy, 0][2]["U"], WHERE[dx, dy, 0][2]["R"]
            for t, tile in enumerate(paired(tiles, 2, dy, sub)):
                send[u + 8 * t : u + 8 * t + 8, :] = tile
            corner = ring + (40 if dy == 1 else 0)
            send[r : r + 8, :] = recvx[corner : corner + 8, :]
        for d in relayed:
            if d[0] == dx:

                @pl.when(sends(d))
                def _():
                    fields(d).start()

    for d in TRAVELS:

        @pl.when(sends(d))
        def _():
            fields(d).wait_send()

        @pl.when(present(sizes, me, d))
        def _():
            force(d).wait_send()

        @pl.when(present(sizes, me, back(d)))
        def _():
            force(d).wait_recv()

        if d[1] or d[2]:

            @pl.when(present(sizes, me, back(d)))
            def _():
                fields(d).wait_recv()

        @pl.when(jnp.logical_not(present(sizes, me, back(d))))
        def _():
            blank(d).wait()


def collide(p, c, rho, u, f):
    inv = 0.5 / rho
    v = [a + inv * b for a, b in zip(u, f)]
    vv = v[0] * v[0] + v[1] * v[1] + v[2] * v[2]
    vf = v[0] * f[0] + v[1] * f[1] + v[2] * f[2]
    factor = 1.0 - 0.5 / TAU
    a0 = (1.0 / TAU) * rho * (1.0 - 1.5 * vv) - (3.0 * factor) * vf
    a1 = (3.0 / TAU) * rho
    a2 = (4.5 / TAU) * rho
    cx, cy, cz, w = c
    pr = cx * v[0] + cy * v[1] + cz * v[2]
    cf = cx * f[0] + cy * f[1] + cz * f[2]
    poly = a0 + pr * (a1 + a2 * pr) + cf * (3.0 * factor + (9.0 * factor) * pr)
    return (1.0 - 1.0 / TAU) * p + w * poly


def forces(recv, ownf, force):
    zl = iota((1, 256), 1)
    zl = jnp.where(zl < 132, zl, jnp.where(zl >= 252, zl - 256, -5000)).astype(F32)
    k8 = iota((8, 1), 0).astype(F32)
    out = {}
    for sx in (-1, 0, 1):
        parts, zs = [], []
        for sy, sz in itertools.product((-1, 0, 1), (0, -1, 1)):
            kn = 8 if sz else 16
            if (sx, sy, sz) == (0, 0, 0):
                ref, f = ownf, 0
            else:
                ref, f = recv, WHERE[-sx, -sy, -sz][2]["F"]
            tile = ref[f : f + kn, :]
            if sx == 0:
                tile = jnp.concatenate([tile, ref[f + kn : f + 2 * kn, :]], axis=1)
            parts.append(tile)
            if sz == 0:
                zs.append(tile[:, 120:121] if sx else tile[:, 192:193])
            else:
                zs.append(k8 + (-1.0 if sz == -1 else 121.0))
        g = jnp.concatenate(parts, axis=0)
        z = jnp.concatenate(zs, axis=0)
        place = jnp.where(z == zl, 1.0, 0.0).astype(BF16)
        hi, lo = halves(g.T)
        out[sx] = dot(hi, place, 1, 0) + dot(lo, place, 1, 0)
    for a, x in itertools.product(range(3), range(8)):
        tile = out[0][64 * a + 8 * x : 64 * a + 8 * x + 8]
        if x < 5:
            tile = tile + out[-1][40 * a + 8 * x : 40 * a + 8 * x + 8]
        if x >= 3:
            tile = tile + out[1][40 * a + 8 * x - 24 : 40 * a + 8 * x - 16]
        force[a, x] = tile


def assemble(recv, recvx, vel, ext, lane, sub):
    low4 = (lane & 7) < 4
    above_rows = bits(sub, (0, 1))
    for sx in (-1, 0, 1):
        xs = range(6) if sx == 0 else range(4)
        x0 = {-1: 0, 0: 4, 1: 10}[sx]
        above, below = WHERE[-sx, -1, 0][2]["U"], WHERE[-sx, 1, 0][2]["U"]
        half = len(xs) // 2
        side = face_tiles(recvx, XROWS[-sx], sub) if sx else None
        for a, x in itertools.product(range(3), xs):
            own = side[4 * a + x] if sx else vel[a, x]
            t = 8 * (a * half + x // 2)
            up = recv[above + t : above + t + 8, :]
            dn = recv[below + t : below + t + 8, :]
            if x % 2:
                up, dn = roll(up, 4, 0), roll(dn, 4, 0)
            ext[a, x0 + x, 0:8, 0:128] = jnp.where(sub < 6, own, up)
            ext[a, x0 + x, 8:16, 0:128] = jnp.where(above_rows, up, jnp.where(sub >= 4, dn, 0.0))

        def merged(sy, t):
            lower = WHERE[-sx, -sy, 1][2]["Z"] + 8 * t
            upper = WHERE[-sx, -sy, -1][2]["Z"] + 8 * t
            return jnp.where(low4, recv[lower : lower + 8, :], recv[upper : upper + 8, :])

        count = 3 * len(xs)
        for t in range((count + 15) // 16):
            if sx == 0:
                slots = range(16 * t, min(16 * t + 16, count))
                m_up, m_dn = merged(1, t), merged(-1, t)
            else:
                slots = range(count)
                m_up, m_dn = merged(1, 0), merged(-1, 0)
            m_up, m_dn = roll(m_up, 6, 0), roll(m_dn, 2, 0)
            second = jnp.where(above_rows, m_up, jnp.where(sub >= 4, m_dn, 0.0))
            for s in slots:
                a, x = s // len(xs), s % len(xs)
                own_slot = s + 108 if sx == 0 else s
                own = unpack(merged(0, own_slot // 16), own_slot)
                ext[a, x0 + x, 0:8, 128:256] = jnp.where(sub < 6, own, unpack(m_up, s))
                ext[a, x0 + x, 8:16, 128:256] = unpack(second, s)


def interpolate(ext, base_s, off_s, occ, wz_s, out):
    base, frac = base_s[...], off_s[...]
    four = [four_weights(frac, a) for a in range(3)]
    wx = node_weights(iota((16, 1), 0) - 4, base[0:1], four[0])
    n = iota((16, 1), 0)
    wy = node_weights(jnp.where(n < 10, n, n - 16), base[1:2], four[1])
    wz_s[...] = jnp.zeros(wz_s.shape, F32)
    wz_s[0:136, :] = node_weights(iota((136, 1), 0), base[2:3], four[2])
    wz_s[248:256, :] = node_weights(iota((8, 1), 0) - 8, base[2:3], four[2])
    w_hi, w_lo = halves(wz_s[...])
    alive = (occ[...] > 0).astype(F32)
    for a in range(3):
        e_hi, e_lo = halves(ext[a].reshape(14 * 16, 256))
        p = dot(e_hi, w_hi, 1, 0) + dot(e_lo, w_hi, 1, 0) + dot(e_hi, w_lo, 1, 0)
        total = jnp.zeros((16, VP), F32)
        for x in range(14):
            total = total + p[16 * x : 16 * x + 16] * wx[x : x + 1]
        row = jnp.sum(total * wy, axis=0, keepdims=True) * alive
        out[a] = row[:, 0:NV]


def kernel_b(col, vel, ownf, base_s, off_s, recvx, recv, occ, nxt, vtx, ext, force, raw, moved, wz_s):
    lane = iota((8, 128), 1)
    sub = iota((8, 128), 0)
    forces(recv, ownf, force)
    assemble(recv, recvx, vel, ext, lane, sub)
    interpolate(ext, base_s, off_s, occ, wz_s, vtx)

    wall = jnp.full((8, 128), jnp.nan, F32)
    low4 = (lane & 7) < 4
    side = jnp.where(lane[0:1] >= 64, 1.0, -1.0)

    def shifts(cz):
        edge = ((cz > 0.5) & (lane == 127)) | ((cz < -0.5) & (lane == 0))

        def move(s, z):
            a = jnp.where(edge, z, s)
            return jnp.where(cz > 0.5, roll(a, 1, 1), jnp.where(cz < -0.5, roll(a, 127, 1), a))

        return move

    cs = [constants(sub, natural_numbers(k)) for k in range(3)]
    movers = [shifts(c[2]) for c in cs]
    z_low = WHERE[0, 0, 1][2]["Z"]
    z_high = WHERE[0, 0, -1][2]["Z"]
    merged = []
    for t in range(7):
        merged.append(jnp.where(low4, recv[z_low + 8 * t : z_low + 8 * t + 8, :], recv[z_high + 8 * t : z_high + 8 * t + 8, :]))
    for x, y in itertools.product(range(BX), range(BY)):
        i = x * BY + y
        rho, flag = col[i, RHO : RHO + 1, :], col[i, FLAG : FLAG + 1, :]
        u = [col[i, VEL + a : VEL + a + 1, :] for a in range(3)]
        f = [force[a, x + 1, y : y + 1, 0:128] for a in range(3)]
        fz = [force[a, x + 1, y : y + 1, 128:256] for a in range(3)]
        zt = [unpack(merged[(3 * i + k) // 16], 3 * i + k) for k in range(3)]
        uz = [zt[2][VEL - 16 + a : VEL - 15 + a] for a in range(3)]
        rho_z, flag_z = zt[2][RHO - 16 : RHO - 15], zt[2][FLAG - 16 : FLAG - 15]
        for k in range(3):
            r = collide(col[i, 8 * k : 8 * k + 8, :], cs[k], rho, u, f)
            raw[i, 8 * k : 8 * k + 8, :] = r
            rz = collide(zt[k], cs[k], rho_z, uz, fz)
            s = jnp.where(flag > 0.5, r, wall)
            sz = jnp.where(flag_z > 0.5, rz, wall)
            moved[x + 1, y + 1, 8 * k : 8 * k + 8, :] = movers[k](s, sz)

    for face, (rows, r_rho, r_flag) in FACE.items():
        dx, dy = face
        numbers = [rows.get(r) for r in range(8)]
        c = constants(sub, numbers)
        mover = shifts(c[2])
        ring = WHERE[dx, dy, 0][2]["R"] if dy else XROWS[dx] + 72
        ring_ref = recv if dy else recvx
        count = 1 if dx and dy else 6
        if count == 6:
            if dx:
                z = [WHERE[dx, 0, s][2]["Z"] for s in (1, -1)]
                slot = 12
            else:
                z = [WHERE[0, dy, s][2]["Z"] + 8 for s in (1, -1)]
                slot = 2
            pz = jnp.where(low4, recv[z[0] : z[0] + 8, :], recv[z[1] : z[1] + 8, :])
            tz = [unpack(pz, slot + t) for t in range(3)]
            cz = (float(dx), float(dy), side, 1.0 / 36.0)
        for j in range(count):
            x = {1: -1, -1: 6, 0: j}[dx]
            y = {1: -1, -1: 6, 0: j}[dy]
            t = ring_ref[ring + 8 * j : ring + 8 * j + 8, :]
            rho, flag = t[r_rho : r_rho + 1], t[r_flag : r_flag + 1]
            yu, yf = y % 16, y % 8
            u = [ext[a, x + 4, yu : yu + 1, 0:128] for a in range(3)]
            f = [force[a, x + 1, yf : yf + 1, 0:128] for a in range(3)]
            s = jnp.where(flag > 0.5, collide(t, c, rho, u, f), wall)
            if count == 6:
                uz = [ext[a, x + 4, yu : yu + 1, 128:256] for a in range(3)]
                fz = [force[a, x + 1, yf : yf + 1, 128:256] for a in range(3)]
                rz = collide(tz[0][j : j + 1], cz, tz[1][j : j + 1], uz, fz)
                sz = jnp.where(tz[2][j : j + 1] > 0.5, rz, wall[0:1])
                s = mover(s, sz)
            for k in sorted({q // 8 for q in rows.values()}):
                out = None
                for shift in sorted({(q - r) % 8 for r, q in rows.items() if q // 8 == k}):
                    tile = roll(s, shift, 0)
                    members = [q % 8 for r, q in rows.items() if q // 8 == k and (q - r) % 8 == shift]
                    out = tile if out is None else jnp.where(bits(sub, members), tile, out)
                moved[x + 1, y + 1, 8 * k : 8 * k + 8, :] = out

    odd = (iota((24, 128), 0) & 1) == 1
    start = iota((24, 128), 0) == 0
    for x, y in itertools.product(range(BX), range(BY)):
        i = x * BY + y
        r = raw[i]
        turned = jnp.where(start, r, jnp.where(odd, roll(r, 23, 0), roll(r, 1, 0)))
        for k in range(3):
            sources = {}
            for q in natural_numbers(k):
                if q is not None:
                    sources.setdefault(LATTICE[q][:2], []).append(q % 8)
            out = None
            for (cx, cy), members in sources.items():
                tile = moved[x + 1 - cx, y + 1 - cy, 8 * k : 8 * k + 8, :]
                out = tile if out is None else jnp.where(bits(sub, members), tile, out)
            out = jnp.where(out == out, out, turned[8 * k : 8 * k + 8])
            last = min(8 * k + 8, 19)
            nxt[i, 8 * k : last, :] = out[0 : last - 8 * k]


def on_device(sizes, populations, fluid_mask, stencil_base, offsets, occupied_cell_slots, triangles):
    pops = jnp.transpose(populations, (1, 2, 0, 3)).reshape(BX * BY, 19, BZ)
    base = stencil_base.reshape(3, 1, NV)
    off = offsets.reshape(3, 1, NV)
    occ = occupied_cell_slots.reshape(1, 1)
    vmem = pl.BlockSpec(memory_space=pltpu.VMEM)
    hbm = pl.BlockSpec(memory_space=pltpu.HBM)
    shape = jax.ShapeDtypeStruct
    dma = pltpu.SemaphoreType.DMA
    col, vel, ownf, base_p, off_p, recvx, recv = pl.pallas_call(
        functools.partial(kernel_a, sizes),
        name="load_and_send",
        out_shape=(
            shape((36, 24, 128), F32),
            shape((3, 6, 8, 128), F32),
            shape((32, 128), F32),
            shape((8, VP), I32),
            shape((8, VP), F32),
            shape((240, 128), F32),
            shape((ROWS, 128), F32),
        ),
        in_specs=[hbm, hbm, hbm, hbm, vmem, hbm],
        out_specs=(vmem,) * 6 + (hbm,),
        scratch_shapes=[
            pltpu.VMEM((ROWS, 128), F32),
            pltpu.VMEM((16, 128), F32),
            pltpu.VMEM((6, 6, 128), I32),
            pltpu.VMEM((3, 1, NV), I32),
            pltpu.VMEM((3, 1, NV), F32),
            pltpu.VMEM((3, NT), I32),
            pltpu.VMEM((VP, NT), BF16),
            pltpu.VMEM((16, VP), F32),
            pltpu.VMEM((384, VP), F32),
            pltpu.VMEM((192, VP), F32),
            pltpu.VMEM((24, 128), F32),
            pltpu.VMEM((152, 128), F32),
            dma((5,)),
            dma((26,)),
            dma((26,)),
            dma((26,)),
            dma((26,)),
            dma((26,)),
        ],
        compiler_params=pltpu.CompilerParams(collective_id=0, has_side_effects=True, vmem_limit_bytes=48 << 20),
    )(*(pltpu.with_memory_space_constraint(a, pltpu.HBM) for a in (pops, fluid_mask, base, off)), occ, pltpu.with_memory_space_constraint(triangles.T, pltpu.HBM))
    nxt, vtx = pl.pallas_call(
        kernel_b,
        name="collide_and_pass",
        out_shape=(shape((36, 19, 128), F32), shape((3, 1, NV), F32)),
        in_specs=[vmem] * 8,
        out_specs=(vmem, vmem),
        scratch_shapes=[
            pltpu.VMEM((3, 14, 16, 256), F32),
            pltpu.VMEM((3, 8, 8, 256), F32),
            pltpu.VMEM((36, 24, 128), F32),
            pltpu.VMEM((8, 8, 24, 128), F32),
            pltpu.VMEM((256, VP), F32),
        ],
        compiler_params=pltpu.CompilerParams(vmem_limit_bytes=48 << 20),
    )(col, vel, ownf, base_p, off_p, recvx, recv, occ)
    nxt = jnp.transpose(nxt.reshape(BX, BY, 19, BZ), (2, 0, 1, 3))
    return nxt, vtx.reshape(1, 1, 1, 3, NV)


def solution(mesh):
    sizes = tuple(mesh.shape[a] for a in AXES)
    placed = (
        P(None, "gx", "gy", "gz"),
        P("gx", "gy", "gz"),
        P("gx", "gy", "gz", None, None),
        P("gx", "gy", "gz", None, None),
        P("gx", "gy", "gz"),
        P(),
    )
    return jax.shard_map(
        functools.partial(on_device, sizes),
        mesh=mesh,
        in_specs=placed,
        out_specs=(P(None, "gx", "gy", "gz"), P("gx", "gy", "gz", None, None)),
        check_vma=False,
    )
```

```python
import functools
import itertools
import math

import jax
import jax.numpy as jnp
from jax import lax
from jax.experimental import pallas as pl
from jax.experimental.pallas import tpu as pltpu
from jax.sharding import PartitionSpec as P

MESH = pl.DeviceIdType.MESH
AXES = ("gx", "gy", "gz")
NV = 642
VP = 768
NT = 1280
BX, BY, BZ = 6, 6, 128
F32, BF16, I32 = jnp.float32, jnp.bfloat16, jnp.int32
FAR = -10000
STIFFNESS, REST, TAU = 0.1, 4.0, 0.8

LATTICE = (
    (0, 0, 0),
    (1, 0, 0),
    (-1, 0, 0),
    (0, 1, 0),
    (0, -1, 0),
    (0, 0, 1),
    (0, 0, -1),
    (1, 1, 0),
    (-1, -1, 0),
    (1, -1, 0),
    (-1, 1, 0),
    (1, 0, 1),
    (-1, 0, -1),
    (1, 0, -1),
    (-1, 0, 1),
    (0, 1, 1),
    (0, -1, -1),
    (0, 1, -1),
    (0, -1, 1),
)
WEIGHT = [1.0 / 3.0] + [1.0 / 18.0] * 6 + [1.0 / 36.0] * 12
NUMBER = {c: q for q, c in enumerate(LATTICE)}

RHO, FLAG, VEL = 19, 20, 21

FACE = {
    (1, 0): ({1: 1, 7: 7, 3: 11, 5: 13, 2: 9}, 0, 4),
    (-1, 0): ({2: 2, 0: 8, 4: 12, 6: 14, 3: 10}, 1, 5),
    (0, 1): ({3: 3, 7: 7, 2: 10, 1: 17, 0: 15}, 4, 5),
    (0, -1): ({4: 4, 0: 8, 1: 9, 2: 18, 3: 16}, 5, 6),
    (1, 1): ({7: 7}, 0, 1),
    (1, -1): ({1: 9}, 0, 2),
    (-1, 1): ({2: 10}, 0, 1),
    (-1, -1): ({0: 8}, 1, 2),
}
UP = {5: 5, 3: 11, 6: 14, 7: 15, 2: 18}
DOWN = {6: 6, 4: 12, 5: 13, 0: 16, 1: 17}
EDGE_VEL = 3
TRAVELS = [d for d in itertools.product((-1, 0, 1), repeat=3) if d != (0, 0, 0)]
TRAVELS.sort(key=lambda d: (d[0] == 0, d[2] != 0, d[1] != 0))


def layout():
    where, row = {}, 0
    for d in TRAVELS:
        dx, dy, dz = d
        rows = {}
        rows["F"] = (16 if dz == 0 else 8) * (2 if dx == 0 else 1)
        if dz == 0:
            rows["R"] = 8 if dx and dy else 48
            rows["U"] = 48 if dx and dy else 72
        elif dx:
            rows["Z"] = 8
        else:
            rows["Z"] = 16 if dy else 40
        spot, begin = {}, row
        for part, count in rows.items():
            spot[part] = row
            row += count
        where[d] = (begin, row - begin, spot)
    return where, row


WHERE, ROWS = layout()


def iota(shape, axis):
    return lax.broadcasted_iota(I32, shape, axis)


def bits(index, members):
    code = sum(1 << m for m in members)
    return (lax.shift_right_logical(jnp.full(index.shape, code, I32), index) & 1) == 1


def per_row(sub, values):
    out = jnp.zeros(sub.shape, F32)
    for value in sorted(set(values)):
        if value != 0:
            members = [r for r, v in enumerate(values) if v == value]
            out = jnp.where(bits(sub, members), F32(value), out)
    return out


def constants(sub, numbers):
    rows = [[0 if q is None else LATTICE[q][a] for q in numbers] for a in range(3)]
    rows.append([0 if q is None else WEIGHT[q] for q in numbers])
    return [per_row(sub, r) for r in rows]


def natural_numbers(k):
    return [q if q < 19 else None for q in range(8 * k, 8 * k + 8)]


def sin_half_pi(f):
    t = f * (0.5 * math.pi)
    t2 = t * t
    out = jnp.full(f.shape, 1.0 / math.factorial(13), F32)
    for k in (11, 9, 7, 5, 3, 1):
        sign = 1.0 if (13 - k) // 2 % 2 == 0 else -1.0
        out = out * t2 + sign / math.factorial(k)
    return out * t


def node_weights(n, base, four):
    d = n - base
    out = jnp.where(d == 3, four[3], 0.0)
    for k in (2, 1, 0):
        out = jnp.where(d == k, four[k], out)
    return out


def four_weights(frac, axis):
    s = sin_half_pi(frac)[axis : axis + 1]
    c = sin_half_pi(1.0 - frac)[axis : axis + 1]
    return [0.25 * (1.0 - s), 0.25 * (1.0 + c), 0.25 * (1.0 + s), 0.25 * (1.0 - c)]


def halves(x):
    hi = x.astype(BF16)
    return hi, (x - hi.astype(F32)).astype(BF16)


def thirds(x):
    hi = x.astype(BF16)
    rest = x - hi.astype(F32)
    mid = rest.astype(BF16)
    return jnp.concatenate([hi, mid, (rest - mid.astype(F32)).astype(BF16)], axis=0)


def dot(a, b, ca, cb):
    return lax.dot_general(a, b, (((ca,), (cb,)), ((), ())), preferred_element_type=F32)


def load_vertices(base, off, base_s, off_s):
    base_s[...] = jnp.full((8, VP), FAR, I32)
    off_s[...] = jnp.zeros((8, VP), F32)
    for a in range(3):
        base_s[a : a + 1, 0:NV] = base[a]
        off_s[a : a + 1, 0:NV] = off[a]


def turn(t, sub):
    one = jnp.where(sub == 2, roll(t, 2, 0), roll(t, 7, 0))
    two = jnp.where(sub == 0, roll(t, 6, 0), roll(t, 1, 0))
    return one, two


def incidence_of(tri, incidence):
    def fill(step, carry):
        rows = pl.multiple_of(step * 16, 16)
        vertex = iota((16, NT), 0) + rows
        hit = (vertex == tri[0:1]) | (vertex == tri[1:2]) | (vertex == tri[2:3])
        incidence[pl.ds(rows, 16), :] = jnp.where(hit, 1.0, 0.0).astype(BF16)
        return carry

    lax.fori_loop(0, 41, fill, 0)
    incidence[656:VP, :] = jnp.zeros((VP - 656, NT), BF16)


def membrane(base_s, off_s, alive, incidence):
    sub = iota((8, VP), 0)
    base = base_s[...]
    x = jnp.where((base > FAR // 2) & (sub < 3), (base - base[:, 0:1]).astype(F32) + off_s[...], 0.0)
    x1, x2 = turn(x, sub)
    xx = x * x
    r2 = xx + x1 * x1 + x2 * x2
    first = (r2 - REST * REST) * x + jnp.where(sub == 3, 1.0, 0.0) + roll(x, 4, 0)
    second = xx + roll(x * x1, 4, 0)
    sums = dot(thirds(jnp.concatenate([first, second], axis=0)), incidence[...], 1, 0)
    sums = sums[0:16] + sums[16:32] + sums[32:48]
    back = dot(thirds(sums), incidence[...], 1, 1)
    back = back[0:16] + back[16:32] + back[32:48]
    cubic, diag = back[0:8], back[8:16]
    count = cubic[3:4]
    lin, cross = roll(cubic, 4, 0), roll(diag, 4, 0)
    turned = diag * x + cross * x1 + turn(cross, sub)[1] * x2
    along, trace = x * lin, jnp.where(sub < 3, diag, 0.0)
    along = along + sum(turn(along, sub))
    trace = trace + sum(turn(trace, sub))
    common = 2.0 * along - r2 * count - (trace - REST * REST * count)
    total = cubic - 2.0 * turned + r2 * lin + x * common
    return (STIFFNESS / (REST * REST)) * alive * total


YN = {0: (0, 1, 2, 3, 4, 5, 6, -1), 1: (6, 7, 8, 9, 10, 11, 12, 5), -1: (-6, -5, -4, -3, -2, -1, 0, -7)}
DYS = (0, 1, -1)


def spread_own(base_s, off_s, loads, outer, mid):
    base, frac = base_s[...], off_s[...]
    four = [four_weights(frac, a) for a in range(3)]
    low = base[2:3, 0:1] - 6
    k = iota((32, 1), 0)
    z = jnp.where(k < 16, low + k, jnp.where(k < 24, 127 - 16 + k, -7 - 24 + k))
    wz = node_weights(z, base[2:3], four[2])
    left = jnp.concatenate([wz * loads[c : c + 1] for c in range(3)], axis=0)
    wx = node_weights(iota((16, 1), 0) - 4, base[0:1], four[0])
    row8 = iota((8, 1), 0)
    for i, dy in enumerate(DYS):
        n = jnp.where(row8 == 7, YN[dy][7], row8 + YN[dy][0])
        wy = node_weights(n, base[1:2], four[1])
        for j in range(5):
            outer[i * 128 + j * 8 : i * 128 + j * 8 + 8, :] = wx[9 + j : 10 + j] * wy
            outer[i * 128 + 40 + j * 8 : i * 128 + 48 + j * 8, :] = wx[j : j + 1] * wy
        outer[i * 128 + 80 : i * 128 + 128, :] = jnp.zeros((48, VP), F32)
        for j in range(8):
            mid[i * 64 + j * 8 : i * 64 + j * 8 + 8, :] = wx[3 + j : 4 + j] * wy
    l_hi, l_lo = halves(left)
    both = jnp.concatenate([l_hi, l_lo], axis=0)

    def product(ref):
        r_hi, r_lo = halves(ref[...])
        out = dot(both, r_hi, 1, 1)
        return out[0:96] + out[96:192] + dot(l_hi, r_lo, 1, 1)

    return product(outer), product(mid), z[0:16].astype(F32)


def roll(x, shift, axis):
    shift = shift % x.shape[axis]
    return x if shift == 0 else pltpu.roll(x, shift, axis)


def force_pieces(outer, mid, z16, lane, dx, dy, dz, put):
    k0, kn = {0: (0, 16), 1: (16, 8), -1: (24, 8)}[dz]
    i = DYS.index(dy)
    lane = iota((kn, 128), 1)
    if dx:
        off = 0 if dx == 1 else 40
        out = jnp.zeros((kn, 128), F32)
        for c in range(3):
            tile = outer[32 * c + k0 : 32 * c + k0 + kn, i * 128 : i * 128 + 128]
            tile = roll(tile, 40 * c - off, 1)
            out = jnp.where((lane >= 40 * c) & (lane < 40 * c + 40), tile, out)
        if dz == 0:
            out = jnp.where(lane >= 120, z16, out)
        put(0, out)
        return
    tiles = []
    for c in range(3):
        t = i // 2 * 128
        tile = mid[32 * c + k0 : 32 * c + k0 + kn, t : t + (128 if i < 2 else 64)]
        if i == 2:
            tile = jnp.concatenate([tile, jnp.zeros((kn, 64), F32)], axis=1)
        tiles.append(roll(tile, 64 * (c % 2) - 64 * (i % 2), 1))
    put(0, jnp.where(lane < 64, tiles[0], tiles[1]))
    rest = z16 if dz == 0 else jnp.zeros((kn, 128), F32)
    put(kn, jnp.where(lane < 64, tiles[2], rest))


def pack(tiles, lane):
    out = jnp.zeros((8, 128), F32)
    for s, tile in enumerate(tiles):
        out = jnp.where((lane >= 8 * s) & (lane < 8 * s + 8), roll(tile, 4 + 8 * s, 1), out)
    return out


def unpack(packed, s):
    return roll(packed, -(4 + 8 * (s % 16)), 1)


def coords():
    return [lax.axis_index(a) for a in AXES]


def present_at(sizes, me, d):
    ok = None
    for m, s, size in zip(me, d, sizes):
        if s:
            here = m < size - 1 if s == 1 else m > 0
            ok = here if ok is None else jnp.logical_and(ok, here)
    return ok


def face_tiles(ref, begin, sub):
    tiles = []
    for a in range(3):
        t = [ref[begin + 8 * (3 * a + j) : begin + 8 * (3 * a + j) + 8, :] for j in range(3)]
        last = jnp.where(sub < 2, roll(t[0], 2, 0), jnp.where(sub < 4, roll(t[1], 4, 0), roll(t[2], 6, 0)))
        tiles += t + [last]
    return tiles


def paired(tiles, half, dy, sub):
    out = []
    for t in range(3 * half):
        one, two = tiles[2 * t], tiles[2 * t + 1]
        if dy == 1:
            out.append(jnp.where(sub >= 4, roll(one, 2, 0), roll(two, 6, 0)))
        else:
            out.append(jnp.where(bits(sub, (0, 1, 6, 7)), roll(one, 6, 0), roll(two, 2, 0)))
    return out


def back(d):
    return tuple(-s for s in d)


def send_all(sizes, pops, mask, base, off, occ, tri, col, vel, ownf, recv, wxy, w_hi, w_lo, send, mask_s, base_v, off_v, tri_v, base_s, off_s, incidence, outer, mid, edge_s, rho_s, in_sem, send_sem, recv_sem, fsend_sem, frecv_sem):
    me = coords()
    there = {d: present_at(sizes, me, d) for d in TRAVELS}

    def present(sizes, me, d):
        return there[d]

    ins = [(pops, col.at[:, pl.ds(0, 19), :]), (mask, mask_s.at[:, pl.ds(0, 6), :]), (base, base_v), (off, off_v), (tri, tri_v)]
    ins = [pltpu.make_async_copy(a, b, in_sem.at[k]) for k, (a, b) in enumerate(ins)]
    for copy in ins:
        copy.start()
    def at(d):
        return tuple(m + s for m, s in zip(me, d))

    barrier = pltpu.get_barrier_semaphore()
    count = jnp.int32(0)
    for d in TRAVELS:
        ok = present(sizes, me, d)
        count = count + ok.astype(I32)

        @pl.when(ok)
        def _():
            pl.semaphore_signal(barrier, inc=1, device_id=at(d), device_id_type=MESH)

    lane = iota((8, 128), 1)
    sub = iota((8, 128), 0)
    for d in TRAVELS:

        @pl.when(jnp.logical_not(present(sizes, me, back(d))))
        def _():
            begin, rows, _ = WHERE[d]
            recv[begin : begin + rows, :] = jnp.zeros((rows, 128), F32)

    cs = [constants(sub, natural_numbers(k)) for k in range(3)]
    vel[...] = jnp.zeros(vel.shape, F32)
    rho_s[...] = jnp.zeros(rho_s.shape, F32)
    for copy in ins:
        copy.wait()

    def columns(x, carry):
        for y in range(BY):
            i = x * BY + y
            col[i, 19:24, :] = jnp.zeros((5, 128), F32)
            v = [col[i, 8 * k : 8 * k + 8, :] for k in range(3)]
            rho = jnp.sum(v[0] + v[1] + v[2], axis=0, keepdims=True)
            col[i, RHO : RHO + 1, :] = rho
            rho_s[x, y : y + 1, :] = rho
            col[i, FLAG : FLAG + 1, :] = mask_s[x, y : y + 1, :].astype(F32)
            for a in range(3):
                m = v[0] * cs[0][a] + v[1] * cs[1][a] + v[2] * cs[2][a]
                u = jnp.sum(m, axis=0, keepdims=True) / rho
                col[i, VEL + a : VEL + a + 1, :] = u
                vel[a, x, y : y + 1, :] = u
        return carry

    lax.fori_loop(0, BX, columns, 0)

    def ring_tile(i, face):
        rows, r_rho, r_flag = FACE[face]
        out = jnp.where(sub == r_rho, col[i, RHO : RHO + 1, :], col[i, FLAG : FLAG + 1, :])
        moves = {}
        for r, q in rows.items():
            moves.setdefault((q // 8, (r - q) % 8), []).append(r)
        for (k, shift), members in moves.items():
            out = jnp.where(bits(sub, members), roll(col[i, 8 * k : 8 * k + 8, :], shift, 0), out)
        return out

    def ends_of(e_rows, dx, dy, column):
        up, down = NUMBER[dx, dy, 1], NUMBER[dx, dy, -1]
        edge_s[...] = jnp.zeros((24, 128), F32)
        for j in range(6):
            i = column(j)
            edge_s[j : j + 1, :] = jnp.where(lane[0:1] >= 64, col[i, up : up + 1, :], col[i, down : down + 1, :])
            edge_s[8 + j : 9 + j, :] = col[i, RHO : RHO + 1, :]
            edge_s[16 + j : 17 + j, :] = col[i, FLAG : FLAG + 1, :]
        return [edge_s[8 * t : 8 * t + 8, :] for t in range(3)]

    us = [vel[a, x] for a in range(3) for x in range(6)]
    first = pack(us[:16], lane)
    for dx in (1, -1):
        u, r = WHERE[dx, 0, 0][2]["U"], WHERE[dx, 0, 0][2]["R"]
        xs = range(2, 6) if dx == 1 else range(4)
        x = 5 if dx == 1 else 0
        for a, j in itertools.product(range(3), range(3)):
            t = u + 8 * (3 * a + j)
            send[t : t + 8, :] = jnp.where(sub < 6, vel[a, xs[j]], roll(vel[a, xs[3]], 6 - 2 * j, 0))
        for y in range(6):
            send[r + 8 * y : r + 8 * y + 8, :] = ring_tile(x * BY + y, (dx, 0))
        tiles = [vel[a, k] for a in range(3) for k in xs] + ends_of(edge_s, dx, 0, lambda j: x * BY + j)
        packed = pack(tiles, lane)
        for dy, dz in itertools.product((0, 1, -1), (1, -1)):
            z = WHERE[dx, dy, dz][2]["Z"]
            send[z : z + 8, :] = packed
        for dy in (1, -1):
            r = WHERE[dx, dy, 0][2]["R"]
            i = x * BY + (5 if dy == 1 else 0)
            send[r : r + 8, :] = ring_tile(i, (dx, dy))
            send[r + EDGE_VEL : r + EDGE_VEL + 3, :] = col[i, VEL : VEL + 3, :]
            u = WHERE[dx, dy, 0][2]["U"]
            for t, tile in enumerate(paired(tiles, 2, dy, sub)):
                send[u + 8 * t : u + 8 * t + 8, :] = tile
    for dy in (1, -1):
        u, r = WHERE[0, dy, 0][2]["U"], WHERE[0, dy, 0][2]["R"]
        y = 5 if dy == 1 else 0
        for t, tile in enumerate(paired(us, 3, dy, sub)):
            send[u + 8 * t : u + 8 * t + 8, :] = tile
        for x in range(6):
            send[r + 8 * x : r + 8 * x + 8, :] = ring_tile(x * BY + y, (0, dy))
        second = pack(us[16:] + ends_of(edge_s, 0, dy, lambda j: j * BY + y), lane)
        for dz in (1, -1):
            z = WHERE[0, dy, dz][2]["Z"]
            send[z : z + 8, :] = first
            send[z + 8 : z + 16, :] = second
    z = WHERE[0, 0, 1][2]["Z"]
    pick = []
    for k in range(2):
        ups = [r for r, q in UP.items() if q // 8 == k]
        downs = [r for r, q in DOWN.items() if q // 8 == k]
        pick.append(((lane >= 64) & bits(sub, ups)) | ((lane < 64) & bits(sub, downs)))
    tiles = []
    for i in range(BX * BY):
        v = [col[i, 8 * k : 8 * k + 8, :] for k in range(3)]
        tiles.append(jnp.where(pick[0], v[0], jnp.where(pick[1], v[1], v[2])))
    tiles += [rho_s[x] for x in range(6)] + [mask_s[x].astype(F32) for x in range(6)] + us
    for t in range(5):
        send[z + 8 * t : z + 8 * t + 8, :] = pack(tiles[16 * t : 16 * t + 16], lane)

    load_vertices(base_v, off_v, base_s, off_s)
    alive = (occ[...] > 0).astype(F32)
    incidence_of(tri_v, incidence)
    pl.semaphore_wait(barrier, count)

    def copy(src, dst, rows, to, sems, t):
        return pltpu.make_async_remote_copy(
            src_ref=send.at[pl.ds(src, rows)],
            dst_ref=recv.at[pl.ds(dst, rows)],
            send_sem=sems[0].at[t],
            recv_sem=sems[1].at[t],
            device_id=at(to),
            device_id_type=MESH,
        )

    faces = [d for d in TRAVELS if sum(map(abs, d)) == 1]
    edges = [d for d in TRAVELS if d[0] and d[1] and d[2] == 0]

    early = faces + edges

    def fields(d):
        begin, rows, spot = WHERE[d]
        row = spot["Z"] if d[2] else spot["U"] if d in edges else spot["R"]
        src = WHERE[0, 0, 1][2]["Z"] if d[2] else row
        return copy(src, row, begin + rows - row, d, (send_sem, recv_sem), TRAVELS.index(d))

    def force_copy(d):
        begin, rows, spot = WHERE[d]
        if d in faces:
            rows = spot["Z" if d[2] else "R"] - begin
        elif d in edges:
            rows = 24
        return copy(begin, begin, rows, d, (fsend_sem, frecv_sem), TRAVELS.index(d))

    for d in early:

        @pl.when(present(sizes, me, d))
        def _():
            fields(d).start()

    loads = membrane(base_s, off_s, alive, incidence)
    f_outer, f_mid, z16 = spread_own(base_s, off_s, loads, outer, mid)

    def own_put(k, tile):
        ownf[k : k + tile.shape[0], :] = tile

    force_pieces(f_outer, f_mid, z16, lane, 0, 0, 0, own_put)
    for d in TRAVELS:

        def put(k, tile, f=WHERE[d][2]["F"]):
            send[f + k : f + k + tile.shape[0], :] = tile

        force_pieces(f_outer, f_mid, z16, lane, *d, put)
    for d in TRAVELS:

        @pl.when(present(sizes, me, d))
        def _():
            force_copy(d).start()

    prepare(base_s, off_s, wxy, w_hi, w_lo)

    for d in TRAVELS:

        @pl.when(present(sizes, me, back(d)))
        def _():
            force_copy(d).wait_recv()
            if d in early:
                fields(d).wait_recv()

    for d in TRAVELS:

        @pl.when(present(sizes, me, d))
        def _():
            force_copy(d).wait_send()
            if d in early:
                fields(d).wait_send()


def collide(p, c, rho, u, f):
    inv = 0.5 / rho
    v = [a + inv * b for a, b in zip(u, f)]
    vv = v[0] * v[0] + v[1] * v[1] + v[2] * v[2]
    vf = v[0] * f[0] + v[1] * f[1] + v[2] * f[2]
    factor = 1.0 - 0.5 / TAU
    a0 = (1.0 / TAU) * rho * (1.0 - 1.5 * vv) - (3.0 * factor) * vf
    a1 = (3.0 / TAU) * rho
    a2 = (4.5 / TAU) * rho
    cx, cy, cz, w = c
    pr = cx * v[0] + cy * v[1] + cz * v[2]
    cf = cx * f[0] + cy * f[1] + cz * f[2]
    poly = a0 + pr * (a1 + a2 * pr) + cf * (3.0 * factor + (9.0 * factor) * pr)
    return (1.0 - 1.0 / TAU) * p + w * poly


def forces(recv, ownf, force):
    zl = iota((1, 256), 1)
    zl = jnp.where(zl < 132, zl, jnp.where(zl >= 252, zl - 256, -5000)).astype(F32)
    k8 = iota((8, 1), 0).astype(F32)
    out = {}
    for sx in (-1, 0, 1):
        parts, zs = [], []
        for sy, sz in itertools.product((-1, 0, 1), (0, -1, 1)):
            kn = 8 if sz else 16
            if (sx, sy, sz) == (0, 0, 0):
                ref, f = ownf, 0
            else:
                ref, f = recv, WHERE[-sx, -sy, -sz][2]["F"]
            tile = ref[f : f + kn, :]
            if sx == 0:
                tile = jnp.concatenate([tile, ref[f + kn : f + 2 * kn, :]], axis=1)
            parts.append(tile)
            if sz == 0:
                zs.append(tile[:, 120:121] if sx else tile[:, 192:193])
            else:
                zs.append(k8 + (-1.0 if sz == -1 else 121.0))
        g = jnp.concatenate(parts, axis=0)
        z = jnp.concatenate(zs, axis=0)
        place = jnp.where(z == zl, 1.0, 0.0).astype(BF16)
        hi, lo = halves(g.T)
        out[sx] = dot(hi, place, 1, 0) + dot(lo, place, 1, 0)
    for a, x in itertools.product(range(3), range(8)):
        tile = out[0][64 * a + 8 * x : 64 * a + 8 * x + 8]
        if x < 5:
            tile = tile + out[-1][40 * a + 8 * x : 40 * a + 8 * x + 8]
        if x >= 3:
            tile = tile + out[1][40 * a + 8 * x - 24 : 40 * a + 8 * x - 16]
        force[a, x] = tile


SIDES = (-1, 0, 1)
X0 = {-1: 0, 0: 4, 1: 10}


def spans(sx):
    return range(6) if sx == 0 else range(4)


def assemble(recv, vel, ext, lane, sub):
    low4 = (lane & 7) < 4
    above_rows = bits(sub, (0, 1))
    for sx in SIDES:
        xs = spans(sx)
        side = face_tiles(recv, WHERE[-sx, 0, 0][2]["U"], sub) if sx else None
        above, below = WHERE[-sx, -1, 0][2]["U"], WHERE[-sx, 1, 0][2]["U"]
        for a, x in itertools.product(range(3), xs):
            own = side[4 * a + x] if sx else vel[a, x]
            t = 8 * (a * (len(xs) // 2) + x // 2)
            up = recv[above + t : above + t + 8, :]
            dn = recv[below + t : below + t + 8, :]
            if x % 2:
                up, dn = roll(up, 4, 0), roll(dn, 4, 0)
            ext[a, X0[sx] + x, 0:8, 0:128] = jnp.where(sub < 6, own, up)
            ext[a, X0[sx] + x, 8:16, 0:128] = jnp.where(above_rows, up, jnp.where(sub >= 4, dn, 0.0))

        def merged(sy, t):
            lower = WHERE[-sx, -sy, 1][2]["Z"] + 8 * t
            upper = WHERE[-sx, -sy, -1][2]["Z"] + 8 * t
            return jnp.where(low4, recv[lower : lower + 8, :], recv[upper : upper + 8, :])

        count = 3 * len(xs)
        for t in range((count + 15) // 16):
            slots = range(16 * t, min(16 * t + 16, count))
            m_up, m_dn = roll(merged(1, t), 6, 0), roll(merged(-1, t), 2, 0)
            m_own = merged(0, t + 3 if sx == 0 else t)
            inner = jnp.where(sub < 6, m_own, m_up)
            second = jnp.where(above_rows, m_up, jnp.where(sub >= 4, m_dn, 0.0))
            for s in slots:
                a, x = s // len(xs), s % len(xs)
                ext[a, X0[sx] + x, 0:8, 128:256] = unpack(inner, s)
                ext[a, X0[sx] + x, 8:16, 128:256] = unpack(second, s)


def prepare(base_s, off_s, wxy, w_hi, w_lo):
    base, frac = base_s[...], off_s[...]
    four = [four_weights(frac, a) for a in range(3)]
    n = iota((16, 1), 0)
    wxy[0:16, :] = node_weights(n - 4, base[0:1], four[0])
    wxy[16:32, :] = node_weights(jnp.where(n < 10, n, n - 16), base[1:2], four[1])
    w_hi[...] = jnp.zeros(w_hi.shape, BF16)
    w_lo[...] = jnp.zeros(w_lo.shape, BF16)
    for begin, rows, shift in ((0, 144, 0), (240, 16, 256)):
        hi, lo = halves(node_weights(iota((rows, 1), 0) + (begin - shift), base[2:3], four[2]))
        w_hi[begin : begin + rows, :] = hi
        w_lo[begin : begin + rows, :] = lo


def interpolate(ext, wxy, w_hi, w_lo, alive, out):
    wy = wxy[16:32, :]
    for a in range(3):
        e_hi, e_lo = halves(ext[a].reshape(14 * 16, 256))
        p = dot(e_hi, w_hi[...], 1, 0) + dot(e_lo, w_hi[...], 1, 0) + dot(e_hi, w_lo[...], 1, 0)
        total = jnp.zeros((16, VP), F32)
        for x in range(14):
            total = total + p[16 * x : 16 * x + 16] * wxy[x : x + 1, :]
        row = jnp.sum(total * wy, axis=0, keepdims=True) * alive
        out[a] = row[:, 0:NV]


def step_nodes(col, recv, ext, force, raw, moved, ends, nxt, lane, sub):
    wall = jnp.full((8, 128), jnp.nan, F32)
    low4 = (lane & 7) < 4
    side = jnp.where(lane[0:1] >= 64, 1.0, -1.0)

    def shifts(cz):
        edge = ((cz > 0.5) & (lane == 127)) | ((cz < -0.5) & (lane == 0))

        def move(s, z):
            a = jnp.where(edge, z, s)
            return jnp.where(cz > 0.5, roll(a, 1, 1), jnp.where(cz < -0.5, roll(a, 127, 1), a))

        return move

    cs = [constants(sub, natural_numbers(k)) for k in range(3)]
    movers = [shifts(c[2]) for c in cs]
    c_up, c_down = [constants(sub, [rows.get(r) for r in range(8)]) for rows in (UP, DOWN)]
    c_end = [jnp.where(lane >= 64, a, b) for a, b in zip(c_up, c_down)]
    z_low = WHERE[0, 0, 1][2]["Z"]
    z_high = WHERE[0, 0, -1][2]["Z"]
    for t in range(3):
        merged = jnp.where(low4, recv[z_low + 8 * t : z_low + 8 * t + 8, :], recv[z_high + 8 * t : z_high + 8 * t + 8, :])
        for s in range(16):
            ends[16 * t + s] = unpack(merged, s)

    def own_columns(x, carry):
        for y in range(BY):
            i = x * BY + y
            rho, flag = col[i, RHO : RHO + 1, :], col[i, FLAG : FLAG + 1, :]
            u = [col[i, VEL + a : VEL + a + 1, :] for a in range(3)]
            f = [force[a, x + 1, y : y + 1, 0:128] for a in range(3)]
            fz = [force[a, x + 1, y : y + 1, 128:256] for a in range(3)]
            uz = [ext[a, x + 4, y : y + 1, 128:256] for a in range(3)]
            rho_z, flag_z = ends[36 + x, y : y + 1, :], ends[42 + x, y : y + 1, :]
            rz = collide(ends[i], c_end, rho_z, uz, fz)
            sz = jnp.where(flag_z > 0.5, rz, wall)
            for k in range(3):
                r = collide(col[i, 8 * k : 8 * k + 8, :], cs[k], rho, u, f)
                raw[i, 8 * k : 8 * k + 8, :] = r
                s = jnp.where(flag > 0.5, r, wall)
                moved[x + 1, y + 1, 8 * k : 8 * k + 8, :] = movers[k](s, sz)
        return carry

    for x in range(BX):
        own_columns(x, 0)

    for face, (rows, r_rho, r_flag) in FACE.items():
        dx, dy = face
        numbers = [rows.get(r) for r in range(8)]
        c = constants(sub, numbers)
        mover = shifts(c[2])
        ring = WHERE[dx, dy, 0][2]["R"]
        count = 1 if dx and dy else 6
        if count == 6:
            if dx:
                z = [WHERE[dx, 0, s][2]["Z"] for s in (1, -1)]
                slot = 12
            else:
                z = [WHERE[0, dy, s][2]["Z"] + 8 for s in (1, -1)]
                slot = 2
            pz = jnp.where(low4, recv[z[0] : z[0] + 8, :], recv[z[1] : z[1] + 8, :])
            tz = [unpack(pz, slot + t) for t in range(3)]
            cz = (float(dx), float(dy), side, 1.0 / 36.0)
        for j in range(count):
            x = {1: -1, -1: 6, 0: j}[dx]
            y = {1: -1, -1: 6, 0: j}[dy]
            t = recv[ring + 8 * j : ring + 8 * j + 8, :]
            rho, flag = t[r_rho : r_rho + 1], t[r_flag : r_flag + 1]
            yu, yf = y % 16, y % 8
            if count == 6:
                u = [ext[a, x + 4, yu : yu + 1, 0:128] for a in range(3)]
            else:
                u = [t[EDGE_VEL + a : EDGE_VEL + a + 1] for a in range(3)]
            f = [force[a, x + 1, yf : yf + 1, 0:128] for a in range(3)]
            s = jnp.where(flag > 0.5, collide(t, c, rho, u, f), wall)
            if count == 6:
                uz = [ext[a, x + 4, yu : yu + 1, 128:256] for a in range(3)]
                fz = [force[a, x + 1, yf : yf + 1, 128:256] for a in range(3)]
                rz = collide(tz[0][j : j + 1], cz, tz[1][j : j + 1], uz, fz)
                sz = jnp.where(tz[2][j : j + 1] > 0.5, rz, wall[0:1])
                s = mover(s, sz)
            for k in sorted({q // 8 for q in rows.values()}):
                out = None
                for shift in sorted({(q - r) % 8 for r, q in rows.items() if q // 8 == k}):
                    tile = roll(s, shift, 0)
                    members = [q % 8 for r, q in rows.items() if q // 8 == k and (q - r) % 8 == shift]
                    out = tile if out is None else jnp.where(bits(sub, members), tile, out)
                moved[x + 1, y + 1, 8 * k : 8 * k + 8, :] = out

    odd = (iota((24, 128), 0) & 1) == 1
    start = iota((24, 128), 0) == 0

    def passing(x, carry):
        for y in range(BY):
            i = x * BY + y
            r = raw[i]
            turned = jnp.where(start, r, jnp.where(odd, roll(r, 23, 0), roll(r, 1, 0)))
            for k in range(3):
                sources = {}
                for q in natural_numbers(k):
                    if q is not None:
                        sources.setdefault(LATTICE[q][:2], []).append(q % 8)
                out = None
                for (cx, cy), members in sources.items():
                    tile = moved[x + 1 - cx, y + 1 - cy, 8 * k : 8 * k + 8, :]
                    out = tile if out is None else jnp.where(bits(sub, members), tile, out)
                out = jnp.where(out == out, out, turned[8 * k : 8 * k + 8])
                last = min(8 * k + 8, 19)
                nxt[i, 8 * k : last, :] = out[0 : last - 8 * k]
        return carry

    for x in range(BX):
        passing(x, 0)


def finish(col, vel, ownf, recv, wxy, w_hi, w_lo, occ, nxt, vtx, ext, force, raw, moved, ends):
    lane = iota((8, 128), 1)
    sub = iota((8, 128), 0)
    alive = (occ[...] > 0).astype(F32)
    assemble(recv, vel, ext, lane, sub)
    forces(recv, ownf, force)
    step_nodes(col, recv, ext, force, raw, moved, ends, nxt, lane, sub)
    interpolate(ext, wxy, w_hi, w_lo, alive, vtx)


def on_device(sizes, populations, fluid_mask, stencil_base, offsets, occupied_cell_slots, triangles):
    pops = jnp.transpose(populations, (1, 2, 0, 3)).reshape(BX * BY, 19, BZ)
    base = stencil_base.reshape(3, 1, NV)
    off = offsets.reshape(3, 1, NV)
    occ = occupied_cell_slots.reshape(1, 1)
    vmem = pl.BlockSpec(memory_space=pltpu.VMEM)
    hbm = pl.BlockSpec(memory_space=pltpu.HBM)
    shape = jax.ShapeDtypeStruct
    dma = pltpu.SemaphoreType.DMA
    vm = pltpu.VMEM
    middle = pl.pallas_call(
        functools.partial(send_all, sizes),
        name="cells_and_halo",
        out_shape=(
            shape((36, 24, 128), F32),
            shape((3, 6, 8, 128), F32),
            shape((32, 128), F32),
            shape((ROWS, 128), F32),
            shape((32, VP), F32),
            shape((256, VP), BF16),
            shape((256, VP), BF16),
        ),
        in_specs=[hbm, hbm, hbm, hbm, vmem, hbm],
        out_specs=(vmem,) * 7,
        scratch_shapes=[
            vm((ROWS, 128), F32),
            vm((6, 8, 128), I32),
            vm((3, 1, NV), I32),
            vm((3, 1, NV), F32),
            vm((3, NT), I32),
            vm((8, VP), I32),
            vm((8, VP), F32),
            vm((VP, NT), BF16),
            vm((384, VP), F32),
            vm((192, VP), F32),
            vm((24, 128), F32),
            vm((6, 8, 128), F32),
            dma((5,)),
            dma((26,)),
            dma((26,)),
            dma((26,)),
            dma((26,)),
        ],
        compiler_params=pltpu.CompilerParams(collective_id=0, has_side_effects=True, vmem_limit_bytes=48 << 20),
    )(*(pltpu.with_memory_space_constraint(a, pltpu.HBM) for a in (pops, fluid_mask, base, off)), occ, pltpu.with_memory_space_constraint(triangles.T, pltpu.HBM))
    nxt, vtx = pl.pallas_call(
        finish,
        name="collide_and_pass",
        out_shape=(shape((36, 19, 128), F32), shape((3, 1, NV), F32)),
        in_specs=[vmem] * 8,
        out_specs=(vmem, vmem),
        scratch_shapes=[
            vm((3, 14, 16, 256), F32),
            vm((3, 8, 8, 256), F32),
            vm((36, 24, 128), F32),
            vm((8, 8, 24, 128), F32),
            vm((48, 8, 128), F32),
        ],
        compiler_params=pltpu.CompilerParams(vmem_limit_bytes=48 << 20),
    )(*middle, occ)
    nxt = jnp.transpose(nxt.reshape(BX, BY, 19, BZ), (2, 0, 1, 3))
    return nxt, vtx.reshape(1, 1, 1, 3, NV)


def solution(mesh):
    sizes = tuple(mesh.shape[a] for a in AXES)
    placed = (
        P(None, "gx", "gy", "gz"),
        P("gx", "gy", "gz"),
        P("gx", "gy", "gz", None, None),
        P("gx", "gy", "gz", None, None),
        P("gx", "gy", "gz"),
        P(),
    )
    return jax.shard_map(
        functools.partial(on_device, sizes),
        mesh=mesh,
        in_specs=placed,
        out_specs=(P(None, "gx", "gy", "gz"), P("gx", "gy", "gz", None, None)),
        check_vma=False,
    )
```

```python
import functools
import itertools
import math

import jax
import jax.numpy as jnp
from jax import lax
from jax.experimental import pallas as pl
from jax.experimental.pallas import tpu as pltpu
from jax.sharding import PartitionSpec as P

MESH = pl.DeviceIdType.MESH
AXES = ("gx", "gy", "gz")
NV = 642
VP = 768
NT = 1280
BX, BY, BZ = 6, 6, 128
F32, BF16, I32 = jnp.float32, jnp.bfloat16, jnp.int32
FAR = -10000
STIFFNESS, REST, TAU = 0.1, 4.0, 0.8

LATTICE = (
    (0, 0, 0),
    (1, 0, 0),
    (-1, 0, 0),
    (0, 1, 0),
    (0, -1, 0),
    (0, 0, 1),
    (0, 0, -1),
    (1, 1, 0),
    (-1, -1, 0),
    (1, -1, 0),
    (-1, 1, 0),
    (1, 0, 1),
    (-1, 0, -1),
    (1, 0, -1),
    (-1, 0, 1),
    (0, 1, 1),
    (0, -1, -1),
    (0, 1, -1),
    (0, -1, 1),
)
WEIGHT = [1.0 / 3.0] + [1.0 / 18.0] * 6 + [1.0 / 36.0] * 12
NUMBER = {c: q for q, c in enumerate(LATTICE)}

RHO, FLAG, VEL = 19, 20, 21

FACE = {
    (1, 0): ({1: 1, 7: 7, 3: 11, 5: 13, 2: 9}, 0, 4),
    (-1, 0): ({2: 2, 0: 8, 4: 12, 6: 14, 3: 10}, 1, 5),
    (0, 1): ({3: 3, 7: 7, 2: 10, 1: 17, 0: 15}, 4, 5),
    (0, -1): ({4: 4, 0: 8, 1: 9, 2: 18, 3: 16}, 5, 6),
    (1, 1): ({7: 7}, 0, 1),
    (1, -1): ({1: 9}, 0, 2),
    (-1, 1): ({2: 10}, 0, 1),
    (-1, -1): ({0: 8}, 1, 2),
}
UP = {5: 5, 3: 11, 6: 14, 7: 15, 2: 18}
DOWN = {6: 6, 4: 12, 5: 13, 0: 16, 1: 17}
EDGE_VEL = 3
TRAVELS = [d for d in itertools.product((-1, 0, 1), repeat=3) if d != (0, 0, 0)]
TRAVELS.sort(key=lambda d: (d[0] == 0, d[2] != 0, d[1] != 0))


def layout():
    where, row = {}, 0
    for d in TRAVELS:
        dx, dy, dz = d
        rows = {}
        if dx and dy and dz == 0:
            rows["R"] = 8
        if dx and dz:
            rows["Z"] = 8
        rows["F"] = (16 if dz == 0 else 8) * (2 if dx == 0 else 1)
        if dz == 0:
            if not (dx and dy):
                rows["R"] = 48
            rows["U"] = 48 if dx and dy else 72
        elif dx == 0:
            rows["Z"] = 16 if dy else 40
        spot, begin = {}, row
        for part, count in rows.items():
            spot[part] = row
            row += count
        where[d] = (begin, row - begin, spot)
    return where, row


WHERE, ROWS = layout()
USED = {16: 11, 8: 5}


def iota(shape, axis):
    return lax.broadcasted_iota(I32, shape, axis)


def bits(index, members):
    code = sum(1 << m for m in members)
    return (lax.shift_right_logical(jnp.full(index.shape, code, I32), index) & 1) == 1


def per_row(sub, values):
    out = jnp.zeros(sub.shape, F32)
    for value in sorted(set(values)):
        if value != 0:
            members = [r for r, v in enumerate(values) if v == value]
            out = jnp.where(bits(sub, members), F32(value), out)
    return out


def constants(sub, numbers):
    rows = [[0 if q is None else LATTICE[q][a] for q in numbers] for a in range(3)]
    rows.append([0 if q is None else WEIGHT[q] for q in numbers])
    return [per_row(sub, r) for r in rows]


def natural_numbers(k):
    return [q if q < 19 else None for q in range(8 * k, 8 * k + 8)]


def sin_half_pi(f):
    t = f * (0.5 * math.pi)
    t2 = t * t
    out = jnp.full(f.shape, 1.0 / math.factorial(13), F32)
    for k in (11, 9, 7, 5, 3, 1):
        sign = 1.0 if (13 - k) // 2 % 2 == 0 else -1.0
        out = out * t2 + sign / math.factorial(k)
    return out * t


def node_weights(n, base, four):
    d = n - base
    out = jnp.where(d == 3, four[3], 0.0)
    for k in (2, 1, 0):
        out = jnp.where(d == k, four[k], out)
    return out


def four_weights(frac, axis):
    s = sin_half_pi(frac)[axis : axis + 1]
    c = sin_half_pi(1.0 - frac)[axis : axis + 1]
    return [0.25 * (1.0 - s), 0.25 * (1.0 + c), 0.25 * (1.0 + s), 0.25 * (1.0 - c)]


def halves(x):
    hi = x.astype(BF16)
    return hi, (x - hi.astype(F32)).astype(BF16)


def thirds(x):
    hi = x.astype(BF16)
    rest = x - hi.astype(F32)
    mid = rest.astype(BF16)
    return jnp.concatenate([hi, mid, (rest - mid.astype(F32)).astype(BF16)], axis=0)


def dot(a, b, ca, cb):
    return lax.dot_general(a, b, (((ca,), (cb,)), ((), ())), preferred_element_type=F32)


def load_vertices(base, off, base_s, off_s):
    base_s[...] = jnp.full((8, VP), FAR, I32)
    off_s[...] = jnp.zeros((8, VP), F32)
    for a in range(3):
        base_s[a : a + 1, 0:NV] = base[a]
        off_s[a : a + 1, 0:NV] = off[a]


def turn(t, sub):
    one = jnp.where(sub == 2, roll(t, 2, 0), roll(t, 7, 0))
    two = jnp.where(sub == 0, roll(t, 6, 0), roll(t, 1, 0))
    return one, two


def incidence_of(tri, incidence):
    def fill(step, carry):
        rows = pl.multiple_of(step * 16, 16)
        vertex = iota((16, NT), 0) + rows
        hit = (vertex == tri[0:1]) | (vertex == tri[1:2]) | (vertex == tri[2:3])
        incidence[pl.ds(rows, 16), :] = jnp.where(hit, 1.0, 0.0).astype(BF16)
        return carry

    lax.fori_loop(0, 41, fill, 0)
    incidence[656:VP, :] = jnp.zeros((VP - 656, NT), BF16)


def membrane(base_s, off_s, alive, incidence):
    sub = iota((8, VP), 0)
    base = base_s[...]
    x = jnp.where((base > FAR // 2) & (sub < 3), (base - base[:, 0:1]).astype(F32) + off_s[...], 0.0)
    x1, x2 = turn(x, sub)
    xx = x * x
    r2 = xx + x1 * x1 + x2 * x2
    first = (r2 - REST * REST) * x + jnp.where(sub == 3, 1.0, 0.0) + roll(x, 4, 0)
    second = xx + roll(x * x1, 4, 0)
    sums = dot(thirds(jnp.concatenate([first, second], axis=0)), incidence[...], 1, 0)
    sums = sums[0:16] + sums[16:32] + sums[32:48]
    back = dot(thirds(sums), incidence[...], 1, 1)
    back = back[0:16] + back[16:32] + back[32:48]
    cubic, diag = back[0:8], back[8:16]
    count = cubic[3:4]
    lin, cross = roll(cubic, 4, 0), roll(diag, 4, 0)
    turned = diag * x + cross * x1 + turn(cross, sub)[1] * x2
    along, trace = x * lin, jnp.where(sub < 3, diag, 0.0)
    along = along + sum(turn(along, sub))
    trace = trace + sum(turn(trace, sub))
    common = 2.0 * along - r2 * count - (trace - REST * REST * count)
    total = cubic - 2.0 * turned + r2 * lin + x * common
    return (STIFFNESS / (REST * REST)) * alive * total


YN = {0: (0, 1, 2, 3, 4, 5, 6, -1), 1: (6, 7, 8, 9, 10, 11, 12, 5), -1: (-6, -5, -4, -3, -2, -1, 0, -7)}
DYS = (0, 1, -1)


def spread_own(base_s, off_s, loads, outer, mid):
    base, frac = base_s[...], off_s[...]
    four = [four_weights(frac, a) for a in range(3)]
    low = jnp.min(jnp.where(base[2:3] > FAR // 2, base[2:3], 1 << 20), axis=1, keepdims=True)
    k = iota((32, 1), 0)
    z = jnp.where(k < 16, low + k, jnp.where(k < 24, 127 - 16 + k, -4 - 24 + k))
    wz = node_weights(z, base[2:3], four[2])
    left = jnp.concatenate([wz * loads[c : c + 1] for c in range(3)], axis=0)
    wx = node_weights(iota((16, 1), 0) - 4, base[0:1], four[0])
    row8 = iota((8, 1), 0)
    for i, dy in enumerate(DYS):
        n = jnp.where(row8 == 7, YN[dy][7], row8 + YN[dy][0])
        wy = node_weights(n, base[1:2], four[1])
        for j in range(5):
            outer[i * 128 + j * 8 : i * 128 + j * 8 + 8, :] = wx[9 + j : 10 + j] * wy
            outer[i * 128 + 40 + j * 8 : i * 128 + 48 + j * 8, :] = wx[j : j + 1] * wy
        outer[i * 128 + 80 : i * 128 + 128, :] = jnp.zeros((48, VP), F32)
        for j in range(8):
            mid[i * 64 + j * 8 : i * 64 + j * 8 + 8, :] = wx[3 + j : 4 + j] * wy
    l_hi, l_lo = halves(left)
    both = jnp.concatenate([l_hi, l_lo], axis=0)

    def product(ref):
        r_hi, r_lo = halves(ref[...])
        out = dot(both, r_hi, 1, 1)
        return out[0:96] + out[96:192] + dot(l_hi, r_lo, 1, 1)

    return product(outer), product(mid), z[0:16].astype(F32)


def roll(x, shift, axis):
    shift = shift % x.shape[axis]
    return x if shift == 0 else pltpu.roll(x, shift, axis)


def force_pieces(outer, mid, z16, lane, dx, dy, dz, put):
    k0, kn = {0: (0, 16), 1: (16, 8), -1: (24, 8)}[dz]
    i = DYS.index(dy)
    lane = iota((kn, 128), 1)
    if dx:
        off = 0 if dx == 1 else 40
        out = jnp.zeros((kn, 128), F32)
        for c in range(3):
            tile = outer[32 * c + k0 : 32 * c + k0 + kn, i * 128 : i * 128 + 128]
            tile = roll(tile, 40 * c - off, 1)
            out = jnp.where((lane >= 40 * c) & (lane < 40 * c + 40), tile, out)
        if dz == 0:
            out = jnp.where(lane >= 120, z16, out)
        put(0, out)
        return
    tiles = []
    for c in range(3):
        t = i // 2 * 128
        tile = mid[32 * c + k0 : 32 * c + k0 + kn, t : t + (128 if i < 2 else 64)]
        if i == 2:
            tile = jnp.concatenate([tile, jnp.zeros((kn, 64), F32)], axis=1)
        tiles.append(roll(tile, 64 * (c % 2) - 64 * (i % 2), 1))
    put(0, jnp.where(lane < 64, tiles[0], tiles[1]))
    rest = z16 if dz == 0 else jnp.zeros((kn, 128), F32)
    put(kn, jnp.where(lane < 64, tiles[2], rest))


def pack(tiles, lane):
    out = jnp.zeros((8, 128), F32)
    for s, tile in enumerate(tiles):
        out = jnp.where((lane >= 8 * s) & (lane < 8 * s + 8), roll(tile, 4 + 8 * s, 1), out)
    return out


def unpack(packed, s):
    return roll(packed, -(4 + 8 * (s % 16)), 1)


def coords():
    return [lax.axis_index(a) for a in AXES]


def present_at(sizes, me, d):
    ok = None
    for m, s, size in zip(me, d, sizes):
        if s:
            here = m < size - 1 if s == 1 else m > 0
            ok = here if ok is None else jnp.logical_and(ok, here)
    return ok


def face_tiles(ref, begin, sub):
    tiles = []
    for a in range(3):
        t = [ref[begin + 8 * (3 * a + j) : begin + 8 * (3 * a + j) + 8, :] for j in range(3)]
        last = jnp.where(sub < 2, roll(t[0], 2, 0), jnp.where(sub < 4, roll(t[1], 4, 0), roll(t[2], 6, 0)))
        tiles += t + [last]
    return tiles


def paired(tiles, half, dy, sub):
    out = []
    for t in range(3 * half):
        one, two = tiles[2 * t], tiles[2 * t + 1]
        if dy == 1:
            out.append(jnp.where(sub >= 4, roll(one, 2, 0), roll(two, 6, 0)))
        else:
            out.append(jnp.where(bits(sub, (0, 1, 6, 7)), roll(one, 6, 0), roll(two, 2, 0)))
    return out


def back(d):
    return tuple(-s for s in d)


def send_all(sizes, pops, mask, base, off, occ, tri, col, vel, ownf, recv, wxy, w_hi, w_lo, send, mask_s, base_v, off_v, tri_v, base_s, off_s, incidence, outer, mid, edge_s, rho_s, in_sem, send_sem, recv_sem, fsend_sem, frecv_sem):
    me = coords()
    there = {d: present_at(sizes, me, d) for d in TRAVELS}

    def present(sizes, me, d):
        return there[d]

    ins = [(pops, col.at[:, pl.ds(0, 19), :]), (mask, mask_s.at[:, pl.ds(0, 6), :]), (base, base_v), (off, off_v), (tri, tri_v)]
    ins = [pltpu.make_async_copy(a, b, in_sem.at[k]) for k, (a, b) in enumerate(ins)]
    for copy in ins:
        copy.start()
    def at(d):
        return tuple(m + s for m, s in zip(me, d))

    barrier = pltpu.get_barrier_semaphore()
    count = jnp.int32(0)
    for d in TRAVELS:
        ok = present(sizes, me, d)
        count = count + ok.astype(I32)

        @pl.when(ok)
        def _():
            pl.semaphore_signal(barrier, inc=1, device_id=at(d), device_id_type=MESH)

    lane = iota((8, 128), 1)
    sub = iota((8, 128), 0)
    for d in TRAVELS:

        @pl.when(jnp.logical_not(present(sizes, me, back(d))))
        def _():
            begin, rows, _ = WHERE[d]
            recv[begin : begin + rows, :] = jnp.zeros((rows, 128), F32)

    cs = [constants(sub, natural_numbers(k)) for k in range(3)]
    vel[...] = jnp.zeros(vel.shape, F32)
    rho_s[...] = jnp.zeros(rho_s.shape, F32)
    for copy in ins:
        copy.wait()

    def columns(x, carry):
        for y in range(BY):
            i = x * BY + y
            col[i, 19:24, :] = jnp.zeros((5, 128), F32)
            v = [col[i, 8 * k : 8 * k + 8, :] for k in range(3)]
            rho = jnp.sum(v[0] + v[1] + v[2], axis=0, keepdims=True)
            col[i, RHO : RHO + 1, :] = rho
            rho_s[x, y : y + 1, :] = rho
            col[i, FLAG : FLAG + 1, :] = mask_s[x, y : y + 1, :].astype(F32)
            for a in range(3):
                m = v[0] * cs[0][a] + v[1] * cs[1][a] + v[2] * cs[2][a]
                u = jnp.sum(m, axis=0, keepdims=True) / rho
                col[i, VEL + a : VEL + a + 1, :] = u
                vel[a, x, y : y + 1, :] = u
        return carry

    lax.fori_loop(0, BX, columns, 0)

    def ring_tile(i, face):
        rows, r_rho, r_flag = FACE[face]
        out = jnp.where(sub == r_rho, col[i, RHO : RHO + 1, :], col[i, FLAG : FLAG + 1, :])
        moves = {}
        for r, q in rows.items():
            moves.setdefault((q // 8, (r - q) % 8), []).append(r)
        for (k, shift), members in moves.items():
            out = jnp.where(bits(sub, members), roll(col[i, 8 * k : 8 * k + 8, :], shift, 0), out)
        return out

    def ends_of(e_rows, dx, dy, column):
        up, down = NUMBER[dx, dy, 1], NUMBER[dx, dy, -1]
        edge_s[...] = jnp.zeros((24, 128), F32)
        for j in range(6):
            i = column(j)
            edge_s[j : j + 1, :] = jnp.where(lane[0:1] >= 64, col[i, up : up + 1, :], col[i, down : down + 1, :])
            edge_s[8 + j : 9 + j, :] = col[i, RHO : RHO + 1, :]
            edge_s[16 + j : 17 + j, :] = col[i, FLAG : FLAG + 1, :]
        return [edge_s[8 * t : 8 * t + 8, :] for t in range(3)]

    us = [vel[a, x] for a in range(3) for x in range(6)]
    first = pack(us[:16], lane)
    for dx in (1, -1):
        u, r = WHERE[dx, 0, 0][2]["U"], WHERE[dx, 0, 0][2]["R"]
        xs = range(2, 6) if dx == 1 else range(4)
        x = 5 if dx == 1 else 0
        for a, j in itertools.product(range(3), range(3)):
            t = u + 8 * (3 * a + j)
            send[t : t + 8, :] = jnp.where(sub < 6, vel[a, xs[j]], roll(vel[a, xs[3]], 6 - 2 * j, 0))
        for y in range(6):
            send[r + 8 * y : r + 8 * y + 8, :] = ring_tile(x * BY + y, (dx, 0))
        tiles = [vel[a, k] for a in range(3) for k in xs] + ends_of(edge_s, dx, 0, lambda j: x * BY + j)
        packed = pack(tiles, lane)
        for dy, dz in itertools.product((0, 1, -1), (1, -1)):
            z = WHERE[dx, dy, dz][2]["Z"]
            send[z : z + 8, :] = packed
        for dy in (1, -1):
            r = WHERE[dx, dy, 0][2]["R"]
            i = x * BY + (5 if dy == 1 else 0)
            send[r : r + 8, :] = ring_tile(i, (dx, dy))
            send[r + EDGE_VEL : r + EDGE_VEL + 3, :] = col[i, VEL : VEL + 3, :]
    for dy in (1, -1):
        u, r = WHERE[0, dy, 0][2]["U"], WHERE[0, dy, 0][2]["R"]
        y = 5 if dy == 1 else 0
        for t, tile in enumerate(paired(us, 3, dy, sub)):
            send[u + 8 * t : u + 8 * t + 8, :] = tile
        for x in range(6):
            send[r + 8 * x : r + 8 * x + 8, :] = ring_tile(x * BY + y, (0, dy))
        second = pack(us[16:] + ends_of(edge_s, 0, dy, lambda j: j * BY + y), lane)
        for dz in (1, -1):
            z = WHERE[0, dy, dz][2]["Z"]
            send[z : z + 8, :] = first
            send[z + 8 : z + 16, :] = second
    z = WHERE[0, 0, 1][2]["Z"]
    pick = []
    for k in range(2):
        ups = [r for r, q in UP.items() if q // 8 == k]
        downs = [r for r, q in DOWN.items() if q // 8 == k]
        pick.append(((lane >= 64) & bits(sub, ups)) | ((lane < 64) & bits(sub, downs)))
    tiles = []
    for i in range(BX * BY):
        v = [col[i, 8 * k : 8 * k + 8, :] for k in range(3)]
        tiles.append(jnp.where(pick[0], v[0], jnp.where(pick[1], v[1], v[2])))
    tiles += [rho_s[x] for x in range(6)] + [mask_s[x].astype(F32) for x in range(6)] + us
    for t in range(5):
        send[z + 8 * t : z + 8 * t + 8, :] = pack(tiles[16 * t : 16 * t + 16], lane)

    load_vertices(base_v, off_v, base_s, off_s)
    alive = (occ[...] > 0).astype(F32)
    incidence_of(tri_v, incidence)
    pl.semaphore_wait(barrier, count)

    def copy(src, dst, rows, to, sems, t):
        return pltpu.make_async_remote_copy(
            src_ref=send.at[pl.ds(src, rows)],
            dst_ref=recv.at[pl.ds(dst, rows)],
            send_sem=sems[0].at[t],
            recv_sem=sems[1].at[t],
            device_id=at(to),
            device_id_type=MESH,
        )

    faces = [d for d in TRAVELS if sum(map(abs, d)) == 1]
    edges = [d for d in TRAVELS if d[0] and d[1] and d[2] == 0]


    def fields(d):
        dx, dy, dz = d
        begin, rows, spot = WHERE[d]
        t = TRAVELS.index(d)
        if d in edges:
            return copy(spot["U"], spot["U"], 48, (0, dy, 0), (send_sem, recv_sem), t)
        row = spot["Z"] if dz else spot["R"]
        src = WHERE[0, 0, 1][2]["Z"] if dz else row
        return copy(src, row, begin + rows - row, d, (send_sem, recv_sem), t)

    def force_copy(d):
        begin, rows, spot = WHERE[d]
        if d[0]:
            rows = spot["F"] - begin + USED[8 if d[2] else 16]
        elif d in faces:
            rows = spot["Z" if d[2] else "R"] - begin
        return copy(begin, begin, rows, d, (fsend_sem, frecv_sem), TRAVELS.index(d))

    for d in faces:

        @pl.when(present(sizes, me, d))
        def _():
            fields(d).start()

    loads = membrane(base_s, off_s, alive, incidence)
    f_outer, f_mid, z16 = spread_own(base_s, off_s, loads, outer, mid)

    def own_put(k, tile):
        ownf[k : k + tile.shape[0], :] = tile

    force_pieces(f_outer, f_mid, z16, lane, 0, 0, 0, own_put)
    for d in TRAVELS:

        def put(k, tile, f=WHERE[d][2]["F"]):
            send[f + k : f + k + tile.shape[0], :] = tile

        force_pieces(f_outer, f_mid, z16, lane, *d, put)
    for d in TRAVELS:

        @pl.when(present(sizes, me, d))
        def _():
            force_copy(d).start()

    prepare(base_s, off_s, wxy, w_hi, w_lo)

    def forward(dx):
        @pl.when(present(sizes, me, (-dx, 0, 0)))
        def _():
            fields((dx, 0, 0)).wait_recv()
            tiles = face_tiles(recv, WHERE[dx, 0, 0][2]["U"], sub)
            for dy in (1, -1):
                u = WHERE[dx, dy, 0][2]["U"]
                for t, tile in enumerate(paired(tiles, 2, dy, sub)):
                    send[u + 8 * t : u + 8 * t + 8, :] = tile

                @pl.when(present(sizes, me, (-dx, dy, 0)))
                def _():
                    fields((dx, dy, 0)).start()

    low_half = me[0] < sizes[0] // 2

    @pl.when(low_half)
    def _():
        forward(1)
        forward(-1)

    @pl.when(jnp.logical_not(low_half))
    def _():
        forward(-1)
        forward(1)

    for d in TRAVELS:

        @pl.when(present(sizes, me, back(d)))
        def _():
            force_copy(d).wait_recv()
            if d in edges or (d in faces and d[0] == 0):
                fields(d).wait_recv()

    for d in TRAVELS:

        @pl.when(present(sizes, me, d))
        def _():
            force_copy(d).wait_send()
            if d in faces:
                fields(d).wait_send()

        if d in edges:

            @pl.when(present(sizes, me, (-d[0], d[1], 0)))
            def _():
                fields(d).wait_send()


def collide(p, c, rho, u, f):
    inv = 0.5 / rho
    v = [a + inv * b for a, b in zip(u, f)]
    vv = v[0] * v[0] + v[1] * v[1] + v[2] * v[2]
    vf = v[0] * f[0] + v[1] * f[1] + v[2] * f[2]
    factor = 1.0 - 0.5 / TAU
    a0 = (1.0 / TAU) * rho * (1.0 - 1.5 * vv) - (3.0 * factor) * vf
    a1 = (3.0 / TAU) * rho
    a2 = (4.5 / TAU) * rho
    cx, cy, cz, w = c
    pr = cx * v[0] + cy * v[1] + cz * v[2]
    cf = cx * f[0] + cy * f[1] + cz * f[2]
    poly = a0 + pr * (a1 + a2 * pr) + cf * (3.0 * factor + (9.0 * factor) * pr)
    return (1.0 - 1.0 / TAU) * p + w * poly


def forces(recv, ownf, force):
    zl = iota((1, 256), 1)
    zl = jnp.where(zl < 132, zl, jnp.where(zl >= 252, zl - 256, -5000)).astype(F32)
    k8 = iota((8, 1), 0).astype(F32)
    out = {}
    for sx in (-1, 0, 1):
        parts, zs = [], []
        for sy, sz in itertools.product((-1, 0, 1), (0, -1, 1)):
            kn = 8 if sz else 16
            if (sx, sy, sz) == (0, 0, 0):
                ref, f = ownf, 0
            else:
                ref, f = recv, WHERE[-sx, -sy, -sz][2]["F"]
            tile = ref[f : f + kn, :]
            if sx == 0:
                tile = jnp.concatenate([tile, ref[f + kn : f + 2 * kn, :]], axis=1)
            else:
                tile = jnp.where(iota((kn, 128), 0) < USED[kn], tile, 0.0)
            parts.append(tile)
            if sz == 0:
                zs.append(tile[:, 120:121] if sx else tile[:, 192:193])
            else:
                zs.append(k8 + (-1.0 if sz == -1 else 124.0))
        g = jnp.concatenate(parts, axis=0)
        z = jnp.concatenate(zs, axis=0)
        place = jnp.where(z == zl, 1.0, 0.0).astype(BF16)
        hi, lo = halves(g.T)
        out[sx] = dot(hi, place, 1, 0) + dot(lo, place, 1, 0)
    for a, x in itertools.product(range(3), range(8)):
        tile = out[0][64 * a + 8 * x : 64 * a + 8 * x + 8]
        if x < 5:
            tile = tile + out[-1][40 * a + 8 * x : 40 * a + 8 * x + 8]
        if x >= 3:
            tile = tile + out[1][40 * a + 8 * x - 24 : 40 * a + 8 * x - 16]
        force[a, x] = tile


SIDES = (-1, 0, 1)
X0 = {-1: 0, 0: 4, 1: 10}


def spans(sx):
    return range(6) if sx == 0 else range(4)


def assemble(recv, vel, ext, lane, sub):
    low4 = (lane & 7) < 4
    above_rows = bits(sub, (0, 1))
    for sx in SIDES:
        xs = spans(sx)
        side = face_tiles(recv, WHERE[-sx, 0, 0][2]["U"], sub) if sx else None
        above, below = WHERE[-sx, -1, 0][2]["U"], WHERE[-sx, 1, 0][2]["U"]
        for a, x in itertools.product(range(3), xs):
            own = side[4 * a + x] if sx else vel[a, x]
            t = 8 * (a * (len(xs) // 2) + x // 2)
            up = recv[above + t : above + t + 8, :]
            dn = recv[below + t : below + t + 8, :]
            if x % 2:
                up, dn = roll(up, 4, 0), roll(dn, 4, 0)
            ext[a, X0[sx] + x, 0:8, 0:128] = jnp.where(sub < 6, own, up)
            ext[a, X0[sx] + x, 8:16, 0:128] = jnp.where(above_rows, up, jnp.where(sub >= 4, dn, 0.0))

        def merged(sy, t):
            lower = WHERE[-sx, -sy, 1][2]["Z"] + 8 * t
            upper = WHERE[-sx, -sy, -1][2]["Z"] + 8 * t
            return jnp.where(low4, recv[lower : lower + 8, :], recv[upper : upper + 8, :])

        count = 3 * len(xs)
        for t in range((count + 15) // 16):
            slots = range(16 * t, min(16 * t + 16, count))
            m_up, m_dn = roll(merged(1, t), 6, 0), roll(merged(-1, t), 2, 0)
            m_own = merged(0, t + 3 if sx == 0 else t)
            inner = jnp.where(sub < 6, m_own, m_up)
            second = jnp.where(above_rows, m_up, jnp.where(sub >= 4, m_dn, 0.0))
            for s in slots:
                a, x = s // len(xs), s % len(xs)
                ext[a, X0[sx] + x, 0:8, 128:256] = unpack(inner, s)
                ext[a, X0[sx] + x, 8:16, 128:256] = unpack(second, s)


def prepare(base_s, off_s, wxy, w_hi, w_lo):
    base, frac = base_s[...], off_s[...]
    four = [four_weights(frac, a) for a in range(3)]
    n = iota((16, 1), 0)
    wxy[0:16, :] = node_weights(n - 4, base[0:1], four[0])
    wxy[16:32, :] = node_weights(jnp.where(n < 10, n, n - 16), base[1:2], four[1])
    w_hi[...] = jnp.zeros(w_hi.shape, BF16)
    w_lo[...] = jnp.zeros(w_lo.shape, BF16)
    for begin, rows, shift in ((0, 144, 0), (240, 16, 256)):
        hi, lo = halves(node_weights(iota((rows, 1), 0) + (begin - shift), base[2:3], four[2]))
        w_hi[begin : begin + rows, :] = hi
        w_lo[begin : begin + rows, :] = lo


def interpolate(ext, wxy, w_hi, w_lo, alive, out):
    wy = wxy[16:32, :]
    for a in range(3):
        e_hi, e_lo = halves(ext[a].reshape(14 * 16, 256))
        p = dot(e_hi, w_hi[...], 1, 0) + dot(e_lo, w_hi[...], 1, 0) + dot(e_hi, w_lo[...], 1, 0)
        total = jnp.zeros((16, VP), F32)
        for x in range(14):
            total = total + p[16 * x : 16 * x + 16] * wxy[x : x + 1, :]
        row = jnp.sum(total * wy, axis=0, keepdims=True) * alive
        out[a] = row[:, 0:NV]


def step_nodes(col, recv, ext, force, raw, moved, ends, nxt, lane, sub):
    wall = jnp.full((8, 128), jnp.nan, F32)
    low4 = (lane & 7) < 4
    side = jnp.where(lane[0:1] >= 64, 1.0, -1.0)

    def shifts(cz):
        edge = ((cz > 0.5) & (lane == 127)) | ((cz < -0.5) & (lane == 0))

        def move(s, z):
            a = jnp.where(edge, z, s)
            return jnp.where(cz > 0.5, roll(a, 1, 1), jnp.where(cz < -0.5, roll(a, 127, 1), a))

        return move

    cs = [constants(sub, natural_numbers(k)) for k in range(3)]
    movers = [shifts(c[2]) for c in cs]
    c_up, c_down = [constants(sub, [rows.get(r) for r in range(8)]) for rows in (UP, DOWN)]
    c_end = [jnp.where(lane >= 64, a, b) for a, b in zip(c_up, c_down)]
    z_low = WHERE[0, 0, 1][2]["Z"]
    z_high = WHERE[0, 0, -1][2]["Z"]
    for t in range(3):
        merged = jnp.where(low4, recv[z_low + 8 * t : z_low + 8 * t + 8, :], recv[z_high + 8 * t : z_high + 8 * t + 8, :])
        for s in range(16):
            ends[16 * t + s] = unpack(merged, s)

    def own_columns(x, carry):
        for y in range(BY):
            i = x * BY + y
            rho, flag = col[i, RHO : RHO + 1, :], col[i, FLAG : FLAG + 1, :]
            u = [col[i, VEL + a : VEL + a + 1, :] for a in range(3)]
            f = [force[a, x + 1, y : y + 1, 0:128] for a in range(3)]
            fz = [force[a, x + 1, y : y + 1, 128:256] for a in range(3)]
            uz = [ext[a, x + 4, y : y + 1, 128:256] for a in range(3)]
            rho_z, flag_z = ends[36 + x, y : y + 1, :], ends[42 + x, y : y + 1, :]
            rz = collide(ends[i], c_end, rho_z, uz, fz)
            sz = jnp.where(flag_z > 0.5, rz, wall)
            for k in range(3):
                r = collide(col[i, 8 * k : 8 * k + 8, :], cs[k], rho, u, f)
                raw[i, 8 * k : 8 * k + 8, :] = r
                s = jnp.where(flag > 0.5, r, wall)
                moved[x + 1, y + 1, 8 * k : 8 * k + 8, :] = movers[k](s, sz)
        return carry

    for x in range(BX):
        own_columns(x, 0)

    for face, (rows, r_rho, r_flag) in FACE.items():
        dx, dy = face
        numbers = [rows.get(r) for r in range(8)]
        c = constants(sub, numbers)
        mover = shifts(c[2])
        ring = WHERE[dx, dy, 0][2]["R"]
        count = 1 if dx and dy else 6
        if count == 6:
            if dx:
                z = [WHERE[dx, 0, s][2]["Z"] for s in (1, -1)]
                slot = 12
            else:
                z = [WHERE[0, dy, s][2]["Z"] + 8 for s in (1, -1)]
                slot = 2
            pz = jnp.where(low4, recv[z[0] : z[0] + 8, :], recv[z[1] : z[1] + 8, :])
            tz = [unpack(pz, slot + t) for t in range(3)]
            cz = (float(dx), float(dy), side, 1.0 / 36.0)
        for j in range(count):
            x = {1: -1, -1: 6, 0: j}[dx]
            y = {1: -1, -1: 6, 0: j}[dy]
            t = recv[ring + 8 * j : ring + 8 * j + 8, :]
            rho, flag = t[r_rho : r_rho + 1], t[r_flag : r_flag + 1]
            yu, yf = y % 16, y % 8
            if count == 6:
                u = [ext[a, x + 4, yu : yu + 1, 0:128] for a in range(3)]
            else:
                u = [t[EDGE_VEL + a : EDGE_VEL + a + 1] for a in range(3)]
            f = [force[a, x + 1, yf : yf + 1, 0:128] for a in range(3)]
            s = jnp.where(flag > 0.5, collide(t, c, rho, u, f), wall)
            if count == 6:
                uz = [ext[a, x + 4, yu : yu + 1, 128:256] for a in range(3)]
                fz = [force[a, x + 1, yf : yf + 1, 128:256] for a in range(3)]
                rz = collide(tz[0][j : j + 1], cz, tz[1][j : j + 1], uz, fz)
                sz = jnp.where(tz[2][j : j + 1] > 0.5, rz, wall[0:1])
                s = mover(s, sz)
            for k in sorted({q // 8 for q in rows.values()}):
                out = None
                for shift in sorted({(q - r) % 8 for r, q in rows.items() if q // 8 == k}):
                    tile = roll(s, shift, 0)
                    members = [q % 8 for r, q in rows.items() if q // 8 == k and (q - r) % 8 == shift]
                    out = tile if out is None else jnp.where(bits(sub, members), tile, out)
                moved[x + 1, y + 1, 8 * k : 8 * k + 8, :] = out

    odd = (iota((24, 128), 0) & 1) == 1
    start = iota((24, 128), 0) == 0

    def passing(x, carry):
        for y in range(BY):
            i = x * BY + y
            r = raw[i]
            turned = jnp.where(start, r, jnp.where(odd, roll(r, 23, 0), roll(r, 1, 0)))
            for k in range(3):
                sources = {}
                for q in natural_numbers(k):
                    if q is not None:
                        sources.setdefault(LATTICE[q][:2], []).append(q % 8)
                out = None
                for (cx, cy), members in sources.items():
                    tile = moved[x + 1 - cx, y + 1 - cy, 8 * k : 8 * k + 8, :]
                    out = tile if out is None else jnp.where(bits(sub, members), tile, out)
                out = jnp.where(out == out, out, turned[8 * k : 8 * k + 8])
                last = min(8 * k + 8, 19)
                nxt[i, 8 * k : last, :] = out[0 : last - 8 * k]
        return carry

    for x in range(BX):
        passing(x, 0)


def finish(col, vel, ownf, recv, wxy, w_hi, w_lo, occ, nxt, vtx, ext, force, raw, moved, ends):
    lane = iota((8, 128), 1)
    sub = iota((8, 128), 0)
    alive = (occ[...] > 0).astype(F32)
    assemble(recv, vel, ext, lane, sub)
    forces(recv, ownf, force)
    step_nodes(col, recv, ext, force, raw, moved, ends, nxt, lane, sub)
    interpolate(ext, wxy, w_hi, w_lo, alive, vtx)


def on_device(sizes, populations, fluid_mask, stencil_base, offsets, occupied_cell_slots, triangles):
    pops = jnp.transpose(populations, (1, 2, 0, 3)).reshape(BX * BY, 19, BZ)
    base = stencil_base.reshape(3, 1, NV)
    off = offsets.reshape(3, 1, NV)
    occ = occupied_cell_slots.reshape(1, 1)
    vmem = pl.BlockSpec(memory_space=pltpu.VMEM)
    hbm = pl.BlockSpec(memory_space=pltpu.HBM)
    shape = jax.ShapeDtypeStruct
    dma = pltpu.SemaphoreType.DMA
    vm = pltpu.VMEM
    middle = pl.pallas_call(
        functools.partial(send_all, sizes),
        name="cells_and_halo",
        out_shape=(
            shape((36, 24, 128), F32),
            shape((3, 6, 8, 128), F32),
            shape((32, 128), F32),
            shape((ROWS, 128), F32),
            shape((32, VP), F32),
            shape((256, VP), BF16),
            shape((256, VP), BF16),
        ),
        in_specs=[hbm, hbm, hbm, hbm, vmem, hbm],
        out_specs=(vmem,) * 7,
        scratch_shapes=[
            vm((ROWS, 128), F32),
            vm((6, 8, 128), I32),
            vm((3, 1, NV), I32),
            vm((3, 1, NV), F32),
            vm((3, NT), I32),
            vm((8, VP), I32),
            vm((8, VP), F32),
            vm((VP, NT), BF16),
            vm((384, VP), F32),
            vm((192, VP), F32),
            vm((24, 128), F32),
            vm((6, 8, 128), F32),
            dma((5,)),
            dma((26,)),
            dma((26,)),
            dma((26,)),
            dma((26,)),
        ],
        compiler_params=pltpu.CompilerParams(collective_id=0, has_side_effects=True, vmem_limit_bytes=48 << 20),
    )(*(pltpu.with_memory_space_constraint(a, pltpu.HBM) for a in (pops, fluid_mask, base, off)), occ, pltpu.with_memory_space_constraint(triangles.T, pltpu.HBM))
    nxt, vtx = pl.pallas_call(
        finish,
        name="collide_and_pass",
        out_shape=(shape((36, 19, 128), F32), shape((3, 1, NV), F32)),
        in_specs=[vmem] * 8,
        out_specs=(vmem, vmem),
        scratch_shapes=[
            vm((3, 14, 16, 256), F32),
            vm((3, 8, 8, 256), F32),
            vm((36, 24, 128), F32),
            vm((8, 8, 24, 128), F32),
            vm((48, 8, 128), F32),
        ],
        compiler_params=pltpu.CompilerParams(vmem_limit_bytes=48 << 20),
    )(*middle, occ)
    nxt = jnp.transpose(nxt.reshape(BX, BY, 19, BZ), (2, 0, 1, 3))
    return nxt, vtx.reshape(1, 1, 1, 3, NV)


def solution(mesh):
    sizes = tuple(mesh.shape[a] for a in AXES)
    placed = (
        P(None, "gx", "gy", "gz"),
        P("gx", "gy", "gz"),
        P("gx", "gy", "gz", None, None),
        P("gx", "gy", "gz", None, None),
        P("gx", "gy", "gz"),
        P(),
    )
    return jax.shard_map(
        functools.partial(on_device, sizes),
        mesh=mesh,
        in_specs=placed,
        out_specs=(P(None, "gx", "gy", "gz"), P("gx", "gy", "gz", None, None)),
        check_vma=False,
    )
```

```python
import functools
import itertools
import math

import jax
import jax.numpy as jnp
from jax import lax
from jax.experimental import pallas as pl
from jax.experimental.pallas import tpu as pltpu
from jax.sharding import PartitionSpec as P

MESH = pl.DeviceIdType.MESH
AXES = ("gx", "gy", "gz")
NV = 642
VP = 768
NT = 1280
BX, BY, BZ = 6, 6, 128
F32, BF16, I32 = jnp.float32, jnp.bfloat16, jnp.int32
FAR = -10000
STIFFNESS, REST, TAU = 0.1, 4.0, 0.8

LATTICE = (
    (0, 0, 0),
    (1, 0, 0),
    (-1, 0, 0),
    (0, 1, 0),
    (0, -1, 0),
    (0, 0, 1),
    (0, 0, -1),
    (1, 1, 0),
    (-1, -1, 0),
    (1, -1, 0),
    (-1, 1, 0),
    (1, 0, 1),
    (-1, 0, -1),
    (1, 0, -1),
    (-1, 0, 1),
    (0, 1, 1),
    (0, -1, -1),
    (0, 1, -1),
    (0, -1, 1),
)
WEIGHT = [1.0 / 3.0] + [1.0 / 18.0] * 6 + [1.0 / 36.0] * 12
NUMBER = {c: q for q, c in enumerate(LATTICE)}

RHO, FLAG, VEL = 19, 20, 21

FACE = {
    (1, 0): ({1: 1, 7: 7, 3: 11, 5: 13, 2: 9}, 0, 4),
    (-1, 0): ({2: 2, 0: 8, 4: 12, 6: 14, 3: 10}, 1, 5),
    (0, 1): ({3: 3, 7: 7, 2: 10, 1: 17, 0: 15}, 4, 5),
    (0, -1): ({4: 4, 0: 8, 1: 9, 2: 18, 3: 16}, 5, 6),
    (1, 1): ({7: 7}, 0, 1),
    (1, -1): ({1: 9}, 0, 2),
    (-1, 1): ({2: 10}, 0, 1),
    (-1, -1): ({0: 8}, 1, 2),
}
UP = {5: 5, 3: 11, 6: 14, 7: 15, 2: 18}
DOWN = {6: 6, 4: 12, 5: 13, 0: 16, 1: 17}
EDGE_VEL = 3
TRAVELS = [d for d in itertools.product((-1, 0, 1), repeat=3) if d != (0, 0, 0)]
TRAVELS.sort(key=lambda d: (d[0] == 0, d[2] != 0, d[1] != 0))


def layout():
    where, row = {}, 0
    for d in TRAVELS:
        dx, dy, dz = d
        rows = {}
        if dx and dy and dz == 0:
            rows["R"] = 8
        rows["F"] = (16 if dz == 0 else 8) * (2 if dx == 0 else 1)
        if dz == 0:
            if not (dx and dy):
                rows["R"] = 48
            rows["U"] = 48 if dx and dy else 72
        else:
            rows["Z"] = 8 if dx else 16 if dy else 40
        spot, begin = {}, row
        for part, count in rows.items():
            spot[part] = row
            row += count
        where[d] = (begin, row - begin, spot)
    return where, row


WHERE, ROWS = layout()
USED = {16: 11, 8: 5}


def iota(shape, axis):
    return lax.broadcasted_iota(I32, shape, axis)


def bits(index, members):
    code = sum(1 << m for m in members)
    return (lax.shift_right_logical(jnp.full(index.shape, code, I32), index) & 1) == 1


def per_row(sub, values):
    out = jnp.zeros(sub.shape, F32)
    for value in sorted(set(values)):
        if value != 0:
            members = [r for r, v in enumerate(values) if v == value]
            out = jnp.where(bits(sub, members), F32(value), out)
    return out


def constants(sub, numbers):
    rows = [[0 if q is None else LATTICE[q][a] for q in numbers] for a in range(3)]
    rows.append([0 if q is None else WEIGHT[q] for q in numbers])
    return [per_row(sub, r) for r in rows]


def natural_numbers(k):
    return [q if q < 19 else None for q in range(8 * k, 8 * k + 8)]


def sin_half_pi(f):
    t = f * (0.5 * math.pi)
    t2 = t * t
    out = jnp.full(f.shape, 1.0 / math.factorial(13), F32)
    for k in (11, 9, 7, 5, 3, 1):
        sign = 1.0 if (13 - k) // 2 % 2 == 0 else -1.0
        out = out * t2 + sign / math.factorial(k)
    return out * t


def node_weights(n, base, four):
    d = n - base
    out = jnp.where(d == 3, four[3], 0.0)
    for k in (2, 1, 0):
        out = jnp.where(d == k, four[k], out)
    return out


def four_weights(frac, axis):
    s = sin_half_pi(frac)[axis : axis + 1]
    c = sin_half_pi(1.0 - frac)[axis : axis + 1]
    return [0.25 * (1.0 - s), 0.25 * (1.0 + c), 0.25 * (1.0 + s), 0.25 * (1.0 - c)]


def halves(x):
    hi = x.astype(BF16)
    return hi, (x - hi.astype(F32)).astype(BF16)


def thirds(x):
    hi = x.astype(BF16)
    rest = x - hi.astype(F32)
    mid = rest.astype(BF16)
    return jnp.concatenate([hi, mid, (rest - mid.astype(F32)).astype(BF16)], axis=0)


def dot(a, b, ca, cb):
    return lax.dot_general(a, b, (((ca,), (cb,)), ((), ())), preferred_element_type=F32)


def load_vertices(base, off, base_s, off_s):
    base_s[...] = jnp.full((8, VP), FAR, I32)
    off_s[...] = jnp.zeros((8, VP), F32)
    for a in range(3):
        base_s[a : a + 1, 0:NV] = base[a]
        off_s[a : a + 1, 0:NV] = off[a]


def turn(t, sub):
    one = jnp.where(sub == 2, roll(t, 2, 0), roll(t, 7, 0))
    two = jnp.where(sub == 0, roll(t, 6, 0), roll(t, 1, 0))
    return one, two


def incidence_of(tri, incidence):
    def fill(step, carry):
        rows = pl.multiple_of(step * 16, 16)
        vertex = iota((16, NT), 0) + rows
        hit = (vertex == tri[0:1]) | (vertex == tri[1:2]) | (vertex == tri[2:3])
        incidence[pl.ds(rows, 16), :] = jnp.where(hit, 1.0, 0.0).astype(BF16)
        return carry

    lax.fori_loop(0, 41, fill, 0)
    incidence[656:VP, :] = jnp.zeros((VP - 656, NT), BF16)


def membrane(base_s, off_s, alive, incidence):
    sub = iota((8, VP), 0)
    base = base_s[...]
    x = jnp.where((base > FAR // 2) & (sub < 3), (base - base[:, 0:1]).astype(F32) + off_s[...], 0.0)
    x1, x2 = turn(x, sub)
    xx = x * x
    r2 = xx + x1 * x1 + x2 * x2
    first = (r2 - REST * REST) * x + jnp.where(sub == 3, 1.0, 0.0) + roll(x, 4, 0)
    second = xx + roll(x * x1, 4, 0)
    sums = dot(thirds(jnp.concatenate([first, second], axis=0)), incidence[...], 1, 0)
    sums = sums[0:16] + sums[16:32] + sums[32:48]
    back = dot(thirds(sums), incidence[...], 1, 1)
    back = back[0:16] + back[16:32] + back[32:48]
    cubic, diag = back[0:8], back[8:16]
    count = cubic[3:4]
    lin, cross = roll(cubic, 4, 0), roll(diag, 4, 0)
    turned = diag * x + cross * x1 + turn(cross, sub)[1] * x2
    along, trace = x * lin, jnp.where(sub < 3, diag, 0.0)
    along = along + sum(turn(along, sub))
    trace = trace + sum(turn(trace, sub))
    common = 2.0 * along - r2 * count - (trace - REST * REST * count)
    total = cubic - 2.0 * turned + r2 * lin + x * common
    return (STIFFNESS / (REST * REST)) * alive * total


YN = {0: (0, 1, 2, 3, 4, 5, 6, -1), 1: (6, 7, 8, 9, 10, 11, 12, 5), -1: (-6, -5, -4, -3, -2, -1, 0, -7)}
DYS = (0, 1, -1)


def spread_own(base_s, off_s, loads, outer, mid):
    base, frac = base_s[...], off_s[...]
    four = [four_weights(frac, a) for a in range(3)]
    low = jnp.min(jnp.where(base[2:3] > FAR // 2, base[2:3], 1 << 20), axis=1, keepdims=True)
    k = iota((32, 1), 0)
    z = jnp.where(k < 16, low + k, jnp.where(k < 24, 127 - 16 + k, -4 - 24 + k))
    wz = node_weights(z, base[2:3], four[2])
    left = jnp.concatenate([wz * loads[c : c + 1] for c in range(3)], axis=0)
    wx = node_weights(iota((16, 1), 0) - 4, base[0:1], four[0])
    row8 = iota((8, 1), 0)
    for i, dy in enumerate(DYS):
        n = jnp.where(row8 == 7, YN[dy][7], row8 + YN[dy][0])
        wy = node_weights(n, base[1:2], four[1])
        for j in range(5):
            outer[i * 128 + j * 8 : i * 128 + j * 8 + 8, :] = wx[9 + j : 10 + j] * wy
            outer[i * 128 + 40 + j * 8 : i * 128 + 48 + j * 8, :] = wx[j : j + 1] * wy
        outer[i * 128 + 80 : i * 128 + 128, :] = jnp.zeros((48, VP), F32)
        for j in range(8):
            mid[i * 64 + j * 8 : i * 64 + j * 8 + 8, :] = wx[3 + j : 4 + j] * wy
    l_hi, l_lo = halves(left)
    both = jnp.concatenate([l_hi, l_lo], axis=0)

    def product(ref):
        r_hi, r_lo = halves(ref[...])
        out = dot(both, r_hi, 1, 1)
        return out[0:96] + out[96:192] + dot(l_hi, r_lo, 1, 1)

    return product(outer), product(mid), z[0:16].astype(F32)


def roll(x, shift, axis):
    shift = shift % x.shape[axis]
    return x if shift == 0 else pltpu.roll(x, shift, axis)


def force_pieces(outer, mid, z16, lane, dx, dy, dz, put):
    k0, kn = {0: (0, 16), 1: (16, 8), -1: (24, 8)}[dz]
    i = DYS.index(dy)
    lane = iota((kn, 128), 1)
    if dx:
        off = 0 if dx == 1 else 40
        out = jnp.zeros((kn, 128), F32)
        for c in range(3):
            tile = outer[32 * c + k0 : 32 * c + k0 + kn, i * 128 : i * 128 + 128]
            tile = roll(tile, 40 * c - off, 1)
            out = jnp.where((lane >= 40 * c) & (lane < 40 * c + 40), tile, out)
        if dz == 0:
            out = jnp.where(lane >= 120, z16, out)
        put(0, out)
        return
    tiles = []
    for c in range(3):
        t = i // 2 * 128
        tile = mid[32 * c + k0 : 32 * c + k0 + kn, t : t + (128 if i < 2 else 64)]
        if i == 2:
            tile = jnp.concatenate([tile, jnp.zeros((kn, 64), F32)], axis=1)
        tiles.append(roll(tile, 64 * (c % 2) - 64 * (i % 2), 1))
    put(0, jnp.where(lane < 64, tiles[0], tiles[1]))
    rest = z16 if dz == 0 else jnp.zeros((kn, 128), F32)
    put(kn, jnp.where(lane < 64, tiles[2], rest))


def pack(tiles, lane):
    out = jnp.zeros((8, 128), F32)
    for s, tile in enumerate(tiles):
        out = jnp.where((lane >= 8 * s) & (lane < 8 * s + 8), roll(tile, 4 + 8 * s, 1), out)
    return out


def unpack(packed, s):
    return roll(packed, -(4 + 8 * (s % 16)), 1)


def coords():
    return [lax.axis_index(a) for a in AXES]


def present_at(sizes, me, d):
    ok = None
    for m, s, size in zip(me, d, sizes):
        if s:
            here = m < size - 1 if s == 1 else m > 0
            ok = here if ok is None else jnp.logical_and(ok, here)
    return ok


def face_tiles(ref, begin, sub):
    tiles = []
    for a in range(3):
        t = [ref[begin + 8 * (3 * a + j) : begin + 8 * (3 * a + j) + 8, :] for j in range(3)]
        last = jnp.where(sub < 2, roll(t[0], 2, 0), jnp.where(sub < 4, roll(t[1], 4, 0), roll(t[2], 6, 0)))
        tiles += t + [last]
    return tiles


def paired(tiles, half, dy, sub):
    out = []
    for t in range(3 * half):
        one, two = tiles[2 * t], tiles[2 * t + 1]
        if dy == 1:
            out.append(jnp.where(sub >= 4, roll(one, 2, 0), roll(two, 6, 0)))
        else:
            out.append(jnp.where(bits(sub, (0, 1, 6, 7)), roll(one, 6, 0), roll(two, 2, 0)))
    return out


def back(d):
    return tuple(-s for s in d)


def send_all(sizes, pops, mask, base, off, occ, tri, col, vel, ownf, recv, wxy, w_hi, w_lo, send, mask_s, base_v, off_v, tri_v, base_s, off_s, incidence, outer, mid, edge_s, rho_s, in_sem, send_sem, recv_sem, fsend_sem, frecv_sem):
    me = coords()
    there = {d: present_at(sizes, me, d) for d in TRAVELS}

    def present(sizes, me, d):
        return there[d]

    ins = [(pops, col.at[:, pl.ds(0, 19), :]), (mask, mask_s.at[:, pl.ds(0, 6), :]), (base, base_v), (off, off_v), (tri, tri_v)]
    ins = [pltpu.make_async_copy(a, b, in_sem.at[k]) for k, (a, b) in enumerate(ins)]
    for copy in ins:
        copy.start()
    def at(d):
        return tuple(m + s for m, s in zip(me, d))

    barrier = pltpu.get_barrier_semaphore()
    count = jnp.int32(0)
    for d in TRAVELS:
        ok = present(sizes, me, d)
        count = count + ok.astype(I32)

        @pl.when(ok)
        def _():
            pl.semaphore_signal(barrier, inc=1, device_id=at(d), device_id_type=MESH)

    lane = iota((8, 128), 1)
    sub = iota((8, 128), 0)
    for d in TRAVELS:

        @pl.when(jnp.logical_not(present(sizes, me, back(d))))
        def _():
            begin, rows, _ = WHERE[d]
            recv[begin : begin + rows, :] = jnp.zeros((rows, 128), F32)

    cs = [constants(sub, natural_numbers(k)) for k in range(3)]
    vel[...] = jnp.zeros(vel.shape, F32)
    rho_s[...] = jnp.zeros(rho_s.shape, F32)
    for copy in ins:
        copy.wait()

    def columns(x, carry):
        for y in range(BY):
            i = x * BY + y
            col[i, 19:24, :] = jnp.zeros((5, 128), F32)
            v = [col[i, 8 * k : 8 * k + 8, :] for k in range(3)]
            rho = jnp.sum(v[0] + v[1] + v[2], axis=0, keepdims=True)
            col[i, RHO : RHO + 1, :] = rho
            rho_s[x, y : y + 1, :] = rho
            col[i, FLAG : FLAG + 1, :] = mask_s[x, y : y + 1, :].astype(F32)
            for a in range(3):
                m = v[0] * cs[0][a] + v[1] * cs[1][a] + v[2] * cs[2][a]
                u = jnp.sum(m, axis=0, keepdims=True) / rho
                col[i, VEL + a : VEL + a + 1, :] = u
                vel[a, x, y : y + 1, :] = u
        return carry

    lax.fori_loop(0, BX, columns, 0)

    def ring_tile(i, face):
        rows, r_rho, r_flag = FACE[face]
        out = jnp.where(sub == r_rho, col[i, RHO : RHO + 1, :], col[i, FLAG : FLAG + 1, :])
        moves = {}
        for r, q in rows.items():
            moves.setdefault((q // 8, (r - q) % 8), []).append(r)
        for (k, shift), members in moves.items():
            out = jnp.where(bits(sub, members), roll(col[i, 8 * k : 8 * k + 8, :], shift, 0), out)
        return out

    def ends_of(e_rows, dx, dy, column):
        up, down = NUMBER[dx, dy, 1], NUMBER[dx, dy, -1]
        edge_s[...] = jnp.zeros((24, 128), F32)
        for j in range(6):
            i = column(j)
            edge_s[j : j + 1, :] = jnp.where(lane[0:1] >= 64, col[i, up : up + 1, :], col[i, down : down + 1, :])
            edge_s[8 + j : 9 + j, :] = col[i, RHO : RHO + 1, :]
            edge_s[16 + j : 17 + j, :] = col[i, FLAG : FLAG + 1, :]
        return [edge_s[8 * t : 8 * t + 8, :] for t in range(3)]

    us = [vel[a, x] for a in range(3) for x in range(6)]
    first = pack(us[:16], lane)
    for dx in (1, -1):
        u, r = WHERE[dx, 0, 0][2]["U"], WHERE[dx, 0, 0][2]["R"]
        xs = range(2, 6) if dx == 1 else range(4)
        x = 5 if dx == 1 else 0
        for a, j in itertools.product(range(3), range(3)):
            t = u + 8 * (3 * a + j)
            send[t : t + 8, :] = jnp.where(sub < 6, vel[a, xs[j]], roll(vel[a, xs[3]], 6 - 2 * j, 0))
        for y in range(6):
            send[r + 8 * y : r + 8 * y + 8, :] = ring_tile(x * BY + y, (dx, 0))
        for dy in (1, -1):
            r = WHERE[dx, dy, 0][2]["R"]
            i = x * BY + (5 if dy == 1 else 0)
            send[r : r + 8, :] = ring_tile(i, (dx, dy))
            send[r + EDGE_VEL : r + EDGE_VEL + 3, :] = col[i, VEL : VEL + 3, :]
    for dy in (1, -1):
        u, r = WHERE[0, dy, 0][2]["U"], WHERE[0, dy, 0][2]["R"]
        y = 5 if dy == 1 else 0
        for t, tile in enumerate(paired(us, 3, dy, sub)):
            send[u + 8 * t : u + 8 * t + 8, :] = tile
        for x in range(6):
            send[r + 8 * x : r + 8 * x + 8, :] = ring_tile(x * BY + y, (0, dy))
        second = pack(us[16:] + ends_of(edge_s, 0, dy, lambda j: j * BY + y), lane)
        for dz in (1, -1):
            z = WHERE[0, dy, dz][2]["Z"]
            send[z : z + 8, :] = first
            send[z + 8 : z + 16, :] = second
    z = WHERE[0, 0, 1][2]["Z"]
    pick = []
    for k in range(2):
        ups = [r for r, q in UP.items() if q // 8 == k]
        downs = [r for r, q in DOWN.items() if q // 8 == k]
        pick.append(((lane >= 64) & bits(sub, ups)) | ((lane < 64) & bits(sub, downs)))
    tiles = []
    for i in range(BX * BY):
        v = [col[i, 8 * k : 8 * k + 8, :] for k in range(3)]
        tiles.append(jnp.where(pick[0], v[0], jnp.where(pick[1], v[1], v[2])))
    tiles += [rho_s[x] for x in range(6)] + [mask_s[x].astype(F32) for x in range(6)] + us
    for t in range(5):
        send[z + 8 * t : z + 8 * t + 8, :] = pack(tiles[16 * t : 16 * t + 16], lane)

    load_vertices(base_v, off_v, base_s, off_s)
    alive = (occ[...] > 0).astype(F32)
    incidence_of(tri_v, incidence)
    pl.semaphore_wait(barrier, count)

    def copy(src, dst, rows, to, sems, t):
        return pltpu.make_async_remote_copy(
            src_ref=send.at[pl.ds(src, rows)],
            dst_ref=recv.at[pl.ds(dst, rows)],
            send_sem=sems[0].at[t],
            recv_sem=sems[1].at[t],
            device_id=at(to),
            device_id_type=MESH,
        )

    faces = [d for d in TRAVELS if sum(map(abs, d)) == 1]
    relayed = [d for d in TRAVELS if d[0] and (d[1] or d[2])]


    def fields(d):
        dx, dy, dz = d
        begin, rows, spot = WHERE[d]
        t = TRAVELS.index(d)
        if d in relayed and dz:
            return copy(WHERE[dx, 0, 1][2]["Z"], spot["Z"], 8, (0, dy, dz), (send_sem, recv_sem), t)
        if d in relayed:
            return copy(spot["U"], spot["U"], 48, (0, dy, 0), (send_sem, recv_sem), t)
        row = spot["Z"] if dz else spot["R"]
        src = WHERE[0, 0, 1][2]["Z"] if dz else row
        return copy(src, row, begin + rows - row, d, (send_sem, recv_sem), t)

    def force_copy(d):
        begin, rows, spot = WHERE[d]
        if d[0]:
            rows = spot["F"] - begin + USED[8 if d[2] else 16]
        elif d in faces:
            rows = spot["Z" if d[2] else "R"] - begin
        return copy(begin, begin, rows, d, (fsend_sem, frecv_sem), TRAVELS.index(d))

    for d in faces:

        @pl.when(present(sizes, me, d))
        def _():
            fields(d).start()

    loads = membrane(base_s, off_s, alive, incidence)
    f_outer, f_mid, z16 = spread_own(base_s, off_s, loads, outer, mid)

    def own_put(k, tile):
        ownf[k : k + tile.shape[0], :] = tile

    force_pieces(f_outer, f_mid, z16, lane, 0, 0, 0, own_put)
    for d in TRAVELS:

        def put(k, tile, f=WHERE[d][2]["F"]):
            send[f + k : f + k + tile.shape[0], :] = tile

        force_pieces(f_outer, f_mid, z16, lane, *d, put)
    for d in TRAVELS:

        @pl.when(present(sizes, me, d))
        def _():
            force_copy(d).start()

    prepare(base_s, off_s, wxy, w_hi, w_lo)

    def forward(dx):
        @pl.when(present(sizes, me, (-dx, 0, 0)))
        def _():
            fields((dx, 0, 0)).wait_recv()
            tiles = face_tiles(recv, WHERE[dx, 0, 0][2]["U"], sub)
            for dy in (1, -1):
                u = WHERE[dx, dy, 0][2]["U"]
                for t, tile in enumerate(paired(tiles, 2, dy, sub)):
                    send[u + 8 * t : u + 8 * t + 8, :] = tile
            rows, r_rho, r_flag = FACE[dx, 0]
            ring, z = WHERE[dx, 0, 0][2]["R"], WHERE[dx, 0, 1][2]["Z"]
            row_of = {q: r for r, q in rows.items()}
            up, down = row_of[NUMBER[dx, 0, 1]], row_of[NUMBER[dx, 0, -1]]
            edge_s[...] = jnp.zeros((24, 128), F32)
            for y in range(6):
                t = recv[ring + 8 * y : ring + 8 * y + 8, :]
                edge_s[y : y + 1, :] = jnp.where(lane[0:1] >= 64, t[up : up + 1], t[down : down + 1])
                edge_s[8 + y : 9 + y, :] = t[r_rho : r_rho + 1]
                edge_s[16 + y : 17 + y, :] = t[r_flag : r_flag + 1]
            send[z : z + 8, :] = pack(tiles + [edge_s[8 * t : 8 * t + 8, :] for t in range(3)], lane)
            for d in relayed:
                if d[0] == dx:

                    @pl.when(present(sizes, me, (-dx, d[1], d[2])))
                    def _():
                        fields(d).start()

    low_half = me[0] < sizes[0] // 2

    @pl.when(low_half)
    def _():
        forward(1)
        forward(-1)

    @pl.when(jnp.logical_not(low_half))
    def _():
        forward(-1)
        forward(1)

    for d in TRAVELS:

        @pl.when(present(sizes, me, back(d)))
        def _():
            force_copy(d).wait_recv()
            if d in relayed or (d in faces and d[0] == 0):
                fields(d).wait_recv()

    for d in TRAVELS:

        @pl.when(present(sizes, me, d))
        def _():
            force_copy(d).wait_send()
            if d in faces:
                fields(d).wait_send()

        if d in relayed:

            @pl.when(present(sizes, me, (-d[0], d[1], d[2])))
            def _():
                fields(d).wait_send()


def collide(p, c, rho, u, f):
    inv = 0.5 / rho
    v = [a + inv * b for a, b in zip(u, f)]
    vv = v[0] * v[0] + v[1] * v[1] + v[2] * v[2]
    vf = v[0] * f[0] + v[1] * f[1] + v[2] * f[2]
    factor = 1.0 - 0.5 / TAU
    a0 = (1.0 / TAU) * rho * (1.0 - 1.5 * vv) - (3.0 * factor) * vf
    a1 = (3.0 / TAU) * rho
    a2 = (4.5 / TAU) * rho
    cx, cy, cz, w = c
    pr = cx * v[0] + cy * v[1] + cz * v[2]
    cf = cx * f[0] + cy * f[1] + cz * f[2]
    poly = a0 + pr * (a1 + a2 * pr) + cf * (3.0 * factor + (9.0 * factor) * pr)
    return (1.0 - 1.0 / TAU) * p + w * poly


def forces(recv, ownf, force):
    zl = iota((1, 256), 1)
    zl = jnp.where(zl < 132, zl, jnp.where(zl >= 252, zl - 256, -5000)).astype(F32)
    k8 = iota((8, 1), 0).astype(F32)
    out = {}
    for sx in (-1, 0, 1):
        parts, zs = [], []
        for sy, sz in itertools.product((-1, 0, 1), (0, -1, 1)):
            kn = 8 if sz else 16
            if (sx, sy, sz) == (0, 0, 0):
                ref, f = ownf, 0
            else:
                ref, f = recv, WHERE[-sx, -sy, -sz][2]["F"]
            tile = ref[f : f + kn, :]
            if sx == 0:
                tile = jnp.concatenate([tile, ref[f + kn : f + 2 * kn, :]], axis=1)
            else:
                tile = jnp.where(iota((kn, 128), 0) < USED[kn], tile, 0.0)
            parts.append(tile)
            if sz == 0:
                zs.append(tile[:, 120:121] if sx else tile[:, 192:193])
            else:
                zs.append(k8 + (-1.0 if sz == -1 else 124.0))
        g = jnp.concatenate(parts, axis=0)
        z = jnp.concatenate(zs, axis=0)
        place = jnp.where(z == zl, 1.0, 0.0).astype(BF16)
        hi, lo = halves(g.T)
        out[sx] = dot(hi, place, 1, 0) + dot(lo, place, 1, 0)
    for a, x in itertools.product(range(3), range(8)):
        tile = out[0][64 * a + 8 * x : 64 * a + 8 * x + 8]
        if x < 5:
            tile = tile + out[-1][40 * a + 8 * x : 40 * a + 8 * x + 8]
        if x >= 3:
            tile = tile + out[1][40 * a + 8 * x - 24 : 40 * a + 8 * x - 16]
        force[a, x] = tile


SIDES = (-1, 0, 1)
X0 = {-1: 0, 0: 4, 1: 10}


def spans(sx):
    return range(6) if sx == 0 else range(4)


def assemble(recv, vel, ext, lane, sub):
    low4 = (lane & 7) < 4
    above_rows = bits(sub, (0, 1))
    for sx in SIDES:
        xs = spans(sx)
        side = face_tiles(recv, WHERE[-sx, 0, 0][2]["U"], sub) if sx else None
        above, below = WHERE[-sx, -1, 0][2]["U"], WHERE[-sx, 1, 0][2]["U"]
        for a, x in itertools.product(range(3), xs):
            own = side[4 * a + x] if sx else vel[a, x]
            t = 8 * (a * (len(xs) // 2) + x // 2)
            up = recv[above + t : above + t + 8, :]
            dn = recv[below + t : below + t + 8, :]
            if x % 2:
                up, dn = roll(up, 4, 0), roll(dn, 4, 0)
            ext[a, X0[sx] + x, 0:8, 0:128] = jnp.where(sub < 6, own, up)
            ext[a, X0[sx] + x, 8:16, 0:128] = jnp.where(above_rows, up, jnp.where(sub >= 4, dn, 0.0))

        def merged(sy, t):
            lower = WHERE[-sx, -sy, 1][2]["Z"] + 8 * t
            upper = WHERE[-sx, -sy, -1][2]["Z"] + 8 * t
            return jnp.where(low4, recv[lower : lower + 8, :], recv[upper : upper + 8, :])

        count = 3 * len(xs)
        for t in range((count + 15) // 16):
            slots = range(16 * t, min(16 * t + 16, count))
            m_up, m_dn = roll(merged(1, t), 6, 0), roll(merged(-1, t), 2, 0)
            m_own = merged(0, t + 3 if sx == 0 else t)
            inner = jnp.where(sub < 6, m_own, m_up)
            second = jnp.where(above_rows, m_up, jnp.where(sub >= 4, m_dn, 0.0))
            for s in slots:
                a, x = s // len(xs), s % len(xs)
                ext[a, X0[sx] + x, 0:8, 128:256] = unpack(inner, s)
                ext[a, X0[sx] + x, 8:16, 128:256] = unpack(second, s)


def prepare(base_s, off_s, wxy, w_hi, w_lo):
    base, frac = base_s[...], off_s[...]
    four = [four_weights(frac, a) for a in range(3)]
    n = iota((16, 1), 0)
    wxy[0:16, :] = node_weights(n - 4, base[0:1], four[0])
    wxy[16:32, :] = node_weights(jnp.where(n < 10, n, n - 16), base[1:2], four[1])
    w_hi[...] = jnp.zeros(w_hi.shape, BF16)
    w_lo[...] = jnp.zeros(w_lo.shape, BF16)
    for begin, rows, shift in ((0, 144, 0), (240, 16, 256)):
        hi, lo = halves(node_weights(iota((rows, 1), 0) + (begin - shift), base[2:3], four[2]))
        w_hi[begin : begin + rows, :] = hi
        w_lo[begin : begin + rows, :] = lo


def interpolate(ext, wxy, w_hi, w_lo, alive, out):
    wy = wxy[16:32, :]
    for a in range(3):
        e_hi, e_lo = halves(ext[a].reshape(14 * 16, 256))
        p = dot(e_hi, w_hi[...], 1, 0) + dot(e_lo, w_hi[...], 1, 0) + dot(e_hi, w_lo[...], 1, 0)
        total = jnp.zeros((16, VP), F32)
        for x in range(14):
            total = total + p[16 * x : 16 * x + 16] * wxy[x : x + 1, :]
        row = jnp.sum(total * wy, axis=0, keepdims=True) * alive
        out[a] = row[:, 0:NV]


def step_nodes(col, recv, ext, force, raw, moved, ends, nxt, lane, sub):
    wall = jnp.full((8, 128), jnp.nan, F32)
    low4 = (lane & 7) < 4
    side = jnp.where(lane[0:1] >= 64, 1.0, -1.0)

    def shifts(cz):
        edge = ((cz > 0.5) & (lane == 127)) | ((cz < -0.5) & (lane == 0))

        def move(s, z):
            a = jnp.where(edge, z, s)
            return jnp.where(cz > 0.5, roll(a, 1, 1), jnp.where(cz < -0.5, roll(a, 127, 1), a))

        return move

    cs = [constants(sub, natural_numbers(k)) for k in range(3)]
    movers = [shifts(c[2]) for c in cs]
    c_up, c_down = [constants(sub, [rows.get(r) for r in range(8)]) for rows in (UP, DOWN)]
    c_end = [jnp.where(lane >= 64, a, b) for a, b in zip(c_up, c_down)]
    z_low = WHERE[0, 0, 1][2]["Z"]
    z_high = WHERE[0, 0, -1][2]["Z"]
    for t in range(3):
        merged = jnp.where(low4, recv[z_low + 8 * t : z_low + 8 * t + 8, :], recv[z_high + 8 * t : z_high + 8 * t + 8, :])
        for s in range(16):
            ends[16 * t + s] = unpack(merged, s)

    def own_columns(x, carry):
        for y in range(BY):
            i = x * BY + y
            rho, flag = col[i, RHO : RHO + 1, :], col[i, FLAG : FLAG + 1, :]
            u = [col[i, VEL + a : VEL + a + 1, :] for a in range(3)]
            f = [force[a, x + 1, y : y + 1, 0:128] for a in range(3)]
            fz = [force[a, x + 1, y : y + 1, 128:256] for a in range(3)]
            uz = [ext[a, x + 4, y : y + 1, 128:256] for a in range(3)]
            rho_z, flag_z = ends[36 + x, y : y + 1, :], ends[42 + x, y : y + 1, :]
            rz = collide(ends[i], c_end, rho_z, uz, fz)
            sz = jnp.where(flag_z > 0.5, rz, wall)
            for k in range(3):
                r = collide(col[i, 8 * k : 8 * k + 8, :], cs[k], rho, u, f)
                raw[i, 8 * k : 8 * k + 8, :] = r
                s = jnp.where(flag > 0.5, r, wall)
                moved[x + 1, y + 1, 8 * k : 8 * k + 8, :] = movers[k](s, sz)
        return carry

    for x in range(BX):
        own_columns(x, 0)

    for face, (rows, r_rho, r_flag) in FACE.items():
        dx, dy = face
        numbers = [rows.get(r) for r in range(8)]
        c = constants(sub, numbers)
        mover = shifts(c[2])
        ring = WHERE[dx, dy, 0][2]["R"]
        count = 1 if dx and dy else 6
        if count == 6:
            if dx:
                z = [WHERE[dx, 0, s][2]["Z"] for s in (1, -1)]
                slot = 12
            else:
                z = [WHERE[0, dy, s][2]["Z"] + 8 for s in (1, -1)]
                slot = 2
            pz = jnp.where(low4, recv[z[0] : z[0] + 8, :], recv[z[1] : z[1] + 8, :])
            tz = [unpack(pz, slot + t) for t in range(3)]
            cz = (float(dx), float(dy), side, 1.0 / 36.0)
        for j in range(count):
            x = {1: -1, -1: 6, 0: j}[dx]
            y = {1: -1, -1: 6, 0: j}[dy]
            t = recv[ring + 8 * j : ring + 8 * j + 8, :]
            rho, flag = t[r_rho : r_rho + 1], t[r_flag : r_flag + 1]
            yu, yf = y % 16, y % 8
            if count == 6:
                u = [ext[a, x + 4, yu : yu + 1, 0:128] for a in range(3)]
            else:
                u = [t[EDGE_VEL + a : EDGE_VEL + a + 1] for a in range(3)]
            f = [force[a, x + 1, yf : yf + 1, 0:128] for a in range(3)]
            s = jnp.where(flag > 0.5, collide(t, c, rho, u, f), wall)
            if count == 6:
                uz = [ext[a, x + 4, yu : yu + 1, 128:256] for a in range(3)]
                fz = [force[a, x + 1, yf : yf + 1, 128:256] for a in range(3)]
                rz = collide(tz[0][j : j + 1], cz, tz[1][j : j + 1], uz, fz)
                sz = jnp.where(tz[2][j : j + 1] > 0.5, rz, wall[0:1])
                s = mover(s, sz)
            for k in sorted({q // 8 for q in rows.values()}):
                out = None
                for shift in sorted({(q - r) % 8 for r, q in rows.items() if q // 8 == k}):
                    tile = roll(s, shift, 0)
                    members = [q % 8 for r, q in rows.items() if q // 8 == k and (q - r) % 8 == shift]
                    out = tile if out is None else jnp.where(bits(sub, members), tile, out)
                moved[x + 1, y + 1, 8 * k : 8 * k + 8, :] = out

    odd = (iota((24, 128), 0) & 1) == 1
    start = iota((24, 128), 0) == 0

    def passing(x, carry):
        for y in range(BY):
            i = x * BY + y
            r = raw[i]
            turned = jnp.where(start, r, jnp.where(odd, roll(r, 23, 0), roll(r, 1, 0)))
            for k in range(3):
                sources = {}
                for q in natural_numbers(k):
                    if q is not None:
                        sources.setdefault(LATTICE[q][:2], []).append(q % 8)
                out = None
                for (cx, cy), members in sources.items():
                    tile = moved[x + 1 - cx, y + 1 - cy, 8 * k : 8 * k + 8, :]
                    out = tile if out is None else jnp.where(bits(sub, members), tile, out)
                out = jnp.where(out == out, out, turned[8 * k : 8 * k + 8])
                last = min(8 * k + 8, 19)
                nxt[i, 8 * k : last, :] = out[0 : last - 8 * k]
        return carry

    for x in range(BX):
        passing(x, 0)


def finish(col, vel, ownf, recv, wxy, w_hi, w_lo, occ, nxt, vtx, ext, force, raw, moved, ends):
    lane = iota((8, 128), 1)
    sub = iota((8, 128), 0)
    alive = (occ[...] > 0).astype(F32)
    assemble(recv, vel, ext, lane, sub)
    forces(recv, ownf, force)
    step_nodes(col, recv, ext, force, raw, moved, ends, nxt, lane, sub)
    interpolate(ext, wxy, w_hi, w_lo, alive, vtx)


def on_device(sizes, populations, fluid_mask, stencil_base, offsets, occupied_cell_slots, triangles):
    pops = jnp.transpose(populations, (1, 2, 0, 3)).reshape(BX * BY, 19, BZ)
    base = stencil_base.reshape(3, 1, NV)
    off = offsets.reshape(3, 1, NV)
    occ = occupied_cell_slots.reshape(1, 1)
    vmem = pl.BlockSpec(memory_space=pltpu.VMEM)
    hbm = pl.BlockSpec(memory_space=pltpu.HBM)
    shape = jax.ShapeDtypeStruct
    dma = pltpu.SemaphoreType.DMA
    vm = pltpu.VMEM
    middle = pl.pallas_call(
        functools.partial(send_all, sizes),
        name="cells_and_halo",
        out_shape=(
            shape((36, 24, 128), F32),
            shape((3, 6, 8, 128), F32),
            shape((32, 128), F32),
            shape((ROWS, 128), F32),
            shape((32, VP), F32),
            shape((256, VP), BF16),
            shape((256, VP), BF16),
        ),
        in_specs=[hbm, hbm, hbm, hbm, vmem, hbm],
        out_specs=(vmem,) * 7,
        scratch_shapes=[
            vm((ROWS, 128), F32),
            vm((6, 8, 128), I32),
            vm((3, 1, NV), I32),
            vm((3, 1, NV), F32),
            vm((3, NT), I32),
            vm((8, VP), I32),
            vm((8, VP), F32),
            vm((VP, NT), BF16),
            vm((384, VP), F32),
            vm((192, VP), F32),
            vm((24, 128), F32),
            vm((6, 8, 128), F32),
            dma((5,)),
            dma((26,)),
            dma((26,)),
            dma((26,)),
            dma((26,)),
        ],
        compiler_params=pltpu.CompilerParams(collective_id=0, has_side_effects=True, vmem_limit_bytes=48 << 20),
    )(*(pltpu.with_memory_space_constraint(a, pltpu.HBM) for a in (pops, fluid_mask, base, off)), occ, pltpu.with_memory_space_constraint(triangles.T, pltpu.HBM))
    nxt, vtx = pl.pallas_call(
        finish,
        name="collide_and_pass",
        out_shape=(shape((36, 19, 128), F32), shape((3, 1, NV), F32)),
        in_specs=[vmem] * 8,
        out_specs=(vmem, vmem),
        scratch_shapes=[
            vm((3, 14, 16, 256), F32),
            vm((3, 8, 8, 256), F32),
            vm((36, 24, 128), F32),
            vm((8, 8, 24, 128), F32),
            vm((48, 8, 128), F32),
        ],
        compiler_params=pltpu.CompilerParams(vmem_limit_bytes=48 << 20),
    )(*middle, occ)
    nxt = jnp.transpose(nxt.reshape(BX, BY, 19, BZ), (2, 0, 1, 3))
    return nxt, vtx.reshape(1, 1, 1, 3, NV)


def solution(mesh):
    sizes = tuple(mesh.shape[a] for a in AXES)
    placed = (
        P(None, "gx", "gy", "gz"),
        P("gx", "gy", "gz"),
        P("gx", "gy", "gz", None, None),
        P("gx", "gy", "gz", None, None),
        P("gx", "gy", "gz"),
        P(),
    )
    return jax.shard_map(
        functools.partial(on_device, sizes),
        mesh=mesh,
        in_specs=placed,
        out_specs=(P(None, "gx", "gy", "gz"), P("gx", "gy", "gz", None, None)),
        check_vma=False,
    )
```

```python
import functools
import itertools
import math

import jax
import jax.numpy as jnp
from jax import lax
from jax.experimental import pallas as pl
from jax.experimental.pallas import tpu as pltpu
from jax.sharding import PartitionSpec as P

MESH = pl.DeviceIdType.MESH
AXES = ("gx", "gy", "gz")
NV = 642
VP = 768
NT = 1280
BX, BY, BZ = 6, 6, 128
F32, BF16, I32 = jnp.float32, jnp.bfloat16, jnp.int32
FAR = -10000
STIFFNESS, REST, TAU = 0.1, 4.0, 0.8

LATTICE = (
    (0, 0, 0),
    (1, 0, 0),
    (-1, 0, 0),
    (0, 1, 0),
    (0, -1, 0),
    (0, 0, 1),
    (0, 0, -1),
    (1, 1, 0),
    (-1, -1, 0),
    (1, -1, 0),
    (-1, 1, 0),
    (1, 0, 1),
    (-1, 0, -1),
    (1, 0, -1),
    (-1, 0, 1),
    (0, 1, 1),
    (0, -1, -1),
    (0, 1, -1),
    (0, -1, 1),
)
WEIGHT = [1.0 / 3.0] + [1.0 / 18.0] * 6 + [1.0 / 36.0] * 12
NUMBER = {c: q for q, c in enumerate(LATTICE)}

RHO, FLAG, VEL = 19, 20, 21

FACE = {
    (1, 0): ({1: 1, 7: 7, 3: 11, 5: 13, 2: 9}, 0, 4),
    (-1, 0): ({2: 2, 0: 8, 4: 12, 6: 14, 3: 10}, 1, 5),
    (0, 1): ({3: 3, 7: 7, 2: 10, 1: 17, 0: 15}, 4, 5),
    (0, -1): ({4: 4, 0: 8, 1: 9, 2: 18, 3: 16}, 5, 6),
    (1, 1): ({7: 7}, 0, 1),
    (1, -1): ({1: 9}, 0, 2),
    (-1, 1): ({2: 10}, 0, 1),
    (-1, -1): ({0: 8}, 1, 2),
}
UP = {5: 5, 3: 11, 6: 14, 7: 15, 2: 18}
DOWN = {6: 6, 4: 12, 5: 13, 0: 16, 1: 17}
EDGE_VEL = 3
TRAVELS = [d for d in itertools.product((-1, 0, 1), repeat=3) if d != (0, 0, 0)]
TRAVELS.sort(key=lambda d: (d[0] == 0, d[2] != 0, d[1] != 0))


def layout():
    where, row = {}, 0
    for d in TRAVELS:
        dx, dy, dz = d
        rows = {}
        if dx and dy and dz == 0:
            rows["R"] = 8
        if dx and dz:
            rows["Z"] = 8
        rows["F"] = (16 if dz == 0 else 8) * (2 if dx == 0 else 1)
        if dz == 0:
            if not (dx and dy):
                rows["R"] = 48
            rows["U"] = 48 if dx and dy else 72
        elif dx == 0:
            rows["Z"] = 16 if dy else 40
        spot, begin = {}, row
        for part, count in rows.items():
            spot[part] = row
            row += count
        where[d] = (begin, row - begin, spot)
    return where, row


WHERE, ROWS = layout()
USED = {16: 11, 8: 5}


def iota(shape, axis):
    return lax.broadcasted_iota(I32, shape, axis)


def bits(index, members):
    code = sum(1 << m for m in members)
    return (lax.shift_right_logical(jnp.full(index.shape, code, I32), index) & 1) == 1


def per_row(sub, values):
    out = jnp.zeros(sub.shape, F32)
    for value in sorted(set(values)):
        if value != 0:
            members = [r for r, v in enumerate(values) if v == value]
            out = jnp.where(bits(sub, members), F32(value), out)
    return out


def constants(sub, numbers):
    rows = [[0 if q is None else LATTICE[q][a] for q in numbers] for a in range(3)]
    rows.append([0 if q is None else WEIGHT[q] for q in numbers])
    return [per_row(sub, r) for r in rows]


def natural_numbers(k):
    return [q if q < 19 else None for q in range(8 * k, 8 * k + 8)]


def sin_half_pi(f):
    t = f * (0.5 * math.pi)
    t2 = t * t
    out = jnp.full(f.shape, 1.0 / math.factorial(13), F32)
    for k in (11, 9, 7, 5, 3, 1):
        sign = 1.0 if (13 - k) // 2 % 2 == 0 else -1.0
        out = out * t2 + sign / math.factorial(k)
    return out * t


def node_weights(n, base, four):
    d = n - base
    out = jnp.where(d == 3, four[3], 0.0)
    for k in (2, 1, 0):
        out = jnp.where(d == k, four[k], out)
    return out


def four_weights(frac, axis):
    s = sin_half_pi(frac)[axis : axis + 1]
    c = sin_half_pi(1.0 - frac)[axis : axis + 1]
    return [0.25 * (1.0 - s), 0.25 * (1.0 + c), 0.25 * (1.0 + s), 0.25 * (1.0 - c)]


def halves(x):
    hi = x.astype(BF16)
    return hi, (x - hi.astype(F32)).astype(BF16)


def thirds(x):
    hi = x.astype(BF16)
    rest = x - hi.astype(F32)
    mid = rest.astype(BF16)
    return jnp.concatenate([hi, mid, (rest - mid.astype(F32)).astype(BF16)], axis=0)


def dot(a, b, ca, cb):
    return lax.dot_general(a, b, (((ca,), (cb,)), ((), ())), preferred_element_type=F32)


def load_vertices(base, off, base_s, off_s):
    base_s[...] = jnp.full((8, VP), FAR, I32)
    off_s[...] = jnp.zeros((8, VP), F32)
    for a in range(3):
        base_s[a : a + 1, 0:NV] = base[a]
        off_s[a : a + 1, 0:NV] = off[a]


def turn(t, sub):
    one = jnp.where(sub == 2, roll(t, 2, 0), roll(t, 7, 0))
    two = jnp.where(sub == 0, roll(t, 6, 0), roll(t, 1, 0))
    return one, two


def incidence_of(tri, incidence):
    vertex = iota((16, NT), 0).astype(jnp.int16)
    one, none = jnp.ones((16, NT), BF16), jnp.zeros((16, NT), BF16)

    def fill(step, carry):
        rows = pl.multiple_of(step * 16, 16)
        t = [jnp.broadcast_to(tri[a : a + 1] - rows, (16, NT)).astype(jnp.int16) for a in range(3)]
        hit = (vertex == t[0]) | (vertex == t[1]) | (vertex == t[2])
        incidence[pl.ds(rows, 16), :] = jnp.where(hit, one, none)
        return carry

    lax.fori_loop(0, 41, fill, 0)
    incidence[656:VP, :] = jnp.zeros((VP - 656, NT), BF16)


def membrane(base_s, off_s, alive, incidence):
    sub = iota((8, VP), 0)
    base = base_s[...]
    x = jnp.where((base > FAR // 2) & (sub < 3), (base - base[:, 0:1]).astype(F32) + off_s[...], 0.0)
    x1, x2 = turn(x, sub)
    xx = x * x
    r2 = xx + x1 * x1 + x2 * x2
    first = (r2 - REST * REST) * x + jnp.where(sub == 3, 1.0, 0.0) + roll(x, 4, 0)
    second = xx + roll(x * x1, 4, 0)
    sums = dot(thirds(jnp.concatenate([first, second], axis=0)), incidence[...], 1, 0)
    sums = sums[0:16] + sums[16:32] + sums[32:48]
    back = dot(thirds(sums), incidence[...], 1, 1)
    back = back[0:16] + back[16:32] + back[32:48]
    cubic, diag = back[0:8], back[8:16]
    count = cubic[3:4]
    lin, cross = roll(cubic, 4, 0), roll(diag, 4, 0)
    turned = diag * x + cross * x1 + turn(cross, sub)[1] * x2
    along, trace = x * lin, jnp.where(sub < 3, diag, 0.0)
    along = along + sum(turn(along, sub))
    trace = trace + sum(turn(trace, sub))
    common = 2.0 * along - r2 * count - (trace - REST * REST * count)
    total = cubic - 2.0 * turned + r2 * lin + x * common
    return (STIFFNESS / (REST * REST)) * alive * total


YN = {0: (0, 1, 2, 3, 4, 5, 6, -1), 1: (6, 7, 8, 9, 10, 11, 12, 5), -1: (-6, -5, -4, -3, -2, -1, 0, -7)}
DYS = (0, 1, -1)


def spread_own(base_s, off_s, loads, outer, mid):
    base, frac = base_s[...], off_s[...]
    four = [four_weights(frac, a) for a in range(3)]
    low = jnp.min(jnp.where(base[2:3] > FAR // 2, base[2:3], 1 << 20), axis=1, keepdims=True)
    k = iota((32, 1), 0)
    z = jnp.where(k < 16, low + k, jnp.where(k < 24, 127 - 16 + k, -4 - 24 + k))
    wz = node_weights(z, base[2:3], four[2])
    left = jnp.concatenate([wz * loads[c : c + 1] for c in range(3)], axis=0)
    wx = node_weights(iota((16, 1), 0) - 4, base[0:1], four[0])
    row8 = iota((8, 1), 0)
    for i, dy in enumerate(DYS):
        n = jnp.where(row8 == 7, YN[dy][7], row8 + YN[dy][0])
        wy = node_weights(n, base[1:2], four[1])
        for j in range(5):
            outer[i * 128 + j * 8 : i * 128 + j * 8 + 8, :] = wx[9 + j : 10 + j] * wy
            outer[i * 128 + 40 + j * 8 : i * 128 + 48 + j * 8, :] = wx[j : j + 1] * wy
        outer[i * 128 + 80 : i * 128 + 128, :] = jnp.zeros((48, VP), F32)
        for j in range(8):
            mid[i * 64 + j * 8 : i * 64 + j * 8 + 8, :] = wx[3 + j : 4 + j] * wy
    l_hi, l_lo = halves(left)
    both = jnp.concatenate([l_hi, l_lo], axis=0)

    def product(ref):
        r_hi, r_lo = halves(ref[...])
        out = dot(both, r_hi, 1, 1)
        return out[0:96] + out[96:192] + dot(l_hi, r_lo, 1, 1)

    return product(outer), product(mid), z[0:16].astype(F32)


def roll(x, shift, axis):
    shift = shift % x.shape[axis]
    return x if shift == 0 else pltpu.roll(x, shift, axis)


def force_pieces(outer, mid, z16, lane, dx, dy, dz, put):
    k0, kn = {0: (0, 16), 1: (16, 8), -1: (24, 8)}[dz]
    i = DYS.index(dy)
    lane = iota((kn, 128), 1)
    if dx:
        off = 0 if dx == 1 else 40
        out = jnp.zeros((kn, 128), F32)
        for c in range(3):
            tile = outer[32 * c + k0 : 32 * c + k0 + kn, i * 128 : i * 128 + 128]
            tile = roll(tile, 40 * c - off, 1)
            out = jnp.where((lane >= 40 * c) & (lane < 40 * c + 40), tile, out)
        if dz == 0:
            out = jnp.where(lane >= 120, z16, out)
        put(0, out)
        return
    tiles = []
    for c in range(3):
        t = i // 2 * 128
        tile = mid[32 * c + k0 : 32 * c + k0 + kn, t : t + (128 if i < 2 else 64)]
        if i == 2:
            tile = jnp.concatenate([tile, jnp.zeros((kn, 64), F32)], axis=1)
        tiles.append(roll(tile, 64 * (c % 2) - 64 * (i % 2), 1))
    put(0, jnp.where(lane < 64, tiles[0], tiles[1]))
    rest = z16 if dz == 0 else jnp.zeros((kn, 128), F32)
    put(kn, jnp.where(lane < 64, tiles[2], rest))


def pack(tiles, lane):
    out = jnp.zeros((8, 128), F32)
    for s, tile in enumerate(tiles):
        out = jnp.where((lane >= 8 * s) & (lane < 8 * s + 8), roll(tile, 4 + 8 * s, 1), out)
    return out


def unpack(packed, s):
    return roll(packed, -(4 + 8 * (s % 16)), 1)


def coords():
    return [lax.axis_index(a) for a in AXES]


def present_at(sizes, me, d):
    ok = None
    for m, s, size in zip(me, d, sizes):
        if s:
            here = m < size - 1 if s == 1 else m > 0
            ok = here if ok is None else jnp.logical_and(ok, here)
    return ok


def face_tiles(ref, begin, sub):
    tiles = []
    for a in range(3):
        t = [ref[begin + 8 * (3 * a + j) : begin + 8 * (3 * a + j) + 8, :] for j in range(3)]
        last = jnp.where(sub < 2, roll(t[0], 2, 0), jnp.where(sub < 4, roll(t[1], 4, 0), roll(t[2], 6, 0)))
        tiles += t + [last]
    return tiles


def paired(tiles, half, dy, sub):
    out = []
    for t in range(3 * half):
        one, two = tiles[2 * t], tiles[2 * t + 1]
        if dy == 1:
            out.append(jnp.where(sub >= 4, roll(one, 2, 0), roll(two, 6, 0)))
        else:
            out.append(jnp.where(bits(sub, (0, 1, 6, 7)), roll(one, 6, 0), roll(two, 2, 0)))
    return out


def back(d):
    return tuple(-s for s in d)


def send_all(sizes, pops, mask, base, off, occ, tri, col, vel, ownf, recv, wxy, w_hi, w_lo, send, mask_s, base_v, off_v, tri_v, base_s, off_s, incidence, outer, mid, edge_s, rho_s, in_sem, send_sem, recv_sem, fsend_sem, frecv_sem):
    me = coords()
    there = {d: present_at(sizes, me, d) for d in TRAVELS}

    def present(sizes, me, d):
        return there[d]

    ins = [(pops, col.at[:, pl.ds(0, 19), :]), (mask, mask_s.at[:, pl.ds(0, 6), :]), (base, base_v), (off, off_v), (tri, tri_v)]
    ins = [pltpu.make_async_copy(a, b, in_sem.at[k]) for k, (a, b) in enumerate(ins)]
    for copy in ins:
        copy.start()
    def at(d):
        return tuple(m + s for m, s in zip(me, d))

    barrier = pltpu.get_barrier_semaphore()
    count = jnp.int32(0)
    for d in sorted(TRAVELS, key=lambda d: d[1]):
        ok = present(sizes, me, d)
        count = count + ok.astype(I32)

        @pl.when(ok)
        def _():
            pl.semaphore_signal(barrier, inc=1, device_id=at(d), device_id_type=MESH)

    lane = iota((8, 128), 1)
    sub = iota((8, 128), 0)
    for d in TRAVELS:

        @pl.when(jnp.logical_not(present(sizes, me, back(d))))
        def _():
            begin, rows, _ = WHERE[d]
            recv[begin : begin + rows, :] = jnp.zeros((rows, 128), F32)

    cs = [constants(sub, natural_numbers(k)) for k in range(3)]
    vel[...] = jnp.zeros(vel.shape, F32)
    rho_s[...] = jnp.zeros(rho_s.shape, F32)
    for copy in ins:
        copy.wait()

    def columns(x, carry):
        for y in range(BY):
            i = x * BY + y
            col[i, 19:24, :] = jnp.zeros((5, 128), F32)
            v = [col[i, 8 * k : 8 * k + 8, :] for k in range(3)]
            rho = jnp.sum(v[0] + v[1] + v[2], axis=0, keepdims=True)
            col[i, RHO : RHO + 1, :] = rho
            rho_s[x, y : y + 1, :] = rho
            col[i, FLAG : FLAG + 1, :] = mask_s[x, y : y + 1, :].astype(F32)
            for a in range(3):
                m = v[0] * cs[0][a] + v[1] * cs[1][a] + v[2] * cs[2][a]
                u = jnp.sum(m, axis=0, keepdims=True) / rho
                col[i, VEL + a : VEL + a + 1, :] = u
                vel[a, x, y : y + 1, :] = u
        return carry

    lax.fori_loop(0, BX, columns, 0)

    def ring_tile(i, face):
        rows, r_rho, r_flag = FACE[face]
        out = jnp.where(sub == r_rho, col[i, RHO : RHO + 1, :], col[i, FLAG : FLAG + 1, :])
        moves = {}
        for r, q in rows.items():
            moves.setdefault((q // 8, (r - q) % 8), []).append(r)
        for (k, shift), members in moves.items():
            out = jnp.where(bits(sub, members), roll(col[i, 8 * k : 8 * k + 8, :], shift, 0), out)
        return out

    def ends_of(e_rows, dx, dy, column):
        up, down = NUMBER[dx, dy, 1], NUMBER[dx, dy, -1]
        edge_s[...] = jnp.zeros((24, 128), F32)
        for j in range(6):
            i = column(j)
            edge_s[j : j + 1, :] = jnp.where(lane[0:1] >= 64, col[i, up : up + 1, :], col[i, down : down + 1, :])
            edge_s[8 + j : 9 + j, :] = col[i, RHO : RHO + 1, :]
            edge_s[16 + j : 17 + j, :] = col[i, FLAG : FLAG + 1, :]
        return [edge_s[8 * t : 8 * t + 8, :] for t in range(3)]

    for dx in (1, -1):
        u, r = WHERE[dx, 0, 0][2]["U"], WHERE[dx, 0, 0][2]["R"]
        xs = range(2, 6) if dx == 1 else range(4)
        x = 5 if dx == 1 else 0
        for a, j in itertools.product(range(3), range(3)):
            t = u + 8 * (3 * a + j)
            send[t : t + 8, :] = jnp.where(sub < 6, vel[a, xs[j]], roll(vel[a, xs[3]], 6 - 2 * j, 0))
        for y in range(6):
            send[r + 8 * y : r + 8 * y + 8, :] = ring_tile(x * BY + y, (dx, 0))
    load_vertices(base_v, off_v, base_s, off_s)
    alive = (occ[...] > 0).astype(F32)
    incidence_of(tri_v, incidence)
    pl.semaphore_wait(barrier, count)

    def copy(src, dst, rows, to, sems, t):
        return pltpu.make_async_remote_copy(
            src_ref=send.at[pl.ds(src, rows)],
            dst_ref=recv.at[pl.ds(dst, rows)],
            send_sem=sems[0].at[t],
            recv_sem=sems[1].at[t],
            device_id=at(to),
            device_id_type=MESH,
        )

    faces = [d for d in TRAVELS if sum(map(abs, d)) == 1]
    edges = [d for d in TRAVELS if d[0] and d[1] and d[2] == 0]


    def fields(d):
        dx, dy, dz = d
        begin, rows, spot = WHERE[d]
        t = TRAVELS.index(d)
        if d in edges:
            return copy(spot["U"], spot["U"], 48, (0, dy, 0), (send_sem, recv_sem), t)
        row = spot["Z"] if dz else spot["R"]
        src = WHERE[0, 0, 1][2]["Z"] if dz else row
        return copy(src, row, begin + rows - row, d, (send_sem, recv_sem), t)

    def force_copy(d):
        begin, rows, spot = WHERE[d]
        if d[0]:
            rows = spot["F"] - begin + USED[8 if d[2] else 16]
        elif d in faces:
            rows = spot["Z" if d[2] else "R"] - begin
        return copy(begin, begin, rows, d, (fsend_sem, frecv_sem), TRAVELS.index(d))

    for d in faces:
        if d[0]:

            @pl.when(present(sizes, me, d))
            def _():
                fields(d).start()

    us = [vel[a, x] for a in range(3) for x in range(6)]
    first = pack(us[:16], lane)
    for dx in (1, -1):
        xs = range(2, 6) if dx == 1 else range(4)
        x = 5 if dx == 1 else 0
        tiles = [vel[a, k] for a in range(3) for k in xs] + ends_of(edge_s, dx, 0, lambda j: x * BY + j)
        packed = pack(tiles, lane)
        for dy, dz in itertools.product((0, 1, -1), (1, -1)):
            z = WHERE[dx, dy, dz][2]["Z"]
            send[z : z + 8, :] = packed
        for dy in (1, -1):
            r = WHERE[dx, dy, 0][2]["R"]
            i = x * BY + (5 if dy == 1 else 0)
            send[r : r + 8, :] = ring_tile(i, (dx, dy))
            send[r + EDGE_VEL : r + EDGE_VEL + 3, :] = col[i, VEL : VEL + 3, :]
    for dy in (1, -1):
        u, r = WHERE[0, dy, 0][2]["U"], WHERE[0, dy, 0][2]["R"]
        y = 5 if dy == 1 else 0
        for t, tile in enumerate(paired(us, 3, dy, sub)):
            send[u + 8 * t : u + 8 * t + 8, :] = tile
        for x in range(6):
            send[r + 8 * x : r + 8 * x + 8, :] = ring_tile(x * BY + y, (0, dy))
        second = pack(us[16:] + ends_of(edge_s, 0, dy, lambda j: j * BY + y), lane)
        for dz in (1, -1):
            z = WHERE[0, dy, dz][2]["Z"]
            send[z : z + 8, :] = first
            send[z + 8 : z + 16, :] = second
    z = WHERE[0, 0, 1][2]["Z"]
    pick = []
    for k in range(2):
        ups = [r for r, q in UP.items() if q // 8 == k]
        downs = [r for r, q in DOWN.items() if q // 8 == k]
        pick.append(((lane >= 64) & bits(sub, ups)) | ((lane < 64) & bits(sub, downs)))
    tiles = []
    for i in range(BX * BY):
        v = [col[i, 8 * k : 8 * k + 8, :] for k in range(3)]
        tiles.append(jnp.where(pick[0], v[0], jnp.where(pick[1], v[1], v[2])))
    tiles += [rho_s[x] for x in range(6)] + [mask_s[x].astype(F32) for x in range(6)] + us
    for t in range(5):
        send[z + 8 * t : z + 8 * t + 8, :] = pack(tiles[16 * t : 16 * t + 16], lane)

    for d in faces:
        if d[0] == 0:

            @pl.when(present(sizes, me, d))
            def _():
                fields(d).start()

    loads = membrane(base_s, off_s, alive, incidence)
    f_outer, f_mid, z16 = spread_own(base_s, off_s, loads, outer, mid)

    def own_put(k, tile):
        ownf[k : k + tile.shape[0], :] = tile

    force_pieces(f_outer, f_mid, z16, lane, 0, 0, 0, own_put)
    for d in TRAVELS:

        def put(k, tile, f=WHERE[d][2]["F"]):
            send[f + k : f + k + tile.shape[0], :] = tile

        force_pieces(f_outer, f_mid, z16, lane, *d, put)
    for d in TRAVELS:

        @pl.when(present(sizes, me, d))
        def _():
            force_copy(d).start()

    prepare(base_s, off_s, wxy, w_hi, w_lo)

    def forward(dx):
        @pl.when(present(sizes, me, (-dx, 0, 0)))
        def _():
            fields((dx, 0, 0)).wait_recv()
            tiles = face_tiles(recv, WHERE[dx, 0, 0][2]["U"], sub)
            for dy in (1, -1):
                u = WHERE[dx, dy, 0][2]["U"]
                for t, tile in enumerate(paired(tiles, 2, dy, sub)):
                    send[u + 8 * t : u + 8 * t + 8, :] = tile

                @pl.when(present(sizes, me, (-dx, dy, 0)))
                def _():
                    fields((dx, dy, 0)).start()

    low_half = me[0] < sizes[0] // 2

    @pl.when(low_half)
    def _():
        forward(1)
        forward(-1)

    @pl.when(jnp.logical_not(low_half))
    def _():
        forward(-1)
        forward(1)

    for d in TRAVELS:

        @pl.when(present(sizes, me, back(d)))
        def _():
            force_copy(d).wait_recv()
            if d in edges or (d in faces and d[0] == 0):
                fields(d).wait_recv()

    for d in TRAVELS:

        @pl.when(present(sizes, me, d))
        def _():
            force_copy(d).wait_send()
            if d in faces:
                fields(d).wait_send()

        if d in edges:

            @pl.when(present(sizes, me, (-d[0], d[1], 0)))
            def _():
                fields(d).wait_send()


def collide(p, c, rho, u, f):
    inv = 0.5 / rho
    v = [a + inv * b for a, b in zip(u, f)]
    vv = v[0] * v[0] + v[1] * v[1] + v[2] * v[2]
    vf = v[0] * f[0] + v[1] * f[1] + v[2] * f[2]
    factor = 1.0 - 0.5 / TAU
    a0 = (1.0 / TAU) * rho * (1.0 - 1.5 * vv) - (3.0 * factor) * vf
    a1 = (3.0 / TAU) * rho
    a2 = (4.5 / TAU) * rho
    cx, cy, cz, w = c
    pr = cx * v[0] + cy * v[1] + cz * v[2]
    cf = cx * f[0] + cy * f[1] + cz * f[2]
    poly = a0 + pr * (a1 + a2 * pr) + cf * (3.0 * factor + (9.0 * factor) * pr)
    return (1.0 - 1.0 / TAU) * p + w * poly


def forces(recv, ownf, force):
    zl = iota((1, 256), 1)
    zl = jnp.where(zl < 132, zl, jnp.where(zl >= 252, zl - 256, -5000)).astype(F32)
    k8 = iota((8, 1), 0).astype(F32)
    out = {}
    for sx in (-1, 0, 1):
        parts, zs = [], []
        for sy, sz in itertools.product((-1, 0, 1), (0, -1, 1)):
            kn = 8 if sz else 16
            if (sx, sy, sz) == (0, 0, 0):
                ref, f = ownf, 0
            else:
                ref, f = recv, WHERE[-sx, -sy, -sz][2]["F"]
            tile = ref[f : f + kn, :]
            if sx == 0:
                tile = jnp.concatenate([tile, ref[f + kn : f + 2 * kn, :]], axis=1)
            else:
                tile = jnp.where(iota((kn, 128), 0) < USED[kn], tile, 0.0)
            parts.append(tile)
            if sz == 0:
                zs.append(tile[:, 120:121] if sx else tile[:, 192:193])
            else:
                zs.append(k8 + (-1.0 if sz == -1 else 124.0))
        g = jnp.concatenate(parts, axis=0)
        z = jnp.concatenate(zs, axis=0)
        place = jnp.where(z == zl, 1.0, 0.0).astype(BF16)
        hi, lo = halves(g.T)
        out[sx] = dot(hi, place, 1, 0) + dot(lo, place, 1, 0)
    for a, x in itertools.product(range(3), range(8)):
        tile = out[0][64 * a + 8 * x : 64 * a + 8 * x + 8]
        if x < 5:
            tile = tile + out[-1][40 * a + 8 * x : 40 * a + 8 * x + 8]
        if x >= 3:
            tile = tile + out[1][40 * a + 8 * x - 24 : 40 * a + 8 * x - 16]
        force[a, x] = tile


SIDES = (-1, 0, 1)
X0 = {-1: 0, 0: 4, 1: 10}


def spans(sx):
    return range(6) if sx == 0 else range(4)


def assemble(recv, vel, ext, lane, sub):
    low4 = (lane & 7) < 4
    above_rows = bits(sub, (0, 1))
    for sx in SIDES:
        xs = spans(sx)
        side = face_tiles(recv, WHERE[-sx, 0, 0][2]["U"], sub) if sx else None
        above, below = WHERE[-sx, -1, 0][2]["U"], WHERE[-sx, 1, 0][2]["U"]
        for a, x in itertools.product(range(3), xs):
            own = side[4 * a + x] if sx else vel[a, x]
            t = 8 * (a * (len(xs) // 2) + x // 2)
            up = recv[above + t : above + t + 8, :]
            dn = recv[below + t : below + t + 8, :]
            if x % 2:
                up, dn = roll(up, 4, 0), roll(dn, 4, 0)
            ext[a, X0[sx] + x, 0:8, 0:128] = jnp.where(sub < 6, own, up)
            ext[a, X0[sx] + x, 8:16, 0:128] = jnp.where(above_rows, up, jnp.where(sub >= 4, dn, 0.0))

        def merged(sy, t):
            lower = WHERE[-sx, -sy, 1][2]["Z"] + 8 * t
            upper = WHERE[-sx, -sy, -1][2]["Z"] + 8 * t
            return jnp.where(low4, recv[lower : lower + 8, :], recv[upper : upper + 8, :])

        count = 3 * len(xs)
        for t in range((count + 15) // 16):
            slots = range(16 * t, min(16 * t + 16, count))
            m_up, m_dn = roll(merged(1, t), 6, 0), roll(merged(-1, t), 2, 0)
            m_own = merged(0, t + 3 if sx == 0 else t)
            inner = jnp.where(sub < 6, m_own, m_up)
            second = jnp.where(above_rows, m_up, jnp.where(sub >= 4, m_dn, 0.0))
            for s in slots:
                a, x = s // len(xs), s % len(xs)
                ext[a, X0[sx] + x, 0:8, 128:256] = unpack(inner, s)
                ext[a, X0[sx] + x, 8:16, 128:256] = unpack(second, s)


def prepare(base_s, off_s, wxy, w_hi, w_lo):
    base, frac = base_s[...], off_s[...]
    four = [four_weights(frac, a) for a in range(3)]
    n = iota((16, 1), 0)
    wxy[0:16, :] = node_weights(n - 4, base[0:1], four[0])
    wxy[16:32, :] = node_weights(jnp.where(n < 10, n, n - 16), base[1:2], four[1])
    w_hi[...] = jnp.zeros(w_hi.shape, BF16)
    w_lo[...] = jnp.zeros(w_lo.shape, BF16)
    for begin, rows, shift in ((0, 144, 0), (240, 16, 256)):
        hi, lo = halves(node_weights(iota((rows, 1), 0) + (begin - shift), base[2:3], four[2]))
        w_hi[begin : begin + rows, :] = hi
        w_lo[begin : begin + rows, :] = lo


def interpolate(ext, wxy, w_hi, w_lo, alive, out):
    wy = wxy[16:32, :]
    for a in range(3):
        e_hi, e_lo = halves(ext[a].reshape(14 * 16, 256))
        p = dot(e_hi, w_hi[...], 1, 0) + dot(e_lo, w_hi[...], 1, 0) + dot(e_hi, w_lo[...], 1, 0)
        total = jnp.zeros((16, VP), F32)
        for x in range(14):
            total = total + p[16 * x : 16 * x + 16] * wxy[x : x + 1, :]
        row = jnp.sum(total * wy, axis=0, keepdims=True) * alive
        out[a] = row[:, 0:NV]


def step_nodes(col, recv, ext, force, raw, moved, ends, nxt, lane, sub):
    wall = jnp.full((8, 128), jnp.nan, F32)
    low4 = (lane & 7) < 4
    side = jnp.where(lane[0:1] >= 64, 1.0, -1.0)

    def shifts(cz):
        edge = ((cz > 0.5) & (lane == 127)) | ((cz < -0.5) & (lane == 0))

        def move(s, z):
            a = jnp.where(edge, z, s)
            return jnp.where(cz > 0.5, roll(a, 1, 1), jnp.where(cz < -0.5, roll(a, 127, 1), a))

        return move

    cs = [constants(sub, natural_numbers(k)) for k in range(3)]
    movers = [shifts(c[2]) for c in cs]
    c_up, c_down = [constants(sub, [rows.get(r) for r in range(8)]) for rows in (UP, DOWN)]
    c_end = [jnp.where(lane >= 64, a, b) for a, b in zip(c_up, c_down)]
    z_low = WHERE[0, 0, 1][2]["Z"]
    z_high = WHERE[0, 0, -1][2]["Z"]
    for t in range(3):
        merged = jnp.where(low4, recv[z_low + 8 * t : z_low + 8 * t + 8, :], recv[z_high + 8 * t : z_high + 8 * t + 8, :])
        for s in range(16):
            ends[16 * t + s] = unpack(merged, s)

    def own_columns(x, carry):
        for y in range(BY):
            i = x * BY + y
            rho, flag = col[i, RHO : RHO + 1, :], col[i, FLAG : FLAG + 1, :]
            u = [col[i, VEL + a : VEL + a + 1, :] for a in range(3)]
            f = [force[a, x + 1, y : y + 1, 0:128] for a in range(3)]
            fz = [force[a, x + 1, y : y + 1, 128:256] for a in range(3)]
            uz = [ext[a, x + 4, y : y + 1, 128:256] for a in range(3)]
            rho_z, flag_z = ends[36 + x, y : y + 1, :], ends[42 + x, y : y + 1, :]
            rz = collide(ends[i], c_end, rho_z, uz, fz)
            sz = jnp.where(flag_z > 0.5, rz, wall)
            for k in range(3):
                r = collide(col[i, 8 * k : 8 * k + 8, :], cs[k], rho, u, f)
                raw[i, 8 * k : 8 * k + 8, :] = r
                s = jnp.where(flag > 0.5, r, wall)
                moved[x + 1, y + 1, 8 * k : 8 * k + 8, :] = movers[k](s, sz)
        return carry

    for x in range(BX):
        own_columns(x, 0)

    for face, (rows, r_rho, r_flag) in FACE.items():
        dx, dy = face
        numbers = [rows.get(r) for r in range(8)]
        c = constants(sub, numbers)
        mover = shifts(c[2])
        ring = WHERE[dx, dy, 0][2]["R"]
        count = 1 if dx and dy else 6
        if count == 6:
            if dx:
                z = [WHERE[dx, 0, s][2]["Z"] for s in (1, -1)]
                slot = 12
            else:
                z = [WHERE[0, dy, s][2]["Z"] + 8 for s in (1, -1)]
                slot = 2
            pz = jnp.where(low4, recv[z[0] : z[0] + 8, :], recv[z[1] : z[1] + 8, :])
            tz = [unpack(pz, slot + t) for t in range(3)]
            cz = (float(dx), float(dy), side, 1.0 / 36.0)
        for j in range(count):
            x = {1: -1, -1: 6, 0: j}[dx]
            y = {1: -1, -1: 6, 0: j}[dy]
            t = recv[ring + 8 * j : ring + 8 * j + 8, :]
            rho, flag = t[r_rho : r_rho + 1], t[r_flag : r_flag + 1]
            yu, yf = y % 16, y % 8
            if count == 6:
                u = [ext[a, x + 4, yu : yu + 1, 0:128] for a in range(3)]
            else:
                u = [t[EDGE_VEL + a : EDGE_VEL + a + 1] for a in range(3)]
            f = [force[a, x + 1, yf : yf + 1, 0:128] for a in range(3)]
            s = jnp.where(flag > 0.5, collide(t, c, rho, u, f), wall)
            if count == 6:
                uz = [ext[a, x + 4, yu : yu + 1, 128:256] for a in range(3)]
                fz = [force[a, x + 1, yf : yf + 1, 128:256] for a in range(3)]
                rz = collide(tz[0][j : j + 1], cz, tz[1][j : j + 1], uz, fz)
                sz = jnp.where(tz[2][j : j + 1] > 0.5, rz, wall[0:1])
                s = mover(s, sz)
            for k in sorted({q // 8 for q in rows.values()}):
                out = None
                for shift in sorted({(q - r) % 8 for r, q in rows.items() if q // 8 == k}):
                    tile = roll(s, shift, 0)
                    members = [q % 8 for r, q in rows.items() if q // 8 == k and (q - r) % 8 == shift]
                    out = tile if out is None else jnp.where(bits(sub, members), tile, out)
                moved[x + 1, y + 1, 8 * k : 8 * k + 8, :] = out

    odd = (iota((24, 128), 0) & 1) == 1
    start = iota((24, 128), 0) == 0

    def passing(x, carry):
        for y in range(BY):
            i = x * BY + y
            r = raw[i]
            turned = jnp.where(start, r, jnp.where(odd, roll(r, 23, 0), roll(r, 1, 0)))
            for k in range(3):
                sources = {}
                for q in natural_numbers(k):
                    if q is not None:
                        sources.setdefault(LATTICE[q][:2], []).append(q % 8)
                out = None
                for (cx, cy), members in sources.items():
                    tile = moved[x + 1 - cx, y + 1 - cy, 8 * k : 8 * k + 8, :]
                    out = tile if out is None else jnp.where(bits(sub, members), tile, out)
                out = jnp.where(out == out, out, turned[8 * k : 8 * k + 8])
                last = min(8 * k + 8, 19)
                nxt[i, 8 * k : last, :] = out[0 : last - 8 * k]
        return carry

    for x in range(BX):
        passing(x, 0)


def finish(col, vel, ownf, recv, wxy, w_hi, w_lo, occ, nxt, vtx, ext, force, raw, moved, ends):
    lane = iota((8, 128), 1)
    sub = iota((8, 128), 0)
    alive = (occ[...] > 0).astype(F32)
    assemble(recv, vel, ext, lane, sub)
    forces(recv, ownf, force)
    step_nodes(col, recv, ext, force, raw, moved, ends, nxt, lane, sub)
    interpolate(ext, wxy, w_hi, w_lo, alive, vtx)


def on_device(sizes, populations, fluid_mask, stencil_base, offsets, occupied_cell_slots, triangles):
    pops = jnp.transpose(populations, (1, 2, 0, 3)).reshape(BX * BY, 19, BZ)
    base = stencil_base.reshape(3, 1, NV)
    off = offsets.reshape(3, 1, NV)
    occ = occupied_cell_slots.reshape(1, 1)
    vmem = pl.BlockSpec(memory_space=pltpu.VMEM)
    hbm = pl.BlockSpec(memory_space=pltpu.HBM)
    shape = jax.ShapeDtypeStruct
    dma = pltpu.SemaphoreType.DMA
    vm = pltpu.VMEM
    middle = pl.pallas_call(
        functools.partial(send_all, sizes),
        name="cells_and_halo",
        out_shape=(
            shape((36, 24, 128), F32),
            shape((3, 6, 8, 128), F32),
            shape((32, 128), F32),
            shape((ROWS, 128), F32),
            shape((32, VP), F32),
            shape((256, VP), BF16),
            shape((256, VP), BF16),
        ),
        in_specs=[hbm, hbm, hbm, hbm, vmem, hbm],
        out_specs=(vmem,) * 7,
        scratch_shapes=[
            vm((ROWS, 128), F32),
            vm((6, 8, 128), I32),
            vm((3, 1, NV), I32),
            vm((3, 1, NV), F32),
            vm((3, NT), I32),
            vm((8, VP), I32),
            vm((8, VP), F32),
            vm((VP, NT), BF16),
            vm((384, VP), F32),
            vm((192, VP), F32),
            vm((24, 128), F32),
            vm((6, 8, 128), F32),
            dma((5,)),
            dma((26,)),
            dma((26,)),
            dma((26,)),
            dma((26,)),
        ],
        compiler_params=pltpu.CompilerParams(collective_id=0, has_side_effects=True, vmem_limit_bytes=48 << 20),
    )(*(pltpu.with_memory_space_constraint(a, pltpu.HBM) for a in (pops, fluid_mask, base, off)), occ, pltpu.with_memory_space_constraint(triangles.T, pltpu.HBM))
    nxt, vtx = pl.pallas_call(
        finish,
        name="collide_and_pass",
        out_shape=(shape((36, 19, 128), F32), shape((3, 1, NV), F32)),
        in_specs=[vmem] * 8,
        out_specs=(vmem, vmem),
        scratch_shapes=[
            vm((3, 14, 16, 256), F32),
            vm((3, 8, 8, 256), F32),
            vm((36, 24, 128), F32),
            vm((8, 8, 24, 128), F32),
            vm((48, 8, 128), F32),
        ],
        compiler_params=pltpu.CompilerParams(vmem_limit_bytes=48 << 20),
    )(*middle, occ)
    nxt = jnp.transpose(nxt.reshape(BX, BY, 19, BZ), (2, 0, 1, 3))
    return nxt, vtx.reshape(1, 1, 1, 3, NV)


def solution(mesh):
    sizes = tuple(mesh.shape[a] for a in AXES)
    placed = (
        P(None, "gx", "gy", "gz"),
        P("gx", "gy", "gz"),
        P("gx", "gy", "gz", None, None),
        P("gx", "gy", "gz", None, None),
        P("gx", "gy", "gz"),
        P(),
    )
    return jax.shard_map(
        functools.partial(on_device, sizes),
        mesh=mesh,
        in_specs=placed,
        out_specs=(P(None, "gx", "gy", "gz"), P("gx", "gy", "gz", None, None)),
        check_vma=False,
    )
```
